32 devices in a mesh: img: 8 (over z, x), pos: 4 (over y, core).
Axes of the slice: x: 2, y: 2, z: 4, core: 2. Of those that a mesh axis runs over, the one named last changes fastest.
Arguments:
- tokens: bfloat16 [8192, 768], P(('img', 'pos')), may hold values from -6 to 6
- image_slot: int32 [8192], P(('img', 'pos')), may hold values from -1 to 4, as said below
- patch_position: int32 [8192], P(('img', 'pos')), may hold values from -1 to 195, as said below
- ln1_gain: float32 [768], replicated, may hold values from 0.5 to 1.5
- ln1_bias: float32 [768], replicated, may hold values from -3 to 3
- w_qkv: bfloat16 [768, 2304], replicated, may hold values from -0.21875 to 0.21875
- bias_query: float32 [768], replicated, may hold values from -3 to 3
- bias_value: float32 [768], replicated, may hold values from -3 to 3
- w_out: bfloat16 [768, 768], replicated, may hold values from -0.875 to 0.875
- bias_out: float32 [768], replicated, may hold values from -3 to 3
- ln2_gain: float32 [768], replicated, may hold values from 0.5 to 1.5
- ln2_bias: float32 [768], replicated, may hold values from -3 to 3
- w_up: bfloat16 [768, 3072], replicated, may hold values from -0.21875 to 0.21875
- bias_up: float32 [3072], replicated, may hold values from -3 to 3
- w_down: bfloat16 [3072, 768], replicated, may hold values from -0.109375 to 0.109375
- bias_down: float32 [768], replicated, may hold values from -3 to 3
- w_proj: bfloat16 [768, 512], replicated, may hold values from -0.21875 to 0.21875
- bias_proj: float32 [512], replicated, may hold values from -3 to 3
- mask_token: bfloat16 [512], replicated, may hold values from -4 to 4
- cotangent: bfloat16 [160, 196, 512], P('img', 'pos'), may hold values from -6 to 6
Outputs:
- decoder_input: bfloat16 [160, 196, 512], P('img', 'pos')
- grad_tokens: bfloat16 [8192, 768], P(('img', 'pos'))
- grad_ln1_gain: float32 [768], replicated
- grad_ln1_bias: float32 [768], replicated
- grad_w_qkv: float32 [768, 2304], P('img')
- grad_bias_query: float32 [768], replicated
- grad_bias_value: float32 [768], replicated
- grad_w_out: float32 [768, 768], P('img')
- grad_bias_out: float32 [768], replicated
- grad_ln2_gain: float32 [768], replicated
- grad_ln2_bias: float32 [768], replicated
- grad_w_up: float32 [768, 3072], P('img')
- grad_bias_up: float32 [3072], replicated
- grad_w_down: float32 [3072, 768], P('img')
- grad_bias_down: float32 [768], replicated
- grad_w_proj: float32 [768, 512], P('img')
- grad_bias_proj: float32 [512], replicated
- grad_mask_token: float32 [512], replicated
The draws below stay inside these ranges and needn't reach their ends.
Inputs may be any that keep to these rules, and one draw needn't show every extreme that they name: `image_slot`: each sequence of 256 rows holds its 5 images in order 0 to 4, each on 49 consecutive rows; the remaining rows are padding, marked -1, in gaps before, between or after images. `patch_position`: rows of one image hold distinct positions; padded rows hold -1. Of each image, between 9 and 16 positions fall in each aligned range of 49 positions, and in every sequence some image has exactly 16 in one range.
All inputs are finite; a program needn't handle non-finite values.
Results may differ from the reference program's by a relative error of at most 0.012.
Values may be sent and summed in bfloat16 or wider, within the bound.
A program may use at most 192 MiB of HBM per device.

```python
import jax
import jax.numpy as jnp
from jax import lax

D = 768
HEADS = 12
HEAD_DIM = 64
FF = 3072
DOUT = 512
ROWS_SEQ = 256
IMG_SEQ = 5
VISIBLE = 49
POSITIONS = 196
SEQS = 32
IMAGES = 160


def packing(key):
    key_gap, key_one, key_two, key_three, key_order, key_offset, key_shuffle = jax.random.split(key, 7)
    spare_rows = ROWS_SEQ - IMG_SEQ * VISIBLE
    quarter_len = POSITIONS // 4
    cut_points = jnp.sort(jax.random.randint(key_gap, (SEQS, IMG_SEQ), 0, spare_rows + 1), axis=1)
    number = jnp.arange(IMG_SEQ, dtype=jnp.int32)
    starts = cut_points + number[None, :] * VISIBLE
    row_index = jnp.arange(ROWS_SEQ, dtype=jnp.int32)
    inside = (row_index[None, :, None] >= starts[:, None, :]) & (row_index[None, :, None] < starts[:, None, :] + VISIBLE)
    slot_of_row = jnp.where(jnp.any(inside, axis=2), jnp.sum(jnp.where(inside, number[None, None, :], 0), axis=2), -1)
    is_first = (number == 0)[None, :]
    extra_one = jnp.where(is_first, 7, jax.random.randint(key_one, (SEQS, IMG_SEQ), 3, 7))
    extra_two = jax.random.randint(key_two, (SEQS, IMG_SEQ), 3, 7)
    extra_three = jax.random.randint(key_three, (SEQS, IMG_SEQ), 0, 14 - extra_one - extra_two)
    extra_four = 13 - extra_one - extra_two - extra_three
    counts = 9 + jnp.stack([extra_one, extra_two, extra_three, extra_four], axis=2)
    count_keys = jax.random.randint(key_order, (SEQS, IMG_SEQ, 4), 0, 1 << 20) * 4 + jnp.arange(4, dtype=jnp.int32)
    count_order = jnp.argsort(count_keys, axis=2, stable=True)
    counts = jnp.take_along_axis(counts, count_order, axis=2)
    range_ends = jnp.cumsum(counts, axis=2)
    token_index = jnp.arange(VISIBLE, dtype=jnp.int32)
    quarter = jnp.sum((token_index[None, None, :, None] >= range_ends[:, :, None, :3]).astype(jnp.int32), axis=3)
    range_start = jnp.take_along_axis(range_ends - counts, quarter, axis=2)
    rank_in = token_index[None, None, :] - range_start
    offset_keys = jax.random.randint(key_offset, (SEQS, IMG_SEQ, 4, quarter_len), 0, 1 << 20) * 64 + jnp.arange(quarter_len, dtype=jnp.int32)
    offsets = jnp.argsort(offset_keys, axis=3, stable=True).reshape(SEQS, IMG_SEQ, 4 * quarter_len)
    within = jnp.take_along_axis(offsets, quarter * quarter_len + rank_in, axis=2)
    position = quarter * quarter_len + within
    shuffle_keys = jax.random.randint(key_shuffle, (SEQS, IMG_SEQ, VISIBLE), 0, 1 << 20) * 64 + token_index
    shuffle = jnp.argsort(shuffle_keys, axis=2, stable=True)
    position = jnp.take_along_axis(position, shuffle, axis=2).reshape(SEQS, IMG_SEQ * VISIBLE)
    start_of_row = jnp.sum(jnp.where(inside, starts[:, None, :], 0), axis=2)
    flat_index = jnp.clip(slot_of_row * VISIBLE + row_index[None, :] - start_of_row, 0, IMG_SEQ * VISIBLE - 1)
    picked = jnp.take_along_axis(position, flat_index, axis=1)
    patch_of_row = jnp.where(slot_of_row >= 0, picked, -1)
    return (slot_of_row.reshape(-1).astype(jnp.int32), patch_of_row.reshape(-1).astype(jnp.int32))


def draw_image_slot(key, part):
    shared = packing(key)
    return shared[0]


def draw_patch_position(key, part):
    shared = packing(key)
    return shared[1]


def level_of(own_key, dims, cuts, low, high):
    def one(dim, parts):
        steps = jax.random.uniform(jax.random.fold_in(jax.random.fold_in(own_key, 6), dim), (parts,), jnp.float32, low / len(cuts), high / len(cuts))
        return jnp.repeat(jnp.exp(steps), dims[dim] // parts).reshape((-1,) + (1,) * (len(dims) - dim - 1))

    level = one(*cuts[0])
    for cut in cuts[1:]:
        level = level * one(*cut)
    return level


def bell_draw(stream_key, dims, scale, bound, cuts=(), held_as=jnp.bfloat16):
    values = jax.random.normal(stream_key, dims, jnp.float32) * scale
    if len(cuts) > 0:
        values = level_of(stream_key, dims, cuts, -0.22, 0.18) * values
    return jnp.clip(values, min=-bound, max=bound).astype(held_as)


def setup_inputs(seed: int = 0) -> dict:
    keys = jax.random.split(jax.random.key(seed), 21)
    return {
        "tokens": bell_draw(keys[0], (SEQS * ROWS_SEQ, D), 1.0, 6.0, ((0, 32),)),
        "image_slot": draw_image_slot(jax.random.fold_in(keys[20], 71), 0),
        "patch_position": draw_patch_position(jax.random.fold_in(keys[20], 71), 0),
        "ln1_gain": jnp.clip(1.0 + 0.1 * jax.random.normal(keys[3], (D,), jnp.float32), 0.5, 1.5),
        "ln1_bias": bell_draw(keys[4], (D,), 0.3, 3.0, (), jnp.float32),
        "w_qkv": bell_draw(keys[5], (D, 3 * D), D ** -0.5, 0.21875),
        "bias_query": bell_draw(keys[6], (D,), 0.3, 3.0, (), jnp.float32),
        "bias_value": bell_draw(keys[7], (D,), 0.3, 3.0, (), jnp.float32),
        "w_out": bell_draw(keys[8], (D, D), (D // 16) ** -0.5, 0.875),
        "bias_out": bell_draw(keys[9], (D,), 0.3, 3.0, (), jnp.float32),
        "ln2_gain": jnp.clip(1.0 + 0.1 * jax.random.normal(keys[10], (D,), jnp.float32), 0.5, 1.5),
        "ln2_bias": bell_draw(keys[11], (D,), 0.3, 3.0, (), jnp.float32),
        "w_up": bell_draw(keys[12], (D, FF), D ** -0.5, 0.21875),
        "bias_up": bell_draw(keys[13], (FF,), 0.3, 3.0, (), jnp.float32),
        "w_down": bell_draw(keys[14], (FF, D), FF ** -0.5, 0.109375),
        "bias_down": bell_draw(keys[15], (D,), 0.3, 3.0, (), jnp.float32),
        "w_proj": bell_draw(keys[16], (D, DOUT), D ** -0.5, 0.21875),
        "bias_proj": bell_draw(keys[17], (DOUT,), 0.3, 3.0, (), jnp.float32),
        "mask_token": bell_draw(keys[18], (DOUT,), 1.0, 4.0),
        "cotangent": bell_draw(keys[19], (IMAGES, POSITIONS, DOUT), 1.0, 6.0, ((0, 8), (1, 4))),
    }


@jax.custom_vjp
def low(v):
    return lax.optimization_barrier(v.astype(jnp.bfloat16)).astype(jnp.float32)

@jax.custom_vjp
def low_back(v):
    return v

def low_keep(v):
    return (low(v), None)

def low_pass(kept, grad):
    return (grad,)

def back_keep(v):
    return (v, None)

def back_low(kept, grad):
    return (low(grad),)
low.defvjp(low_keep, low_pass)
low_back.defvjp(back_keep, back_low)
EPSILON = 1e-05
NEGATIVE = -1e+30
GELU_COEF = 0.7978845608028654

def layer_norm(values, gain_vec, shift_vec):
    centre = lax.optimization_barrier(jnp.mean(values, axis=-1, keepdims=True))
    centred = values - centre
    return centred * lax.rsqrt(lax.optimization_barrier(jnp.mean(centred * centred, axis=-1, keepdims=True)) + EPSILON) * gain_vec + shift_vec

def gelu_tanh(values):
    return 0.5 * values * (1.0 + jnp.tanh(GELU_COEF * (values + 0.044715 * values * values * values)))

def matmul_full(left, right):
    return jnp.dot(left, right, precision=lax.Precision.HIGHEST, preferred_element_type=jnp.float32)

def encode(row_block, slot_block, weights):
    ln1_gain, ln1_bias, w_qkv, bias_query, bias_value, w_out, bias_out, ln2_gain, ln2_bias, w_up, bias_up, w_down, bias_down, w_proj, bias_proj = weights
    seq_count = slot_block.shape[0]
    head_shape = (seq_count, ROWS_SEQ, HEADS, HEAD_DIM)
    normed_one = low(layer_norm(row_block, ln1_gain, ln1_bias))
    qkv_all = matmul_full(normed_one, w_qkv)
    queries = low(low_back(qkv_all[:, :D] + bias_query)).reshape(head_shape)
    keys_h = low(low_back(qkv_all[:, D:2 * D])).reshape(head_shape)
    values_h = low(low_back(qkv_all[:, 2 * D:] + bias_value)).reshape(head_shape)
    allowed = slot_block[:, None, :, None] == slot_block[:, None, None, :]
    raw_scores = jnp.einsum('sqhd,skhd->shqk', queries, keys_h, precision=lax.Precision.HIGHEST) * HEAD_DIM ** (-0.5)
    scores = low_back(jnp.where(allowed, raw_scores, NEGATIVE))
    probs_low = low(jax.nn.softmax(scores, axis=-1))
    attended = jnp.einsum('shqk,skhd->sqhd', probs_low, values_h, precision=lax.Precision.HIGHEST)
    attended = low(low_back(attended.reshape(-1, D)))
    residual = row_block + low_back(matmul_full(attended, w_out) + bias_out)
    normed_mlp = low(layer_norm(residual, ln2_gain, ln2_bias))
    up_proj = low_back(matmul_full(normed_mlp, w_up) + bias_up)
    hidden = low(gelu_tanh(up_proj))
    block_out = residual + low_back(matmul_full(hidden, w_down) + bias_down)
    return low(low_back(matmul_full(low(block_out), w_proj) + bias_proj))

def decode_all(inputs, image_slot, patch_position):
    row_input = inputs[0]
    weights = inputs[1:16]
    mask_vec = inputs[16]
    groups = SEQS // 16
    row_blocks = row_input.reshape(groups, 16 * ROWS_SEQ, D)
    slot_blocks = image_slot.reshape(groups, 16, ROWS_SEQ)

    def one_group(pair):
        return encode(pair[0], pair[1], weights)
    projected = lax.map(jax.checkpoint(one_group), (row_blocks, slot_blocks)).reshape(-1, DOUT)
    row_seq = jnp.arange(SEQS * ROWS_SEQ, dtype=jnp.int32) // ROWS_SEQ
    target = jnp.where(image_slot >= 0, (row_seq * IMG_SEQ + image_slot) * POSITIONS + patch_position, IMAGES * POSITIONS).astype(jnp.int32)
    grid = jnp.zeros((IMAGES * POSITIONS, DOUT), dtype=projected.dtype).at[target].add(projected, mode='drop')
    seen = jnp.zeros((IMAGES * POSITIONS,), jnp.int32).at[target].add(jnp.ones_like(target), mode='drop')
    return jnp.where(seen[:, None] > 0, grid, mask_vec[None, :]).reshape(IMAGES, POSITIONS, DOUT)

def reference(tokens, image_slot, patch_position, ln1_gain, ln1_bias, w_qkv, bias_query, bias_value, w_out, bias_out, ln2_gain, ln2_bias, w_up, bias_up, w_down, bias_down, w_proj, bias_proj, mask_token, cotangent):
    floats = (tokens.astype(jnp.float32), ln1_gain, ln1_bias, w_qkv.astype(jnp.float32), bias_query, bias_value, w_out.astype(jnp.float32), bias_out, ln2_gain, ln2_bias, w_up.astype(jnp.float32), bias_up, w_down.astype(jnp.float32), bias_down, w_proj.astype(jnp.float32), bias_proj, mask_token.astype(jnp.float32))

    def forward(*inputs):
        return decode_all(inputs, image_slot, patch_position)
    decoded, pullback = jax.vjp(forward, *floats)
    grads = pullback(cotangent.astype(jnp.float32))
    return (decoded.astype(jnp.bfloat16), grads[0].astype(jnp.bfloat16), grads[1], grads[2], grads[3], grads[4], grads[5], grads[6], grads[7], grads[8], grads[9], grads[10], grads[11], grads[12], grads[13], grads[14], grads[15], grads[16])
```

```python
import jax
import jax.numpy as jnp
from jax import lax
from jax.experimental import pallas as pl
from jax.experimental.pallas import tpu as pltpu
from jax.sharding import PartitionSpec as P

MESH_ID = pl.DeviceIdType.MESH

HEADS = 12
HEAD_DIM = 64
ROWS_SEQ = 256
IMG_SEQ = 5
POSITIONS = 196
CAP = 16


EPSILON = 1e-05
NEGATIVE = -1e30
GELU_COEF = 0.7978845608028654


def layer_norm(values, gain_vec, shift_vec):
    centre = jnp.mean(values, axis=-1, keepdims=True)
    centred = values - centre
    return (
        centred
        * lax.rsqrt(jnp.mean(centred * centred, axis=-1, keepdims=True) + EPSILON)
        * gain_vec
        + shift_vec
    )


def gelu_tanh(values):
    return (
        0.5 * values * (1.0 + jnp.tanh(GELU_COEF * (values + 0.044715 * values * values * values)))
    )


def matmul_rows(left, right):
    return jnp.dot(left, right, preferred_element_type=jnp.float32)


def column_sums(values):
    return jnp.sum(values.astype(jnp.float32), axis=0)


def reduce_matrices(members):
    img_count = lax.axis_size("img")
    pos_count = lax.axis_size("pos")
    pieces = [member.reshape(img_count, pos_count, -1) for member in members]
    bucket = jnp.concatenate(pieces, axis=2)
    flat_bucket = bucket.reshape(img_count * pos_count, -1)
    share = lax.psum_scatter(flat_bucket, ("img", "pos"), scatter_dimension=0, tiled=True).reshape(
        1, 1, -1
    )
    summed = lax.all_gather(share.astype(jnp.bfloat16), "pos", axis=1, tiled=True).astype(
        share.dtype
    )
    results = []
    offset = 0
    for member in members:
        extent = member.size // (img_count * pos_count)
        block = summed[0, :, offset : offset + extent]
        results.append(block.reshape(member.shape[0] // img_count, member.shape[1]))
        offset = offset + extent
    return results


def reduce_vectors(members):
    return lax.psum(tuple(members), ("img", "pos"))


AXES = ("zh", "zl", "x", "y")
MATRICES = ("down", "up", "proj", "out", "qkv")
JOBS = (
    ("down", 0, 256, ("zl", "zh", "x", "y")),
    ("down", 256, 256, ("zl", "zh", "x", "y")),
    ("down", 512, 256, ("zl", "zh", "x", "y")),
    ("up", 0, 512, ("y", "x", "zl", "zh")),
    ("up", 512, 512, ("y", "x", "zl", "zh")),
    ("up", 1024, 512, ("y", "x", "zl", "zh")),
    ("proj", 0, 256, ("x", "y", "zl", "zh")),
    ("out", 0, 384, ("x", "y", "zl", "zh")),
    ("qkv", 0, 384, ("x", "y", "zl", "zh")),
    ("qkv", 384, 384, ("x", "y", "zl", "zh")),
    ("qkv", 768, 384, ("x", "y", "zl", "zh")),
)
ORDER = (
    (6, 0),
    (0, 0),
    (3, 0),
    (7, 0),
    (1, 0),
    (4, 0),
    (8, 0),
    (2, 0),
    (9, 0),
    (5, 0),
    (0, 1),
    (6, 1),
    (10, 0),
    (7, 1),
    (1, 1),
    (8, 1),
    (3, 1),
    (2, 1),
    (6, 2),
    (9, 1),
    (7, 2),
    (4, 1),
    (8, 2),
    (10, 1),
    (3, 2),
    (6, 3),
    (5, 1),
    (9, 2),
    (7, 3),
    (6, 4),
    (0, 2),
    (4, 2),
    (6, 5),
    (8, 3),
    (7, 4),
    (1, 2),
    (0, 3),
    (10, 2),
    (2, 2),
    (7, 5),
    (3, 3),
    (8, 4),
    (1, 3),
    (5, 2),
    (0, 4),
    (8, 5),
    (9, 3),
    (2, 3),
    (4, 3),
    (3, 4),
    (0, 5),
    (10, 3),
    (1, 4),
    (5, 3),
    (9, 4),
    (3, 5),
    (2, 4),
    (1, 5),
    (4, 4),
    (9, 5),
    (10, 4),
    (2, 5),
    (5, 4),
    (4, 5),
    (10, 5),
    (5, 5),
)
VEC_STEPS = ("core", "x", "y", "zl", "zh")


def device_coords():
    img = lax.axis_index("img")
    pos = lax.axis_index("pos")
    return {"zh": img // 4, "zl": (img // 2) % 2, "x": img % 2, "y": pos // 2, "core": pos % 2}


def device_of(where):
    return (where["zh"] * 4 + where["zl"] * 2 + where["x"], where["y"] * 2 + where["core"])


def job_rows(name):
    return 96 if name == "down" else 48


def reduce_kernel(*refs):
    count = iter(refs)
    lefts = {name: next(count) for name in MATRICES}
    rights = {name: next(count) for name in MATRICES}
    vec_ref = next(count)
    outs = {name: next(count) for name in MATRICES}
    vec_out = next(count)
    lefts_in = {name: next(count) for name in MATRICES}
    rights_in = {name: next(count) for name in MATRICES}
    partial = [next(count) for _ in JOBS]
    landed = [[next(count) for _ in range(4)] for _ in JOBS]
    final = {name: next(count) for name in MATRICES}
    vec_held = next(count)
    vec_in = next(count)
    core_send, core_recv, job_send, job_recv, vec_send, vec_recv = count
    me = device_coords()
    core = me["core"]

    def peer(axis):
        return device_of({**me, axis: 1 - me[axis]})

    barrier = pltpu.get_barrier_semaphore()
    for axis in AXES + ("core",):
        pl.semaphore_signal(barrier, inc=1, device_id=peer(axis), device_id_type=MESH_ID)
    pl.semaphore_wait(barrier, 5)

    def remote(source, target, send_sem, recv_sem, axis):
        return pltpu.make_async_remote_copy(
            src_ref=source,
            dst_ref=target,
            send_sem=send_sem,
            recv_sem=recv_sem,
            device_id=peer(axis),
            device_id_type=MESH_ID,
        )

    started = []
    core_copies = {}
    for number, name in enumerate(MATRICES):
        if name == "down":
            left_src, right_src = lefts[name].at[:, 1 - core], rights[name]
        else:
            left_src, right_src = lefts[name], rights[name].at[1 - core]
        pair = (
            remote(left_src, lefts_in[name], core_send.at[number, 0], core_recv.at[number, 0], "core"),
            remote(right_src, rights_in[name], core_send.at[number, 1], core_recv.at[number, 1], "core"),
        )
        for copy in pair:
            copy.start()
            started.append(copy)
        core_copies[name] = pair

    def job_copy(number, stage):
        name, first, wide, dims = JOBS[number]
        columns = pl.ds(first, wide)
        sems = (job_send.at[number, stage], job_recv.at[number, stage])
        if stage < 4:
            pick = []
            for axis in AXES:
                if axis in dims[:stage]:
                    pick.append(me[axis])
                elif axis == dims[stage]:
                    pick.append(1 - me[axis])
                else:
                    pick.append(slice(None))
            return remote(partial[number].at[tuple(pick)], landed[number][stage], *sems, dims[stage])
        if stage == 4:
            place = final[name].at[core, me["y"], :, columns]
            return remote(place, place, *sems, "y")
        place = final[name].at[core, :, :, columns]
        return remote(place, place, *sems, "core")

    def start_job(number, stage):
        copy = job_copy(number, stage)
        copy.start()
        started.append(copy)

    def vec_copy(stage):
        return remote(
            vec_held.at[stage], vec_in.at[stage], vec_send.at[stage], vec_recv.at[stage], VEC_STEPS[stage]
        )

    def start_vec(stage):
        copy = vec_copy(stage)
        copy.start()
        started.append(copy)

    vec_held[0] = vec_ref[...]
    start_vec(0)

    def multiply(name):
        numbers = [number for number, job in enumerate(JOBS) if job[0] == name]
        for copy in core_copies[name]:
            copy.wait_recv()
        rows = job_rows(name)
        if name == "down":
            for block in range(8):
                high, low, side = block // 4, (block // 2) % 2, block % 2
                total = jnp.dot(
                    lefts[name][block, core], rights[name][...], preferred_element_type=jnp.float32
                ) + jnp.dot(
                    lefts_in[name][block], rights_in[name][...], preferred_element_type=jnp.float32
                )
                total = total.astype(jnp.bfloat16)
                for number in numbers:
                    _, first, wide, _ = JOBS[number]
                    for half in range(2):
                        partial[number][high, low, side, half] = total[
                            half * rows : (half + 1) * rows, first : first + wide
                        ]
            for number in numbers:
                start_job(number, 0)
            return
        for number in numbers:
            _, first, wide, _ = JOBS[number]
            for high in range(2):
                span = slice(high * 8 * rows, (high + 1) * 8 * rows)
                total = jnp.dot(
                    lefts[name][span], rights[name][core, :, first : first + wide], preferred_element_type=jnp.float32
                ) + jnp.dot(
                    lefts_in[name][span], rights_in[name][:, first : first + wide], preferred_element_type=jnp.float32
                )
                total = total.astype(jnp.bfloat16)
                for part in range(8):
                    low, side, half = part // 4, (part // 2) % 2, part % 2
                    partial[number][high, low, side, half] = total[part * rows : (part + 1) * rows]
            start_job(number, 0)

    def arrive(number, stage):
        name, first, wide, dims = JOBS[number]
        copy = job_copy(number, stage)
        copy.wait_recv()
        if stage < 4:
            fixed = dims[: stage + 1]
            free = [axis for axis in AXES if axis not in fixed]
            for code in range(2 ** len(free)):
                bits = {axis: (code >> (len(free) - 1 - spot)) % 2 for spot, axis in enumerate(free)}
                here = tuple(me[axis] if axis in fixed else bits[axis] for axis in AXES)
                there = tuple(bits[axis] for axis in free)
                sums = partial[number][here] + landed[number][stage][there]
                if stage < 3:
                    partial[number][here] = sums
                else:
                    final[name][core, me["y"], :, first : first + wide] = sums
        if stage < 5:
            start_job(number, stage + 1)

    def arrive_vec(stage):
        vec_copy(stage).wait_recv()
        sums = vec_held[stage] + vec_in[stage]
        if stage < 4:
            vec_held[stage + 1] = sums
            start_vec(stage + 1)
        else:
            vec_out[...] = sums

    for name in MATRICES:
        multiply(name)
    for spot, (number, stage) in enumerate(ORDER):
        arrive(number, stage)
        if spot % 8 == 7 and spot // 8 < 5:
            arrive_vec(spot // 8)
    for name in MATRICES:
        rows = job_rows(name)
        half_wide = final[name].shape[3]
        for side in range(2):
            for half in range(2):
                piece = final[name][side, half].astype(outs[name].dtype)
                if name == "down":
                    outs[name][(side * 2 + half) * rows : (side * 2 + half + 1) * rows, :] = piece
                else:
                    outs[name][half * rows : (half + 1) * rows, side * half_wide : (side + 1) * half_wide] = piece
    for copy in started:
        copy.wait_send()


def reduce_all(lefts, rights, vectors):
    low = jnp.bfloat16
    operands, outs, left_in, right_in, final = [], [], [], [], []
    for name in MATRICES:
        left = lefts[name]
        operands.append(left.reshape(8, 2, 192, -1) if name == "down" else left)
    for name in MATRICES:
        right = rights[name]
        rows, wide = right.shape
        operands.append(right if name == "down" else right.reshape(rows, 2, wide // 2).transpose(1, 0, 2))
    for name in MATRICES:
        depth, rows = lefts[name].shape
        wide = rights[name].shape[1]
        outs.append(jax.ShapeDtypeStruct((depth // 8, wide), jnp.float32))
        if name == "down":
            left_in.append(pltpu.VMEM((8, 192, rows), low))
            right_in.append(pltpu.VMEM((rows, wide), low))
            final.append(pltpu.VMEM((2, 2, 96, wide), low))
        else:
            left_in.append(pltpu.VMEM((depth, rows), low))
            right_in.append(pltpu.VMEM((rows, wide // 2), low))
            final.append(pltpu.VMEM((2, 2, 48, wide // 2), low))
    partial, landed = [], []
    for name, _, wide, _ in JOBS:
        rows = job_rows(name)
        partial.append(pltpu.VMEM((2, 2, 2, 2, rows, wide), low))
        for stage in range(4):
            landed.append(pltpu.VMEM((2,) * (3 - stage) + (rows, wide), low))
    dma = pltpu.SemaphoreType.DMA
    vmem = pl.BlockSpec(memory_space=pltpu.VMEM)
    results = pl.pallas_call(
        reduce_kernel,
        out_shape=outs + [jax.ShapeDtypeStruct(vectors.shape, jnp.float32)],
        in_specs=[vmem] * (len(operands) + 1),
        out_specs=[vmem] * (len(outs) + 1),
        scratch_shapes=left_in
        + right_in
        + partial
        + landed
        + final
        + [pltpu.VMEM((5,) + vectors.shape, jnp.float32)] * 2
        + [dma((5, 2)), dma((5, 2)), dma((len(JOBS), 6)), dma((len(JOBS), 6)), dma((5,)), dma((5,))],
        compiler_params=pltpu.CompilerParams(
            collective_id=0, has_side_effects=True, vmem_limit_bytes=60 * 2**20
        ),
        name="reduce_grads",
    )(*operands, vectors)
    return dict(zip(MATRICES, results)), results[-1]


def per_device(
    tokens,
    image_slot,
    patch_position,
    ln1_gain,
    ln1_bias,
    w_qkv,
    bias_query,
    bias_value,
    w_out,
    bias_out,
    ln2_gain,
    ln2_bias,
    w_up,
    bias_up,
    w_down,
    bias_down,
    w_proj,
    bias_proj,
    mask_token,
    cotangent,
):
    seq_count = tokens.shape[0] // ROWS_SEQ
    width = w_out.shape[0]
    out_width = w_proj.shape[1]
    pos_count = lax.axis_size("pos")
    quarter_len = POSITIONS // pos_count
    score_scale = HEAD_DIM ** (-0.5)
    head_shape = (seq_count, ROWS_SEQ, HEADS, HEAD_DIM)
    rows_f = tokens.astype(jnp.float32)
    normed_low = layer_norm(rows_f, ln1_gain, ln1_bias).astype(jnp.bfloat16)
    qkv_all = matmul_rows(normed_low, w_qkv)
    queries = (qkv_all[:, :width] + bias_query).astype(jnp.bfloat16).reshape(head_shape)
    keys_h = qkv_all[:, width : 2 * width].astype(jnp.bfloat16).reshape(head_shape)
    values_h = (qkv_all[:, 2 * width :] + bias_value).astype(jnp.bfloat16).reshape(head_shape)
    slot_rows = image_slot.reshape(seq_count, ROWS_SEQ)
    allowed = slot_rows[:, None, :, None] == slot_rows[:, None, None, :]
    raw_scores = (
        jnp.einsum("sqhd,skhd->shqk", queries, keys_h, preferred_element_type=jnp.float32)
        * score_scale
    )
    scores = jnp.where(allowed, raw_scores, NEGATIVE)
    top_score = jnp.max(scores, axis=-1, keepdims=True)
    log_total = top_score + jnp.log(jnp.sum(jnp.exp(scores - top_score), axis=-1, keepdims=True))
    attn_probs = jnp.exp(scores - log_total)
    probs_low = attn_probs.astype(jnp.bfloat16)
    attended = jnp.einsum(
        "shqk,skhd->sqhd", probs_low, values_h, preferred_element_type=jnp.float32
    )
    attended = attended.reshape(-1, width).astype(jnp.bfloat16)
    residual = rows_f + matmul_rows(attended, w_out) + bias_out
    normed_mlp = layer_norm(residual, ln2_gain, ln2_bias).astype(jnp.bfloat16)
    up_proj = matmul_rows(normed_mlp, w_up) + bias_up
    hidden = gelu_tanh(up_proj).astype(jnp.bfloat16)
    block_out = residual + matmul_rows(hidden, w_down) + bias_down
    block_low = block_out.astype(jnp.bfloat16)
    projected = (matmul_rows(block_low, w_proj) + bias_proj).astype(jnp.bfloat16)
    row_index = jnp.arange(ROWS_SEQ, dtype=jnp.int32)
    pos_rows = patch_position.reshape(seq_count, ROWS_SEQ)
    live = slot_rows >= 0
    bucket_id = jnp.where(live, slot_rows * pos_count + pos_rows // quarter_len, -1)
    earlier = (bucket_id[:, :, None] == bucket_id[:, None, :]) & (
        row_index[None, :, None] > row_index[None, None, :]
    )
    rank_in = jnp.sum(earlier.astype(jnp.int32), axis=2)
    target = jnp.where(live, bucket_id * CAP + rank_in, -1)
    slot_index = jnp.arange(IMG_SEQ * pos_count * CAP, dtype=jnp.int32)
    selected = slot_index[None, :, None] == target[:, None, :]
    select_low = selected.astype(jnp.bfloat16)
    outgoing = jnp.einsum(
        "sjr,src->sjc",
        select_low,
        projected.reshape(seq_count, ROWS_SEQ, out_width),
        preferred_element_type=jnp.float32,
    ).astype(jnp.bfloat16)
    outgoing = outgoing.reshape(seq_count * IMG_SEQ, pos_count, CAP, out_width)
    slot_place = (
        jnp.sum(jnp.where(selected, (pos_rows % quarter_len + 1)[:, None, :], 0), axis=2) - 1
    )
    slot_place = slot_place.reshape(seq_count * IMG_SEQ, pos_count, CAP)
    arrived, arrived_place = (
        lax.all_to_all(outgoing, "pos", split_axis=1, concat_axis=0, tiled=True),
        lax.all_to_all(slot_place, "pos", split_axis=1, concat_axis=0, tiled=True),
    )
    arrived = arrived[:, 0]
    arrived_place = arrived_place[:, 0]
    placing = jnp.arange(quarter_len, dtype=jnp.int32)[None, :, None] == arrived_place[:, None, :]
    placing_low = placing.astype(jnp.bfloat16)
    visible = jnp.any(placing, axis=2)
    filled = jnp.einsum("gqj,gjc->gqc", placing_low, arrived, preferred_element_type=jnp.float32)
    decoder_input = jnp.where(
        visible[:, :, None], filled, mask_token.astype(jnp.float32)[None, None, :]
    )
    decoder_input = decoder_input.astype(jnp.bfloat16)
    grad_mask = jnp.sum(
        jnp.where(visible[:, :, None], 0.0, cotangent.astype(jnp.float32)), axis=(0, 1)
    )
    back_slots = jnp.einsum(
        "gqj,gqc->gjc", placing_low, cotangent, preferred_element_type=jnp.float32
    ).astype(jnp.bfloat16)
    returned = lax.all_to_all(back_slots[:, None], "pos", split_axis=0, concat_axis=1, tiled=True)
    delta_proj = (
        jnp.einsum(
            "sjr,sjc->src",
            select_low,
            returned.reshape(seq_count, -1, out_width),
            preferred_element_type=jnp.float32,
        )
        .reshape(-1, out_width)
        .astype(jnp.bfloat16)
    )
    grad_bproj = column_sums(delta_proj)
    delta_block = jnp.einsum("rc,dc->rd", delta_proj, w_proj, preferred_element_type=jnp.float32)
    delta_down = delta_block.astype(jnp.bfloat16)
    grad_bdown = column_sums(delta_down)
    delta_hidden = jnp.einsum("rd,fd->rf", delta_down, w_down, preferred_element_type=jnp.float32)
    gelu_back = jax.vjp(gelu_tanh, up_proj)[1]
    delta_up = gelu_back(delta_hidden)[0].astype(jnp.bfloat16)
    grad_bup = column_sums(delta_up)
    delta_normed = jnp.einsum("rf,df->rd", delta_up, w_up, preferred_element_type=jnp.float32)
    norm_back = jax.vjp(layer_norm, residual, ln2_gain, ln2_bias)[1]
    delta_resid_norm, grad_gain_two, grad_shift_two = norm_back(delta_normed)
    delta_residual = delta_block + delta_resid_norm
    delta_branch = delta_residual.astype(jnp.bfloat16)
    grad_bout = column_sums(delta_branch)
    delta_attended = jnp.einsum(
        "rd,ed->re", delta_branch, w_out, preferred_element_type=jnp.float32
    )
    delta_attended = delta_attended.astype(jnp.bfloat16).reshape(head_shape)
    delta_values = jnp.einsum(
        "shqk,sqhd->skhd", probs_low, delta_attended, preferred_element_type=jnp.float32
    ).astype(jnp.bfloat16)
    delta_probs = jnp.einsum(
        "sqhd,skhd->shqk", delta_attended, values_h, preferred_element_type=jnp.float32
    )
    delta_scores = attn_probs * (
        delta_probs - jnp.sum(delta_probs * attn_probs, axis=-1, keepdims=True)
    )
    delta_scores = delta_scores.astype(jnp.bfloat16)
    delta_queries = (
        (
            jnp.einsum("shqk,skhd->sqhd", delta_scores, keys_h, preferred_element_type=jnp.float32)
            * score_scale
        )
        .astype(jnp.bfloat16)
        .reshape(-1, width)
    )
    delta_keys = (
        (
            jnp.einsum("shqk,sqhd->skhd", delta_scores, queries, preferred_element_type=jnp.float32)
            * score_scale
        )
        .astype(jnp.bfloat16)
        .reshape(-1, width)
    )
    delta_values = delta_values.reshape(-1, width)
    delta_qkv = jnp.concatenate([delta_queries, delta_keys, delta_values], axis=1)
    grad_bquery = column_sums(delta_queries)
    grad_bvalue = column_sums(delta_values)
    delta_first = jnp.einsum("re,de->rd", delta_qkv, w_qkv, preferred_element_type=jnp.float32)
    first_back = jax.vjp(layer_norm, rows_f, ln1_gain, ln1_bias)[1]
    delta_rows, grad_gain_one, grad_shift_one = first_back(delta_first)
    grad_tokens = (delta_residual + delta_rows).astype(jnp.bfloat16)
    lefts = {"down": hidden.T, "up": normed_mlp.T, "proj": block_low.T, "out": attended.T, "qkv": normed_low.T}
    rights = {
        "down": delta_down,
        "up": delta_up,
        "proj": delta_proj,
        "out": delta_branch,
        "qkv": delta_qkv,
    }
    members = (
        grad_gain_one,
        grad_shift_one,
        grad_bquery,
        grad_bvalue,
        grad_bout,
        grad_gain_two,
        grad_shift_two,
        grad_bup,
        grad_bdown,
        grad_bproj,
        grad_mask,
    )
    if lax.axis_size("img") == 8 and pos_count == 4:
        mats, vec_sums = reduce_all(lefts, rights, jnp.concatenate(members).reshape(-1, 128))
        flat = vec_sums.reshape(-1)
        vecs = []
        offset = 0
        for member in members:
            vecs.append(flat[offset : offset + member.size])
            offset = offset + member.size
    else:
        grads = [matmul_rows(lefts[name], rights[name]) for name in MATRICES]
        mats = dict(zip(MATRICES, reduce_matrices(grads)))
        vecs = reduce_vectors(members)
    return (
        decoder_input,
        grad_tokens,
        vecs[0],
        vecs[1],
        mats["qkv"],
        vecs[2],
        vecs[3],
        mats["out"],
        vecs[4],
        vecs[5],
        vecs[6],
        mats["up"],
        vecs[7],
        mats["down"],
        vecs[8],
        mats["proj"],
        vecs[9],
        vecs[10],
    )


def solution(mesh):
    placed = (
        P(("img", "pos"), None),
        P(("img", "pos")),
        P(("img", "pos")),
        P(),
        P(),
        P(),
        P(),
        P(),
        P(),
        P(),
        P(),
        P(),
        P(),
        P(),
        P(),
        P(),
        P(),
        P(),
        P(),
        P("img", "pos", None),
    )
    return jax.shard_map(
        per_device,
        mesh=mesh,
        in_specs=placed,
        out_specs=(
            P("img", "pos", None),
            P(("img", "pos"), None),
            P(),
            P(),
            P("img", None),
            P(),
            P(),
            P("img", None),
            P(),
            P(),
            P(),
            P("img", None),
            P(),
            P("img", None),
            P(),
            P("img", None),
            P(),
            P(),
        ),
        check_vma=False,
    )
```

```python
import functools

import jax
import jax.numpy as jnp
from jax import lax
from jax.experimental import pallas as pl
from jax.experimental.pallas import tpu as pltpu
from jax.sharding import PartitionSpec as P

HEADS = 12
HEAD_DIM = 64
ROWS_SEQ = 256
IMG_SEQ = 5
POSITIONS = 196
CAP = 16


EPSILON = 1e-05
NEGATIVE = -1e30
GELU_COEF = 0.7978845608028654


def layer_norm(values, gain_vec, shift_vec):
    centre = jnp.mean(values, axis=-1, keepdims=True)
    centred = values - centre
    return (
        centred
        * lax.rsqrt(jnp.mean(centred * centred, axis=-1, keepdims=True) + EPSILON)
        * gain_vec
        + shift_vec
    )


def gelu_tanh(values):
    return (
        0.5 * values * (1.0 + jnp.tanh(GELU_COEF * (values + 0.044715 * values * values * values)))
    )


def matmul_rows(left, right):
    return jnp.dot(left, right, preferred_element_type=jnp.float32)


def column_sums(values):
    return jnp.sum(values.astype(jnp.float32), axis=0)


def reduce_matrices(members):
    img_count = lax.axis_size("img")
    pos_count = lax.axis_size("pos")
    pieces = [member.reshape(img_count, pos_count, -1) for member in members]
    bucket = jnp.concatenate(pieces, axis=2)
    flat_bucket = bucket.reshape(img_count * pos_count, -1)
    share = lax.psum_scatter(flat_bucket, ("img", "pos"), scatter_dimension=0, tiled=True).reshape(
        1, 1, -1
    )
    summed = lax.all_gather(share.astype(jnp.bfloat16), "pos", axis=1, tiled=True).astype(
        share.dtype
    )
    results = []
    offset = 0
    for member in members:
        extent = member.size // (img_count * pos_count)
        block = summed[0, :, offset : offset + extent]
        results.append(block.reshape(member.shape[0] // img_count, member.shape[1]))
        offset = offset + extent
    return results


def reduce_vectors(members):
    return lax.psum(tuple(members), ("img", "pos"))


def general_device(
    tokens,
    image_slot,
    patch_position,
    ln1_gain,
    ln1_bias,
    w_qkv,
    bias_query,
    bias_value,
    w_out,
    bias_out,
    ln2_gain,
    ln2_bias,
    w_up,
    bias_up,
    w_down,
    bias_down,
    w_proj,
    bias_proj,
    mask_token,
    cotangent,
):
    seq_count = tokens.shape[0] // ROWS_SEQ
    width = w_out.shape[0]
    out_width = w_proj.shape[1]
    pos_count = lax.axis_size("pos")
    quarter_len = POSITIONS // pos_count
    score_scale = HEAD_DIM ** (-0.5)
    head_shape = (seq_count, ROWS_SEQ, HEADS, HEAD_DIM)
    rows_f = tokens.astype(jnp.float32)
    normed_low = layer_norm(rows_f, ln1_gain, ln1_bias).astype(jnp.bfloat16)
    qkv_all = matmul_rows(normed_low, w_qkv)
    queries = (qkv_all[:, :width] + bias_query).astype(jnp.bfloat16).reshape(head_shape)
    keys_h = qkv_all[:, width : 2 * width].astype(jnp.bfloat16).reshape(head_shape)
    values_h = (qkv_all[:, 2 * width :] + bias_value).astype(jnp.bfloat16).reshape(head_shape)
    slot_rows = image_slot.reshape(seq_count, ROWS_SEQ)
    allowed = slot_rows[:, None, :, None] == slot_rows[:, None, None, :]
    raw_scores = (
        jnp.einsum("sqhd,skhd->shqk", queries, keys_h, preferred_element_type=jnp.float32)
        * score_scale
    )
    scores = jnp.where(allowed, raw_scores, NEGATIVE)
    top_score = jnp.max(scores, axis=-1, keepdims=True)
    log_total = top_score + jnp.log(jnp.sum(jnp.exp(scores - top_score), axis=-1, keepdims=True))
    attn_probs = jnp.exp(scores - log_total)
    probs_low = attn_probs.astype(jnp.bfloat16)
    attended = jnp.einsum(
        "shqk,skhd->sqhd", probs_low, values_h, preferred_element_type=jnp.float32
    )
    attended = attended.reshape(-1, width).astype(jnp.bfloat16)
    residual = rows_f + matmul_rows(attended, w_out) + bias_out
    normed_mlp = layer_norm(residual, ln2_gain, ln2_bias).astype(jnp.bfloat16)
    up_proj = matmul_rows(normed_mlp, w_up) + bias_up
    hidden = gelu_tanh(up_proj).astype(jnp.bfloat16)
    block_out = residual + matmul_rows(hidden, w_down) + bias_down
    block_low = block_out.astype(jnp.bfloat16)
    projected = (matmul_rows(block_low, w_proj) + bias_proj).astype(jnp.bfloat16)
    row_index = jnp.arange(ROWS_SEQ, dtype=jnp.int32)
    pos_rows = patch_position.reshape(seq_count, ROWS_SEQ)
    live = slot_rows >= 0
    bucket_id = jnp.where(live, slot_rows * pos_count + pos_rows // quarter_len, -1)
    earlier = (bucket_id[:, :, None] == bucket_id[:, None, :]) & (
        row_index[None, :, None] > row_index[None, None, :]
    )
    rank_in = jnp.sum(earlier.astype(jnp.int32), axis=2)
    target = jnp.where(live, bucket_id * CAP + rank_in, -1)
    slot_index = jnp.arange(IMG_SEQ * pos_count * CAP, dtype=jnp.int32)
    selected = slot_index[None, :, None] == target[:, None, :]
    select_low = selected.astype(jnp.bfloat16)
    outgoing = jnp.einsum(
        "sjr,src->sjc",
        select_low,
        projected.reshape(seq_count, ROWS_SEQ, out_width),
        preferred_element_type=jnp.float32,
    ).astype(jnp.bfloat16)
    outgoing = outgoing.reshape(seq_count * IMG_SEQ, pos_count, CAP, out_width)
    slot_place = (
        jnp.sum(jnp.where(selected, (pos_rows % quarter_len + 1)[:, None, :], 0), axis=2) - 1
    )
    slot_place = slot_place.reshape(seq_count * IMG_SEQ, pos_count, CAP)
    arrived, arrived_place = (
        lax.all_to_all(outgoing, "pos", split_axis=1, concat_axis=0, tiled=True),
        lax.all_to_all(slot_place, "pos", split_axis=1, concat_axis=0, tiled=True),
    )
    arrived = arrived[:, 0]
    arrived_place = arrived_place[:, 0]
    placing = jnp.arange(quarter_len, dtype=jnp.int32)[None, :, None] == arrived_place[:, None, :]
    placing_low = placing.astype(jnp.bfloat16)
    visible = jnp.any(placing, axis=2)
    filled = jnp.einsum("gqj,gjc->gqc", placing_low, arrived, preferred_element_type=jnp.float32)
    decoder_input = jnp.where(
        visible[:, :, None], filled, mask_token.astype(jnp.float32)[None, None, :]
    )
    decoder_input = decoder_input.astype(jnp.bfloat16)
    grad_mask = jnp.sum(
        jnp.where(visible[:, :, None], 0.0, cotangent.astype(jnp.float32)), axis=(0, 1)
    )
    back_slots = jnp.einsum(
        "gqj,gqc->gjc", placing_low, cotangent, preferred_element_type=jnp.float32
    ).astype(jnp.bfloat16)
    returned = lax.all_to_all(back_slots[:, None], "pos", split_axis=0, concat_axis=1, tiled=True)
    delta_proj = (
        jnp.einsum(
            "sjr,sjc->src",
            select_low,
            returned.reshape(seq_count, -1, out_width),
            preferred_element_type=jnp.float32,
        )
        .reshape(-1, out_width)
        .astype(jnp.bfloat16)
    )
    grad_proj = jnp.einsum("rd,rc->dc", block_low, delta_proj, preferred_element_type=jnp.float32)
    grad_bproj = column_sums(delta_proj)
    delta_block = jnp.einsum("rc,dc->rd", delta_proj, w_proj, preferred_element_type=jnp.float32)
    delta_down = delta_block.astype(jnp.bfloat16)
    grad_down = jnp.einsum("rf,rd->fd", hidden, delta_down, preferred_element_type=jnp.float32)
    grad_bdown = column_sums(delta_down)
    delta_hidden = jnp.einsum("rd,fd->rf", delta_down, w_down, preferred_element_type=jnp.float32)
    gelu_back = jax.vjp(gelu_tanh, up_proj)[1]
    delta_up = gelu_back(delta_hidden)[0].astype(jnp.bfloat16)
    grad_up = jnp.einsum("rd,rf->df", normed_mlp, delta_up, preferred_element_type=jnp.float32)
    grad_bup = column_sums(delta_up)
    delta_normed = jnp.einsum("rf,df->rd", delta_up, w_up, preferred_element_type=jnp.float32)
    norm_back = jax.vjp(layer_norm, residual, ln2_gain, ln2_bias)[1]
    delta_resid_norm, grad_gain_two, grad_shift_two = norm_back(delta_normed)
    delta_residual = delta_block + delta_resid_norm
    mlp_mats = reduce_matrices((grad_proj, grad_down, grad_up))
    mlp_vecs = reduce_vectors(
        (grad_bproj, grad_bdown, grad_bup, grad_gain_two, grad_shift_two, grad_mask)
    )
    delta_branch = delta_residual.astype(jnp.bfloat16)
    grad_out = jnp.einsum("re,rd->ed", attended, delta_branch, preferred_element_type=jnp.float32)
    grad_bout = column_sums(delta_branch)
    delta_attended = jnp.einsum(
        "rd,ed->re", delta_branch, w_out, preferred_element_type=jnp.float32
    )
    delta_attended = delta_attended.astype(jnp.bfloat16).reshape(head_shape)
    delta_values = jnp.einsum(
        "shqk,sqhd->skhd", probs_low, delta_attended, preferred_element_type=jnp.float32
    ).astype(jnp.bfloat16)
    delta_probs = jnp.einsum(
        "sqhd,skhd->shqk", delta_attended, values_h, preferred_element_type=jnp.float32
    )
    delta_scores = attn_probs * (
        delta_probs - jnp.sum(delta_probs * attn_probs, axis=-1, keepdims=True)
    )
    delta_scores = delta_scores.astype(jnp.bfloat16)
    delta_queries = (
        (
            jnp.einsum("shqk,skhd->sqhd", delta_scores, keys_h, preferred_element_type=jnp.float32)
            * score_scale
        )
        .astype(jnp.bfloat16)
        .reshape(-1, width)
    )
    delta_keys = (
        (
            jnp.einsum("shqk,sqhd->skhd", delta_scores, queries, preferred_element_type=jnp.float32)
            * score_scale
        )
        .astype(jnp.bfloat16)
        .reshape(-1, width)
    )
    delta_values = delta_values.reshape(-1, width)
    delta_qkv = jnp.concatenate([delta_queries, delta_keys, delta_values], axis=1)
    grad_qkv = jnp.einsum("rd,re->de", normed_low, delta_qkv, preferred_element_type=jnp.float32)
    grad_bquery = column_sums(delta_queries)
    grad_bvalue = column_sums(delta_values)
    delta_first = jnp.einsum("re,de->rd", delta_qkv, w_qkv, preferred_element_type=jnp.float32)
    first_back = jax.vjp(layer_norm, rows_f, ln1_gain, ln1_bias)[1]
    delta_rows, grad_gain_one, grad_shift_one = first_back(delta_first)
    grad_tokens = (delta_residual + delta_rows).astype(jnp.bfloat16)
    attn_mats = reduce_matrices((grad_qkv, grad_out))
    attn_vecs = reduce_vectors((grad_bquery, grad_bvalue, grad_bout, grad_gain_one, grad_shift_one))
    return (
        decoder_input,
        grad_tokens,
        attn_vecs[3],
        attn_vecs[4],
        attn_mats[0],
        attn_vecs[0],
        attn_vecs[1],
        attn_mats[1],
        attn_vecs[2],
        mlp_vecs[3],
        mlp_vecs[4],
        mlp_mats[2],
        mlp_vecs[2],
        mlp_mats[1],
        mlp_vecs[1],
        mlp_mats[0],
        mlp_vecs[0],
        mlp_vecs[5],
    )


MESH_ID = pl.DeviceIdType.MESH
LOW = jnp.bfloat16
FULL = jnp.float32

AXES = ("zh", "zl", "x", "y")
MATRICES = ("down", "up", "proj", "out", "qkv")
JOBS = (
    ("down", 0, 256, ("zl", "zh", "x", "y")),
    ("down", 256, 256, ("zl", "zh", "x", "y")),
    ("down", 512, 256, ("zl", "zh", "x", "y")),
    ("up", 0, 512, ("y", "x", "zl", "zh")),
    ("up", 512, 512, ("y", "x", "zl", "zh")),
    ("up", 1024, 512, ("y", "x", "zl", "zh")),
    ("proj", 0, 256, ("x", "y", "zl", "zh")),
    ("out", 0, 384, ("x", "y", "zl", "zh")),
    ("qkv", 0, 384, ("x", "y", "zl", "zh")),
    ("qkv", 384, 384, ("x", "y", "zl", "zh")),
    ("qkv", 768, 384, ("x", "y", "zl", "zh")),
)
ORDER = (
    (6, 0),
    (0, 0),
    (3, 0),
    (7, 0),
    (1, 0),
    (4, 0),
    (3, 1),
    (2, 0),
    (8, 0),
    (5, 0),
    (6, 1),
    (0, 1),
    (7, 1),
    (9, 0),
    (1, 1),
    (8, 1),
    (3, 2),
    (9, 1),
    (10, 0),
    (2, 1),
    (6, 2),
    (4, 1),
    (7, 2),
    (10, 1),
    (8, 2),
    (3, 3),
    (5, 1),
    (9, 2),
    (6, 3),
    (3, 4),
    (0, 2),
    (4, 2),
    (6, 4),
    (7, 3),
    (3, 5),
    (1, 2),
    (10, 2),
    (0, 3),
    (6, 5),
    (8, 3),
    (2, 2),
    (7, 4),
    (1, 3),
    (5, 2),
    (0, 4),
    (9, 3),
    (7, 5),
    (8, 4),
    (4, 3),
    (2, 3),
    (10, 3),
    (0, 5),
    (1, 4),
    (8, 5),
    (5, 3),
    (9, 4),
    (4, 4),
    (1, 5),
    (2, 4),
    (9, 5),
    (10, 4),
    (4, 5),
    (5, 4),
    (2, 5),
    (10, 5),
    (5, 5),
)
VEC_STEPS = ("core", "x", "y", "zl", "zh")
PEERS = ("y", "core", "diagonal")
PLACES = 64
LN1_GAIN, LN1_BIAS, BIAS_Q, BIAS_V, BIAS_OUT, LN2_GAIN, LN2_BIAS, BIAS_DOWN, BIAS_UP, BIAS_PROJ, MASK = (
    0, 1, 2, 3, 4, 5, 6, 7, 8, 12, 13,
)


def device_coords():
    img = lax.axis_index("img")
    pos = lax.axis_index("pos")
    return {"zh": img // 4, "zl": (img // 2) % 2, "x": img % 2, "y": pos // 2, "core": pos % 2}


def device_of(where):
    return (where["zh"] * 4 + where["zl"] * 2 + where["x"], where["y"] * 2 + where["core"])


def block_rows(name):
    return 96 if name == "down" else 48


def dot(left, right):
    return jnp.dot(left, right, preferred_element_type=FULL)


def dot_nt(left, right):
    return lax.dot_general(left, right, (((1,), (1,)), ((), ())), preferred_element_type=FULL)


def dot_tn(left, right):
    return lax.dot_general(left, right, (((0,), (0,)), ((), ())), preferred_element_type=FULL)


def normalised(values):
    centred = values - jnp.mean(values, axis=-1, keepdims=True)
    rstd = lax.rsqrt(jnp.mean(centred * centred, axis=-1, keepdims=True) + EPSILON)
    return centred * rstd, rstd


def norm_rows_back(delta, values, gain):
    xhat, rstd = normalised(values)
    scaled = delta * gain
    rows = rstd * (
        scaled
        - jnp.mean(scaled, axis=-1, keepdims=True)
        - xhat * jnp.mean(scaled * xhat, axis=-1, keepdims=True)
    )
    return rows, delta * xhat


def layer_kernel(names, *refs):
    ref = dict(zip(names, refs))
    me = device_coords()
    core = me["core"]
    my_pos = me["y"] * 2 + core
    width = ref["tokens"].shape[1]
    ff = ref["w_up"].shape[1]
    quarter_len = POSITIONS // 4

    def peer(axis):
        if axis == "diagonal":
            return device_of({**me, "y": 1 - me["y"], "core": 1 - core})
        return device_of({**me, axis: 1 - me[axis]})

    started = []

    def remote(source, target, kind, spot, axis):
        return pltpu.make_async_remote_copy(
            src_ref=source,
            dst_ref=target,
            send_sem=ref[kind + "_send"].at[spot],
            recv_sem=ref[kind + "_recv"].at[spot],
            device_id=peer(axis),
            device_id_type=MESH_ID,
        )

    def begin(copy):
        copy.start()
        started.append(copy)

    loads = {}
    for number, name in enumerate(("w_qkv", "w_out", "w_proj", "w_up", "w_down")):
        loads[name] = pltpu.make_async_copy(ref[name], ref[name + "_held"], ref["load"].at[number])
        loads[name].start()

    barrier = pltpu.get_barrier_semaphore()
    for axis in AXES + ("core", "diagonal"):
        pl.semaphore_signal(barrier, inc=1, device_id=peer(axis), device_id_type=MESH_ID)

    ref["places"][my_pos, 0:1, :] = ref["slot"][...]
    ref["places"][my_pos, 1:2, :] = ref["position"][...]

    def first_norm(step, carry):
        rows = pl.ds(pl.multiple_of(step * 64, 64), 64)
        xhat, _ = normalised(ref["tokens"][rows, :].astype(FULL))
        ref["normed"][rows, :] = (xhat * ref["ln1_gain"][...] + ref["ln1_bias"][...]).astype(LOW)
        return carry

    lax.fori_loop(0, 4, first_norm, 0)

    pl.semaphore_wait(barrier, 6)
    for number, axis in enumerate(PEERS):
        begin(remote(ref["places"].at[my_pos], ref["places"].at[my_pos], "place", number, axis))

    loads["w_qkv"].wait()
    third = width // 256
    for number in range(3 * third):
        columns = slice(number * 256, (number + 1) * 256)
        part = dot(ref["normed"][...], ref["w_qkv_held"][:, columns])
        if number < third:
            part = part + ref["bias_query"][:, columns]
            part = part.astype(LOW) * LOW(HEAD_DIM ** (-0.5))
        elif number >= 2 * third:
            part = part + ref["bias_value"][:, (number - 2 * third) * 256 : (number - 2 * third + 1) * 256]
        ref["qkv"][:, columns] = part.astype(LOW)
    ref["left_qkv"][...] = ref["normed"][...].T

    row_ids = lax.broadcasted_iota(jnp.int32, (ROWS_SEQ, ROWS_SEQ), 0)
    lane_ids = lax.broadcasted_iota(jnp.int32, (ROWS_SEQ, ROWS_SEQ), 1)
    earlier = (row_ids < lane_ids).astype(FULL).astype(LOW)

    def one_hot(count, row):
        ids = lax.broadcasted_iota(jnp.int32, (count, ROWS_SEQ), 0)
        return jnp.where(ids == row, 1.0, 0.0)

    def picked(slot, position, quarter):
        offset = position - quarter * quarter_len
        inside = (slot >= 0) & (offset >= 0) & (offset < quarter_len)
        kinds = one_hot(8, jnp.where(inside, slot, -1))
        ranks = jnp.sum(kinds * dot(kinds.astype(LOW), earlier), axis=0, keepdims=True).astype(jnp.int32)
        chosen = one_hot(IMG_SEQ * CAP, jnp.where(inside, slot * CAP + ranks, -1))
        return chosen.astype(LOW), jnp.where(inside, slot * PLACES + offset, -1)

    for quarter in range(4):
        chosen, _ = picked(ref["slot"][...], ref["position"][...], quarter)
        ref["chosen"][quarter] = chosen

    slots = one_hot(8, ref["slot"][...] + 1).astype(LOW)
    ref["allowed"][...] = jnp.where(dot_tn(slots, slots) > 0.5, 0.0, NEGATIVE)

    ref["cot_wide"][...] = jnp.zeros_like(ref["cot_wide"])
    for image in range(4 * IMG_SEQ):
        ref["cot_wide"][image, 0:quarter_len, :] = ref["cotangent"][image]
    mask_sum = jnp.zeros((8, ref["cotangent"].shape[2]), FULL)
    for number, axis in enumerate(PEERS + ("self",)):
        if axis == "self":
            source = my_pos
        else:
            source = peer(axis)[1]
            remote(ref["places"].at[source], ref["places"].at[source], "place", number, axis).wait_recv()
        slot = ref["places"][source, 0:1, :]
        position = ref["places"][source, 1:2, :]
        chosen, place = picked(slot, position, my_pos)
        filled = one_hot(IMG_SEQ * PLACES, place).astype(LOW)
        placing = dot_nt(filled, chosen)
        placing_low = placing.astype(LOW)
        ref["placing"][number] = placing_low
        cot = ref["cot_wide"][pl.ds(source * IMG_SEQ, IMG_SEQ)].reshape(IMG_SEQ * PLACES, -1)
        back = dot_tn(placing_low, cot).astype(LOW)
        if axis == "self":
            ref["back_in"][my_pos] = back
        else:
            ref["back_out"][number] = back
            begin(remote(ref["back_out"].at[number], ref["back_in"].at[my_pos], "back", number, axis))
        seen = dot_nt(jnp.ones((8, IMG_SEQ * CAP), LOW), placing_low)
        mask_sum = mask_sum + dot((1.0 - seen).astype(LOW), cot)
    ref["vec_own"][...] = jnp.zeros_like(ref["vec_own"])
    ref["vec_own"][MASK : MASK + 1, : mask_sum.shape[1]] = mask_sum[0:1]

    lane = lax.broadcasted_iota(jnp.int32, (1, 2 * HEAD_DIM), 1)
    sides_full = [(lane < HEAD_DIM).astype(FULL), (lane >= HEAD_DIM).astype(FULL)]
    sides = [side.astype(LOW) for side in sides_full]

    def head_columns(pair, first):
        return pl.ds(pl.multiple_of(first + pair * 2 * HEAD_DIM, 2 * HEAD_DIM), 2 * HEAD_DIM)

    def attend(pair, carry):
        queries = ref["qkv"][:, head_columns(pair, 0)]
        keys = ref["qkv"][:, head_columns(pair, width)]
        values = ref["qkv"][:, head_columns(pair, 2 * width)]
        total = None
        for side in range(2):
            scores = dot_nt(queries * sides[side], keys) + ref["allowed"][...]
            powers = jnp.exp(scores - jnp.max(scores, axis=-1, keepdims=True))
            probs = powers / jnp.sum(powers, axis=-1, keepdims=True)
            ref["probs"][pair * 2 + side] = probs
            part = dot(probs.astype(LOW), values) * sides_full[side]
            total = part if total is None else total + part
        ref["attended"][:, head_columns(pair, 0)] = total.astype(LOW)
        return carry

    lax.fori_loop(0, HEADS // 2, attend, 0)
    ref["left_out"][...] = ref["attended"][...].T

    loads["w_out"].wait()
    for number in range(third):
        columns = slice(number * 256, (number + 1) * 256)
        ref["residual"][:, columns] = (
            ref["tokens"][:, columns].astype(FULL)
            + dot(ref["attended"][...], ref["w_out_held"][:, columns])
            + ref["bias_out"][:, columns]
        )

    def second_norm(step, carry):
        rows = pl.ds(pl.multiple_of(step * 64, 64), 64)
        xhat, _ = normalised(ref["residual"][rows, :])
        ref["normed"][rows, :] = (xhat * ref["ln2_gain"][...] + ref["ln2_bias"][...]).astype(LOW)
        return carry

    lax.fori_loop(0, 4, second_norm, 0)
    ref["left_up"][...] = ref["normed"][...].T

    loads["w_proj"].wait()
    for number, axis in enumerate(PEERS):
        remote(ref["back_out"].at[number], ref["back_in"].at[my_pos], "back", number, axis).wait_recv()
    chosen_all = ref["chosen"][...].reshape(4 * IMG_SEQ * CAP, ROWS_SEQ)
    returned = ref["back_in"][...].reshape(4 * IMG_SEQ * CAP, -1)
    delta_proj = dot_tn(chosen_all, returned)
    ref["vec_own"][BIAS_PROJ : BIAS_PROJ + 1, : delta_proj.shape[1]] = jnp.sum(delta_proj, axis=0, keepdims=True)
    ref["right_proj"][...] = delta_proj.astype(LOW)
    for number in range(third):
        columns = slice(number * 256, (number + 1) * 256)
        part = dot_nt(ref["right_proj"][...], ref["w_proj_held"][columns, :])
        ref["delta_block"][:, columns] = part
        part = part.astype(LOW)
        ref["right_down"][:, columns] = part
        ref["vec_own"][BIAS_DOWN : BIAS_DOWN + 1, columns] = jnp.sum(part.astype(FULL), axis=0, keepdims=True)

    loads["w_up"].wait()
    loads["w_down"].wait()
    ref["mlp_out"][...] = jnp.zeros_like(ref["mlp_out"])
    ref["delta_normed"][...] = jnp.zeros_like(ref["delta_normed"])

    def feed(step, carry):
        columns = pl.ds(pl.multiple_of(step * 256, 256), 256)
        up = dot(ref["normed"][...], ref["w_up_held"][:, columns]) + ref["bias_up"][:, columns]
        square = up * up
        bent = jnp.tanh(GELU_COEF * (up + 0.044715 * up * square))
        half = 0.5 * (1.0 + bent)
        slope = half + 0.5 * up * (1.0 - bent * bent) * (GELU_COEF * (1.0 + 0.134145 * square))
        hidden = (up * half).astype(LOW)
        ref["left_down"][columns, :] = hidden.T
        back = dot_nt(ref["right_down"][...], ref["w_down_held"][columns, :])
        delta_up = (back * slope).astype(LOW)
        ref["right_up"][:, columns] = delta_up
        ref["bias_up_sum"][:, columns] = jnp.sum(delta_up.astype(FULL), axis=0, keepdims=True)
        ref["mlp_out"][...] += dot(hidden, ref["w_down_held"][columns, :])
        ref["delta_normed"][...] += dot_nt(delta_up, ref["w_up_held"][:, columns])
        return carry

    lax.fori_loop(0, ff // 256, feed, 0)
    for number in range(ff // width):
        ref["vec_own"][BIAS_UP + number : BIAS_UP + number + 1, :] = ref["bias_up_sum"][
            :, number * width : (number + 1) * width
        ]

    def half_columns(name, side):
        wide = ref["right_" + name].shape[1] // 2
        return pl.ds(pl.multiple_of(side * wide, 128), wide)

    def core_copies(name):
        spot = MATRICES.index(name)
        if name == "down":
            left = ref["left_down"].reshape(8, 2, 192, ROWS_SEQ).at[:, 1 - core]
            right = ref["right_down"]
        else:
            left = ref["left_" + name]
            right = ref["right_" + name].at[:, half_columns(name, 1 - core)]
        return (
            remote(left, ref["left_in_" + name], "core", (spot, 0), "core"),
            remote(right, ref["right_in_" + name], "core", (spot, 1), "core"),
        )

    def swap(name):
        for copy in core_copies(name):
            begin(copy)

    def job_copy(number, stage):
        name, first, wide, dims = JOBS[number]
        columns = pl.ds(first, wide)
        if stage < 4:
            pick = []
            for axis in AXES:
                if axis in dims[:stage]:
                    pick.append(me[axis])
                elif axis == dims[stage]:
                    pick.append(1 - me[axis])
                else:
                    pick.append(slice(None))
            source = ref["partial%d" % number].at[tuple(pick)]
            return remote(source, ref["landed%d_%d" % (number, stage)], "job", (number, stage), dims[stage])
        if stage == 4:
            place = ref["final_" + name].at[core, me["y"], :, columns]
            return remote(place, place, "job", (number, stage), "y")
        place = ref["final_" + name].at[core, :, :, columns]
        return remote(place, place, "job", (number, stage), "core")

    def multiply(name):
        numbers = [number for number, job in enumerate(JOBS) if job[0] == name]
        for copy in core_copies(name):
            copy.wait_recv()
        rows = block_rows(name)
        left, right = ref["left_" + name], ref["right_" + name]
        left_in, right_in = ref["left_in_" + name], ref["right_in_" + name]
        if name == "down":
            for block in range(8):
                spot = pl.multiple_of(block * 384 + core * 192, 192)
                total = dot(left[pl.ds(spot, 192), :], right[...]) + dot(left_in[block], right_in[...])
                total = total.astype(LOW)
                for number in numbers:
                    _, first, wide, _ = JOBS[number]
                    for half in range(2):
                        ref["partial%d" % number][block // 4, (block // 2) % 2, block % 2, half] = total[
                            half * rows : (half + 1) * rows, first : first + wide
                        ]
            for number in numbers:
                begin(job_copy(number, 0))
            return
        wide_half = right.shape[1] // 2
        for number in numbers:
            _, first, wide, _ = JOBS[number]
            columns = pl.ds(pl.multiple_of(core * wide_half + first, 128), wide)
            for high in range(2):
                span = slice(high * 8 * rows, (high + 1) * 8 * rows)
                total = dot(left[span, :], right[:, columns]) + dot(
                    left_in[span, :], right_in[:, first : first + wide]
                )
                total = total.astype(LOW)
                for part in range(8):
                    ref["partial%d" % number][high, part // 4, (part // 2) % 2, part % 2] = total[
                        part * rows : (part + 1) * rows
                    ]
            begin(job_copy(number, 0))

    def arrive(number, stage):
        name, first, wide, dims = JOBS[number]
        job_copy(number, stage).wait_recv()
        if stage < 4:
            partial, landed = ref["partial%d" % number], ref["landed%d_%d" % (number, stage)]
            fixed = dims[: stage + 1]
            free = [axis for axis in AXES if axis not in fixed]
            for code in range(2 ** len(free)):
                bits = {axis: (code >> (len(free) - 1 - spot)) % 2 for spot, axis in enumerate(free)}
                here = tuple(me[axis] if axis in fixed else bits[axis] for axis in AXES)
                sums = partial[here] + landed[tuple(bits[axis] for axis in free)]
                if stage < 3:
                    partial[here] = sums
                else:
                    ref["final_" + name][core, me["y"], :, first : first + wide] = sums
        if stage < 5:
            begin(job_copy(number, stage + 1))

    def vec_copy(stage):
        return remote(ref["vec_held"].at[stage], ref["vec_in"].at[stage], "vec", stage, VEC_STEPS[stage])

    def arrive_vec(stage):
        vec_copy(stage).wait_recv()
        sums = ref["vec_held"][stage] + ref["vec_in"][stage]
        if stage < 4:
            ref["vec_held"][stage + 1] = sums
            begin(vec_copy(stage + 1))
        else:
            ref["vec_sums"][...] = sums

    swap("down")
    swap("up")

    for number in range(third):
        columns = slice(number * 256, (number + 1) * 256)
        ref["block_low"][:, columns] = (
            ref["residual"][:, columns] + ref["mlp_out"][:, columns] + ref["bias_down"][:, columns]
        ).astype(LOW)
    ref["left_proj"][...] = ref["block_low"][...].T
    swap("proj")
    projected = (dot(ref["block_low"][...], ref["w_proj_held"][...]) + ref["bias_proj"][...]).astype(LOW)
    outgoing = dot(chosen_all, projected).astype(LOW)
    ref["grid_out"][...] = outgoing.reshape(4, IMG_SEQ * CAP, -1)
    for number, axis in enumerate(PEERS):
        begin(remote(ref["grid_out"].at[peer(axis)[1]], ref["grid_in"].at[number], "grid", number, axis))

    multiply("down")
    multiply("up")
    multiply("proj")

    def second_back(step, sums):
        rows = pl.ds(pl.multiple_of(step * 64, 64), 64)
        delta = ref["delta_normed"][rows, :]
        row_term, gains = norm_rows_back(delta, ref["residual"][rows, :], ref["ln2_gain"][...])
        total = ref["delta_block"][rows, :] + row_term
        low = total.astype(LOW)
        ref["delta_block"][rows, :] = total
        ref["right_out"][rows, :] = low
        news = (gains, delta, low.astype(FULL))
        return tuple(old + jnp.sum(new, axis=0, keepdims=True) for old, new in zip(sums, news))

    zeros = jnp.zeros((1, width), FULL)
    sums = lax.fori_loop(0, 4, second_back, (zeros, zeros, zeros))
    for spot, total in zip((LN2_GAIN, LN2_BIAS, BIAS_OUT), sums):
        ref["vec_own"][spot : spot + 1, :] = total
    swap("out")
    for number in range(third):
        columns = slice(number * 256, (number + 1) * 256)
        ref["delta_attended"][:, columns] = dot_nt(ref["right_out"][...], ref["w_out_held"][columns, :]).astype(LOW)

    def attend_back(pair, carry):
        queries = ref["qkv"][:, head_columns(pair, 0)]
        keys = ref["qkv"][:, head_columns(pair, width)]
        values = ref["qkv"][:, head_columns(pair, 2 * width)]
        delta = ref["delta_attended"][:, head_columns(pair, 0)]
        totals = [None, None, None]
        for side in range(2):
            probs = ref["probs"][pair * 2 + side]
            delta_probs = dot_nt(delta * sides[side], values)
            delta_scores = probs * (delta_probs - jnp.sum(delta_probs * probs, axis=-1, keepdims=True))
            delta_scores = delta_scores.astype(LOW)
            parts = (
                dot(delta_scores, keys) * (HEAD_DIM ** (-0.5)),
                dot_tn(delta_scores, queries),
                dot_tn(probs.astype(LOW), delta),
            )
            for spot, part in enumerate(parts):
                part = part * sides_full[side]
                totals[spot] = part if totals[spot] is None else totals[spot] + part
        for spot, total in enumerate(totals):
            ref["right_qkv"][:, head_columns(pair, spot * width)] = total.astype(LOW)
        return carry

    lax.fori_loop(0, HEADS // 2, attend_back, 0)
    swap("qkv")
    multiply("out")
    for number in range(third):
        columns = slice(number * 256, (number + 1) * 256)
        part = dot_nt(ref["right_qkv"][...], ref["w_qkv_held"][columns, :])
        ref["delta_normed"][:, columns] = part
    for spot, first in ((BIAS_Q, 0), (BIAS_V, 2 * width)):
        ref["vec_own"][spot : spot + 1, :] = jnp.sum(
            ref["right_qkv"][:, first : first + width].astype(FULL), axis=0, keepdims=True
        )
    multiply("qkv")

    def first_back(step, sums):
        rows = pl.ds(pl.multiple_of(step * 64, 64), 64)
        delta = ref["delta_normed"][rows, :]
        row_term, gains = norm_rows_back(delta, ref["tokens"][rows, :].astype(FULL), ref["ln1_gain"][...])
        ref["grad_tokens"][rows, :] = (ref["delta_block"][rows, :] + row_term).astype(LOW)
        return tuple(old + jnp.sum(new, axis=0, keepdims=True) for old, new in zip(sums, (gains, delta)))

    sums = lax.fori_loop(0, 4, first_back, (zeros, zeros))
    for spot, total in zip((LN1_GAIN, LN1_BIAS), sums):
        ref["vec_own"][spot : spot + 1, :] = total
    ref["vec_held"][0] = ref["vec_own"][...]
    begin(vec_copy(0))

    for number, axis in enumerate(PEERS + ("self",)):
        if axis == "self":
            source = my_pos
            arrived = ref["grid_out"][my_pos]
        else:
            source = peer(axis)[1]
            remote(ref["grid_out"].at[source], ref["grid_in"].at[number], "grid", number, axis).wait_recv()
            arrived = ref["grid_in"][number]
        placing = ref["placing"][number]
        visible = jnp.sum(placing.astype(FULL), axis=1, keepdims=True)
        filled = jnp.where(visible > 0.5, dot(placing, arrived), ref["mask_token"][...].astype(FULL)).astype(LOW)
        for image in range(IMG_SEQ):
            ref["decoder_input"][source * IMG_SEQ + image] = filled[
                image * PLACES : image * PLACES + quarter_len
            ]

    for spot, (number, stage) in enumerate(ORDER):
        arrive(number, stage)
        if spot % 6 == 5 and spot // 6 < 5:
            arrive_vec(spot // 6)
    for name in MATRICES:
        rows = block_rows(name)
        final, out = ref["final_" + name], ref["grad_" + name]
        wide = final.shape[3]
        for side in range(2):
            for half in range(2):
                piece = final[side, half]
                if name == "down":
                    out[(side * 2 + half) * rows : (side * 2 + half + 1) * rows, :] = piece
                else:
                    out[half * rows : (half + 1) * rows, side * wide : (side + 1) * wide] = piece
    for copy in started:
        copy.wait_send()


def finish_kernel(*refs):
    ins, outs = refs[:8], refs[8:]
    for source, target in zip(ins[:7], outs[:7]):
        target[...] = source[...].astype(target.dtype)
    sums = ins[7]
    for spot, target in zip(
        (LN1_GAIN, LN1_BIAS, BIAS_Q, BIAS_V, BIAS_OUT, LN2_GAIN, LN2_BIAS, BIAS_DOWN, BIAS_PROJ, MASK), outs[7:17]
    ):
        target[...] = sums[spot : spot + 1, : target.shape[1]]
    wide = sums.shape[1]
    for number in range(outs[17].shape[1] // wide):
        outs[17][:, number * wide : (number + 1) * wide] = sums[BIAS_UP + number : BIAS_UP + number + 1, :]


def layer_device(
    tokens,
    image_slot,
    patch_position,
    ln1_gain,
    ln1_bias,
    w_qkv,
    bias_query,
    bias_value,
    w_out,
    bias_out,
    ln2_gain,
    ln2_bias,
    w_up,
    bias_up,
    w_down,
    bias_down,
    w_proj,
    bias_proj,
    mask_token,
    cotangent,
):
    rows, width = tokens.shape
    ff = w_up.shape[1]
    out_width = w_proj.shape[1]
    row = lambda vec: vec.reshape(1, -1)
    vmem = pl.BlockSpec(memory_space=pltpu.VMEM)
    hbm = pl.BlockSpec(memory_space=pl.ANY)
    inputs = {
        "tokens": tokens,
        "slot": row(image_slot),
        "position": row(patch_position),
        "ln1_gain": row(ln1_gain),
        "ln1_bias": row(ln1_bias),
        "bias_query": row(bias_query),
        "bias_value": row(bias_value),
        "bias_out": row(bias_out),
        "ln2_gain": row(ln2_gain),
        "ln2_bias": row(ln2_bias),
        "bias_up": row(bias_up),
        "bias_down": row(bias_down),
        "bias_proj": row(bias_proj),
        "mask_token": row(mask_token),
        "cotangent": cotangent,
        "w_qkv": w_qkv,
        "w_out": w_out,
        "w_proj": w_proj,
        "w_up": w_up,
        "w_down": w_down,
    }
    lefts = {"down": ff, "up": width, "proj": width, "out": width, "qkv": width}
    rights = {"down": width, "up": ff, "proj": out_width, "out": width, "qkv": 3 * width}
    results = {name: jax.ShapeDtypeStruct((lefts[name] // 8, rights[name]), LOW) for name in MATRICES}
    outs = {"grad_" + name: results[name] for name in MATRICES}
    outs["decoder_input"] = jax.ShapeDtypeStruct(cotangent.shape, LOW)
    outs["grad_tokens"] = jax.ShapeDtypeStruct(tokens.shape, LOW)
    outs["vec_sums"] = jax.ShapeDtypeStruct((16, width), FULL)
    dma = pltpu.SemaphoreType.DMA
    room = {
        "w_qkv_held": (w_qkv.shape, LOW),
        "w_out_held": (w_out.shape, LOW),
        "w_proj_held": (w_proj.shape, LOW),
        "w_up_held": (w_up.shape, LOW),
        "w_down_held": (w_down.shape, LOW),
        "places": ((4, 8, rows), jnp.int32),
        "chosen": ((4, IMG_SEQ * CAP, rows), LOW),
        "placing": ((4, IMG_SEQ * PLACES, IMG_SEQ * CAP), LOW),
        "allowed": ((rows, rows), FULL),
        "cot_wide": ((4 * IMG_SEQ, PLACES, out_width), LOW),
        "back_out": ((3, IMG_SEQ * CAP, out_width), LOW),
        "back_in": ((4, IMG_SEQ * CAP, out_width), LOW),
        "grid_out": ((4, IMG_SEQ * CAP, out_width), LOW),
        "grid_in": ((3, IMG_SEQ * CAP, out_width), LOW),
        "normed": ((rows, width), LOW),
        "qkv": ((rows, 3 * width), LOW),
        "probs": ((HEADS, rows, rows), FULL),
        "attended": ((rows, width), LOW),
        "residual": ((rows, width), FULL),
        "delta_block": ((rows, width), FULL),
        "mlp_out": ((rows, width), FULL),
        "delta_normed": ((rows, width), FULL),
        "block_low": ((rows, width), LOW),
        "delta_attended": ((rows, width), LOW),
        "bias_up_sum": ((1, ff), FULL),
        "vec_own": ((16, width), FULL),
        "vec_held": ((5, 16, width), FULL),
        "vec_in": ((5, 16, width), FULL),
    }
    for name in MATRICES:
        room["left_" + name] = ((lefts[name], rows), LOW)
        room["right_" + name] = ((rows, rights[name]), LOW)
        if name == "down":
            room["left_in_down"] = ((8, 192, rows), LOW)
            room["right_in_down"] = ((rows, rights[name]), LOW)
            room["final_down"] = ((2, 2, 96, rights[name]), LOW)
        else:
            room["left_in_" + name] = ((lefts[name], rows), LOW)
            room["right_in_" + name] = ((rows, rights[name] // 2), LOW)
            room["final_" + name] = ((2, 2, 48, rights[name] // 2), LOW)
    for number, (name, _, wide, _) in enumerate(JOBS):
        block = (block_rows(name), wide)
        room["partial%d" % number] = ((2, 2, 2, 2) + block, LOW)
        for stage in range(4):
            room["landed%d_%d" % (number, stage)] = ((2,) * (3 - stage) + block, LOW)
    scratch = {name: pltpu.VMEM(shape, dtype) for name, (shape, dtype) in room.items()}
    scratch["load"] = dma((5,))
    for kind, shape in (
        ("place", (3,)),
        ("back", (3,)),
        ("grid", (3,)),
        ("core", (5, 2)),
        ("job", (len(JOBS), 6)),
        ("vec", (5,)),
    ):
        scratch[kind + "_send"] = dma(shape)
        scratch[kind + "_recv"] = dma(shape)
    names = tuple(inputs) + tuple(outs) + tuple(scratch)
    found = pl.pallas_call(
        functools.partial(layer_kernel, names),
        out_shape=list(outs.values()),
        in_specs=[hbm if name.startswith("w_") else vmem for name in inputs],
        out_specs=[vmem] * len(outs),
        scratch_shapes=list(scratch.values()),
        compiler_params=pltpu.CompilerParams(
            collective_id=0, has_side_effects=True, vmem_limit_bytes=63 * 2**20
        ),
        name="layer",
    )(*inputs.values())
    found = dict(zip(outs, found))
    sources = [found["grad_" + name] for name in MATRICES] + [found["decoder_input"], found["grad_tokens"]]
    shapes = [jax.ShapeDtypeStruct(source.shape, FULL) for source in sources[:5]]
    shapes += [jax.ShapeDtypeStruct(source.shape, LOW) for source in sources[5:]]
    vec_width = [width] * 8 + [out_width] * 2 + [ff]
    shapes += [jax.ShapeDtypeStruct((1, wide), FULL) for wide in vec_width]
    done = pl.pallas_call(
        finish_kernel,
        out_shape=shapes,
        in_specs=[vmem] * 8,
        out_specs=[vmem] * len(shapes),
        compiler_params=pltpu.CompilerParams(vmem_limit_bytes=40 * 2**20),
        name="finish",
    )(*sources, found["vec_sums"])
    down, up, proj, out, qkv, decoder_input, grad_tokens = done[:7]
    gain1, bias1, b_query, b_value, b_out, gain2, bias2, b_down, b_proj, mask, b_up = [
        vec.reshape(-1) for vec in done[7:]
    ]
    return (
        decoder_input,
        grad_tokens,
        gain1,
        bias1,
        qkv,
        b_query,
        b_value,
        out,
        b_out,
        gain2,
        bias2,
        up,
        b_up,
        down,
        b_down,
        proj,
        b_proj,
        mask,
    )


def solution(mesh):
    placed = (
        P(("img", "pos"), None),
        P(("img", "pos")),
        P(("img", "pos")),
        P(),
        P(),
        P(),
        P(),
        P(),
        P(),
        P(),
        P(),
        P(),
        P(),
        P(),
        P(),
        P(),
        P(),
        P(),
        P(),
        P("img", "pos", None),
    )
    fits = mesh.shape["img"] == 8 and mesh.shape["pos"] == 4
    return jax.shard_map(
        layer_device if fits else general_device,
        mesh=mesh,
        in_specs=placed,
        out_specs=(
            P("img", "pos", None),
            P(("img", "pos"), None),
            P(),
            P(),
            P("img", None),
            P(),
            P(),
            P("img", None),
            P(),
            P(),
            P(),
            P("img", None),
            P(),
            P("img", None),
            P(),
            P("img", None),
            P(),
            P(),
        ),
        check_vma=False,
    )
```

```python
import functools

import jax
import jax.numpy as jnp
from jax import lax
from jax.experimental import pallas as pl
from jax.experimental.pallas import tpu as pltpu
from jax.sharding import PartitionSpec as P

HEADS = 12
HEAD_DIM = 64
ROWS_SEQ = 256
IMG_SEQ = 5
POSITIONS = 196
CAP = 16


EPSILON = 1e-05
NEGATIVE = -1e30
GELU_COEF = 0.7978845608028654


def layer_norm(values, gain_vec, shift_vec):
    centre = jnp.mean(values, axis=-1, keepdims=True)
    centred = values - centre
    return (
        centred
        * lax.rsqrt(jnp.mean(centred * centred, axis=-1, keepdims=True) + EPSILON)
        * gain_vec
        + shift_vec
    )


def gelu_tanh(values):
    return (
        0.5 * values * (1.0 + jnp.tanh(GELU_COEF * (values + 0.044715 * values * values * values)))
    )


def matmul_rows(left, right):
    return jnp.dot(left, right, preferred_element_type=jnp.float32)


def column_sums(values):
    return jnp.sum(values.astype(jnp.float32), axis=0)


def reduce_matrices(members):
    img_count = lax.axis_size("img")
    pos_count = lax.axis_size("pos")
    pieces = [member.reshape(img_count, pos_count, -1) for member in members]
    bucket = jnp.concatenate(pieces, axis=2)
    flat_bucket = bucket.reshape(img_count * pos_count, -1)
    share = lax.psum_scatter(flat_bucket, ("img", "pos"), scatter_dimension=0, tiled=True).reshape(
        1, 1, -1
    )
    summed = lax.all_gather(share.astype(jnp.bfloat16), "pos", axis=1, tiled=True).astype(
        share.dtype
    )
    results = []
    offset = 0
    for member in members:
        extent = member.size // (img_count * pos_count)
        block = summed[0, :, offset : offset + extent]
        results.append(block.reshape(member.shape[0] // img_count, member.shape[1]))
        offset = offset + extent
    return results


def reduce_vectors(members):
    return lax.psum(tuple(members), ("img", "pos"))


def general_device(
    tokens,
    image_slot,
    patch_position,
    ln1_gain,
    ln1_bias,
    w_qkv,
    bias_query,
    bias_value,
    w_out,
    bias_out,
    ln2_gain,
    ln2_bias,
    w_up,
    bias_up,
    w_down,
    bias_down,
    w_proj,
    bias_proj,
    mask_token,
    cotangent,
):
    seq_count = tokens.shape[0] // ROWS_SEQ
    width = w_out.shape[0]
    out_width = w_proj.shape[1]
    pos_count = lax.axis_size("pos")
    quarter_len = POSITIONS // pos_count
    score_scale = HEAD_DIM ** (-0.5)
    head_shape = (seq_count, ROWS_SEQ, HEADS, HEAD_DIM)
    rows_f = tokens.astype(jnp.float32)
    normed_low = layer_norm(rows_f, ln1_gain, ln1_bias).astype(jnp.bfloat16)
    qkv_all = matmul_rows(normed_low, w_qkv)
    queries = (qkv_all[:, :width] + bias_query).astype(jnp.bfloat16).reshape(head_shape)
    keys_h = qkv_all[:, width : 2 * width].astype(jnp.bfloat16).reshape(head_shape)
    values_h = (qkv_all[:, 2 * width :] + bias_value).astype(jnp.bfloat16).reshape(head_shape)
    slot_rows = image_slot.reshape(seq_count, ROWS_SEQ)
    allowed = slot_rows[:, None, :, None] == slot_rows[:, None, None, :]
    raw_scores = (
        jnp.einsum("sqhd,skhd->shqk", queries, keys_h, preferred_element_type=jnp.float32)
        * score_scale
    )
    scores = jnp.where(allowed, raw_scores, NEGATIVE)
    top_score = jnp.max(scores, axis=-1, keepdims=True)
    log_total = top_score + jnp.log(jnp.sum(jnp.exp(scores - top_score), axis=-1, keepdims=True))
    attn_probs = jnp.exp(scores - log_total)
    probs_low = attn_probs.astype(jnp.bfloat16)
    attended = jnp.einsum(
        "shqk,skhd->sqhd", probs_low, values_h, preferred_element_type=jnp.float32
    )
    attended = attended.reshape(-1, width).astype(jnp.bfloat16)
    residual = rows_f + matmul_rows(attended, w_out) + bias_out
    normed_mlp = layer_norm(residual, ln2_gain, ln2_bias).astype(jnp.bfloat16)
    up_proj = matmul_rows(normed_mlp, w_up) + bias_up
    hidden = gelu_tanh(up_proj).astype(jnp.bfloat16)
    block_out = residual + matmul_rows(hidden, w_down) + bias_down
    block_low = block_out.astype(jnp.bfloat16)
    projected = (matmul_rows(block_low, w_proj) + bias_proj).astype(jnp.bfloat16)
    row_index = jnp.arange(ROWS_SEQ, dtype=jnp.int32)
    pos_rows = patch_position.reshape(seq_count, ROWS_SEQ)
    live = slot_rows >= 0
    bucket_id = jnp.where(live, slot_rows * pos_count + pos_rows // quarter_len, -1)
    earlier = (bucket_id[:, :, None] == bucket_id[:, None, :]) & (
        row_index[None, :, None] > row_index[None, None, :]
    )
    rank_in = jnp.sum(earlier.astype(jnp.int32), axis=2)
    target = jnp.where(live, bucket_id * CAP + rank_in, -1)
    slot_index = jnp.arange(IMG_SEQ * pos_count * CAP, dtype=jnp.int32)
    selected = slot_index[None, :, None] == target[:, None, :]
    select_low = selected.astype(jnp.bfloat16)
    outgoing = jnp.einsum(
        "sjr,src->sjc",
        select_low,
        projected.reshape(seq_count, ROWS_SEQ, out_width),
        preferred_element_type=jnp.float32,
    ).astype(jnp.bfloat16)
    outgoing = outgoing.reshape(seq_count * IMG_SEQ, pos_count, CAP, out_width)
    slot_place = (
        jnp.sum(jnp.where(selected, (pos_rows % quarter_len + 1)[:, None, :], 0), axis=2) - 1
    )
    slot_place = slot_place.reshape(seq_count * IMG_SEQ, pos_count, CAP)
    arrived, arrived_place = (
        lax.all_to_all(outgoing, "pos", split_axis=1, concat_axis=0, tiled=True),
        lax.all_to_all(slot_place, "pos", split_axis=1, concat_axis=0, tiled=True),
    )
    arrived = arrived[:, 0]
    arrived_place = arrived_place[:, 0]
    placing = jnp.arange(quarter_len, dtype=jnp.int32)[None, :, None] == arrived_place[:, None, :]
    placing_low = placing.astype(jnp.bfloat16)
    visible = jnp.any(placing, axis=2)
    filled = jnp.einsum("gqj,gjc->gqc", placing_low, arrived, preferred_element_type=jnp.float32)
    decoder_input = jnp.where(
        visible[:, :, None], filled, mask_token.astype(jnp.float32)[None, None, :]
    )
    decoder_input = decoder_input.astype(jnp.bfloat16)
    grad_mask = jnp.sum(
        jnp.where(visible[:, :, None], 0.0, cotangent.astype(jnp.float32)), axis=(0, 1)
    )
    back_slots = jnp.einsum(
        "gqj,gqc->gjc", placing_low, cotangent, preferred_element_type=jnp.float32
    ).astype(jnp.bfloat16)
    returned = lax.all_to_all(back_slots[:, None], "pos", split_axis=0, concat_axis=1, tiled=True)
    delta_proj = (
        jnp.einsum(
            "sjr,sjc->src",
            select_low,
            returned.reshape(seq_count, -1, out_width),
            preferred_element_type=jnp.float32,
        )
        .reshape(-1, out_width)
        .astype(jnp.bfloat16)
    )
    grad_proj = jnp.einsum("rd,rc->dc", block_low, delta_proj, preferred_element_type=jnp.float32)
    grad_bproj = column_sums(delta_proj)
    delta_block = jnp.einsum("rc,dc->rd", delta_proj, w_proj, preferred_element_type=jnp.float32)
    delta_down = delta_block.astype(jnp.bfloat16)
    grad_down = jnp.einsum("rf,rd->fd", hidden, delta_down, preferred_element_type=jnp.float32)
    grad_bdown = column_sums(delta_down)
    delta_hidden = jnp.einsum("rd,fd->rf", delta_down, w_down, preferred_element_type=jnp.float32)
    gelu_back = jax.vjp(gelu_tanh, up_proj)[1]
    delta_up = gelu_back(delta_hidden)[0].astype(jnp.bfloat16)
    grad_up = jnp.einsum("rd,rf->df", normed_mlp, delta_up, preferred_element_type=jnp.float32)
    grad_bup = column_sums(delta_up)
    delta_normed = jnp.einsum("rf,df->rd", delta_up, w_up, preferred_element_type=jnp.float32)
    norm_back = jax.vjp(layer_norm, residual, ln2_gain, ln2_bias)[1]
    delta_resid_norm, grad_gain_two, grad_shift_two = norm_back(delta_normed)
    delta_residual = delta_block + delta_resid_norm
    mlp_mats = reduce_matrices((grad_proj, grad_down, grad_up))
    mlp_vecs = reduce_vectors(
        (grad_bproj, grad_bdown, grad_bup, grad_gain_two, grad_shift_two, grad_mask)
    )
    delta_branch = delta_residual.astype(jnp.bfloat16)
    grad_out = jnp.einsum("re,rd->ed", attended, delta_branch, preferred_element_type=jnp.float32)
    grad_bout = column_sums(delta_branch)
    delta_attended = jnp.einsum(
        "rd,ed->re", delta_branch, w_out, preferred_element_type=jnp.float32
    )
    delta_attended = delta_attended.astype(jnp.bfloat16).reshape(head_shape)
    delta_values = jnp.einsum(
        "shqk,sqhd->skhd", probs_low, delta_attended, preferred_element_type=jnp.float32
    ).astype(jnp.bfloat16)
    delta_probs = jnp.einsum(
        "sqhd,skhd->shqk", delta_attended, values_h, preferred_element_type=jnp.float32
    )
    delta_scores = attn_probs * (
        delta_probs - jnp.sum(delta_probs * attn_probs, axis=-1, keepdims=True)
    )
    delta_scores = delta_scores.astype(jnp.bfloat16)
    delta_queries = (
        (
            jnp.einsum("shqk,skhd->sqhd", delta_scores, keys_h, preferred_element_type=jnp.float32)
            * score_scale
        )
        .astype(jnp.bfloat16)
        .reshape(-1, width)
    )
    delta_keys = (
        (
            jnp.einsum("shqk,sqhd->skhd", delta_scores, queries, preferred_element_type=jnp.float32)
            * score_scale
        )
        .astype(jnp.bfloat16)
        .reshape(-1, width)
    )
    delta_values = delta_values.reshape(-1, width)
    delta_qkv = jnp.concatenate([delta_queries, delta_keys, delta_values], axis=1)
    grad_qkv = jnp.einsum("rd,re->de", normed_low, delta_qkv, preferred_element_type=jnp.float32)
    grad_bquery = column_sums(delta_queries)
    grad_bvalue = column_sums(delta_values)
    delta_first = jnp.einsum("re,de->rd", delta_qkv, w_qkv, preferred_element_type=jnp.float32)
    first_back = jax.vjp(layer_norm, rows_f, ln1_gain, ln1_bias)[1]
    delta_rows, grad_gain_one, grad_shift_one = first_back(delta_first)
    grad_tokens = (delta_residual + delta_rows).astype(jnp.bfloat16)
    attn_mats = reduce_matrices((grad_qkv, grad_out))
    attn_vecs = reduce_vectors((grad_bquery, grad_bvalue, grad_bout, grad_gain_one, grad_shift_one))
    return (
        decoder_input,
        grad_tokens,
        attn_vecs[3],
        attn_vecs[4],
        attn_mats[0],
        attn_vecs[0],
        attn_vecs[1],
        attn_mats[1],
        attn_vecs[2],
        mlp_vecs[3],
        mlp_vecs[4],
        mlp_mats[2],
        mlp_vecs[2],
        mlp_mats[1],
        mlp_vecs[1],
        mlp_mats[0],
        mlp_vecs[0],
        mlp_vecs[5],
    )


MESH_ID = pl.DeviceIdType.MESH
LOW = jnp.bfloat16
FULL = jnp.float32

AXES = ("zh", "zl", "x", "y")
MATRICES = ("down", "up", "proj", "out", "qkv")
JOBS = {
    "down0": ("down", None, 0, 256, ("zl", "y", "zh", "x")),
    "down1": ("down", None, 256, 256, ("zl", "zh", "x", "y")),
    "down2": ("down", None, 512, 256, ("zl", "y", "x", "zh")),
    "up0": ("up", 0, 0, 384, ("x", "y", "zl", "zh")),
    "up1": ("up", 1, 0, 384, ("x", "y", "zl", "zh")),
    "up2": ("up", 2, 0, 384, ("x", "y", "zl", "zh")),
    "up3": ("up", 3, 0, 384, ("x", "y", "zl", "zh")),
    "proj0": ("proj", None, 0, 256, ("y", "zl", "x", "zh")),
    "out0": ("out", None, 0, 384, ("x", "y", "zl", "zh")),
    "qkv0": ("qkv", None, 0, 384, ("x", "y", "zl", "zh")),
    "qkv1": ("qkv", None, 384, 384, ("y", "zl", "zh", "x")),
    "qkv2": ("qkv", None, 768, 384, ("x", "y", "zl", "zh")),
}
PLAN = (
    ("do", "feed0"),
    ("do", "feed1"),
    ("do", "multiply_feed0"),
    ("do", "feed2"),
    ("do", "multiply_feed1"),
    ("do", "feed3"),
    ("do", "multiply_feed2"),
    ("do", "project"),
    ("down0", 0, "a"),
    ("do", "multiply_feed3"),
    ("up0", 0, ""),
    ("do", "second_back"),
    ("down1", 0, "a"),
    ("do", "swapped_proj"),
    ("do", "multiply_proj0"),
    ("do", "attended_back"),
    ("do", "attend_back0"),
    ("do", "attend_back1"),
    ("do", "attend_back2"),
    ("do", "attend_back3"),
    ("up0", 1, ""),
    ("down2", 0, "a"),
    ("up1", 0, ""),
    ("do", "attend_back4"),
    ("do", "attend_back5"),
    ("do", "swapped_out"),
    ("do", "multiply_out0"),
    ("do", "delta_first"),
    ("proj0", 0, ""),
    ("down0", 0, "b"),
    ("do", "swapped_qkv"),
    ("do", "multiply_qkv0"),
    ("do", "multiply_qkv1"),
    ("do", "multiply_qkv2"),
    ("up2", 0, ""),
    ("up1", 1, ""),
    ("do", "first_back"),
    ("down1", 0, "b"),
    ("do", "decode"),
    ("vec", 0),
    ("down0", 1, ""),
    ("down2", 0, "b"),
    ("up3", 0, ""),
    ("qkv1", 0, ""),
    ("up1", 2, ""),
    ("out0", 0, ""),
    ("proj0", 1, ""),
    ("up2", 1, ""),
    ("down1", 1, ""),
    ("up0", 2, ""),
    ("down2", 1, ""),
    ("qkv0", 0, ""),
    ("down0", 2, ""),
    ("qkv1", 1, ""),
    ("up3", 1, ""),
    ("up3", 2, ""),
    ("up3", 3, ""),
    ("out0", 1, ""),
    ("qkv2", 0, ""),
    ("vec", 1),
    ("proj0", 2, ""),
    ("up2", 2, ""),
    ("up2", 3, ""),
    ("qkv0", 1, ""),
    ("up3", 4, ""),
    ("qkv1", 2, ""),
    ("down1", 2, ""),
    ("out0", 2, ""),
    ("up1", 3, ""),
    ("up3", 5, ""),
    ("down2", 2, ""),
    ("proj0", 3, ""),
    ("qkv2", 1, ""),
    ("down0", 3, ""),
    ("qkv0", 2, ""),
    ("vec", 2),
    ("up0", 3, ""),
    ("qkv1", 3, ""),
    ("up2", 4, ""),
    ("down1", 3, ""),
    ("out0", 3, ""),
    ("up1", 4, ""),
    ("proj0", 4, ""),
    ("qkv2", 2, ""),
    ("up2", 5, ""),
    ("down0", 4, ""),
    ("down2", 3, ""),
    ("up0", 4, ""),
    ("up1", 5, ""),
    ("vec", 3),
    ("proj0", 5, ""),
    ("qkv1", 4, ""),
    ("qkv0", 3, ""),
    ("down0", 5, ""),
    ("down1", 4, ""),
    ("up0", 5, ""),
    ("out0", 4, ""),
    ("qkv2", 3, ""),
    ("qkv1", 5, ""),
    ("down2", 4, ""),
    ("qkv0", 4, ""),
    ("down1", 5, ""),
    ("out0", 5, ""),
    ("vec", 4),
    ("qkv2", 4, ""),
    ("down2", 5, ""),
    ("qkv0", 5, ""),
    ("qkv2", 5, ""),
)
VEC_STEPS = ("core", "x", "y", "zl", "zh")
PEERS = ("y", "core", "diagonal")
PLACES = 64
LN1_GAIN, LN1_BIAS, BIAS_Q, BIAS_V, BIAS_OUT, LN2_GAIN, LN2_BIAS, BIAS_DOWN, BIAS_UP, BIAS_PROJ, MASK = (
    0, 1, 2, 3, 4, 5, 6, 7, 8, 12, 13,
)


def device_coords():
    img = lax.axis_index("img")
    pos = lax.axis_index("pos")
    return {"zh": img // 4, "zl": (img // 2) % 2, "x": img % 2, "y": pos // 2, "core": pos % 2}


def device_of(where):
    return (where["zh"] * 4 + where["zl"] * 2 + where["x"], where["y"] * 2 + where["core"])


def block_rows(name):
    return 96 if name == "down" else 48


def dot(left, right):
    return jnp.dot(left, right, preferred_element_type=FULL)


def dot_nt(left, right):
    return lax.dot_general(left, right, (((1,), (1,)), ((), ())), preferred_element_type=FULL)


def dot_tn(left, right):
    return lax.dot_general(left, right, (((0,), (0,)), ((), ())), preferred_element_type=FULL)


def normalised(values):
    centred = values - jnp.mean(values, axis=-1, keepdims=True)
    rstd = lax.rsqrt(jnp.mean(centred * centred, axis=-1, keepdims=True) + EPSILON)
    return centred * rstd, rstd


def norm_rows_back(delta, values, gain):
    xhat, rstd = normalised(values)
    scaled = delta * gain
    rows = rstd * (
        scaled
        - jnp.mean(scaled, axis=-1, keepdims=True)
        - xhat * jnp.mean(scaled * xhat, axis=-1, keepdims=True)
    )
    return rows, delta * xhat


def layer_kernel(names, *refs):
    ref = dict(zip(names, refs))

    def row_of(name, columns=slice(None)):
        return ref[name][...].reshape(1, -1)[:, columns]

    me = device_coords()
    core = me["core"]
    my_pos = me["y"] * 2 + core
    width = ref["tokens"].shape[1]
    ff = ref["w_up"].shape[1]
    quarter_len = POSITIONS // 4

    def peer(axis):
        if axis == "diagonal":
            return device_of({**me, "y": 1 - me["y"], "core": 1 - core})
        return device_of({**me, axis: 1 - me[axis]})

    started = []

    def remote(source, target, kind, spot, axis):
        return pltpu.make_async_remote_copy(
            src_ref=source,
            dst_ref=target,
            send_sem=ref[kind + "_send"].at[spot],
            recv_sem=ref[kind + "_recv"].at[spot],
            device_id=peer(axis),
            device_id_type=MESH_ID,
        )

    def begin(copy):
        copy.start()
        started.append(copy)

    loads = {}
    for number, name in enumerate(("w_qkv", "cotangent", "w_out", "w_proj", "w_up", "w_down")):
        loads[name] = pltpu.make_async_copy(ref[name], ref[name + "_held"], ref["load"].at[number])
        loads[name].start()

    barrier = pltpu.get_barrier_semaphore()
    for axis in AXES + ("core", "diagonal"):
        pl.semaphore_signal(barrier, inc=1, device_id=peer(axis), device_id_type=MESH_ID)

    ref["places"][my_pos, 0:1, :] = ref["slot"][...]
    ref["places"][my_pos, 1:2, :] = ref["position"][...]

    def first_norm(step, carry):
        rows = pl.ds(pl.multiple_of(step * 64, 64), 64)
        xhat, _ = normalised(ref["tokens"][rows, :].astype(FULL))
        ref["normed"][rows, :] = (xhat * row_of("ln1_gain") + row_of("ln1_bias")).astype(LOW)
        return carry

    lax.fori_loop(0, 4, first_norm, 0, unroll=4)

    pl.semaphore_wait(barrier, 6)
    for number, axis in enumerate(PEERS):
        begin(remote(ref["places"].at[my_pos], ref["places"].at[my_pos], "place", number, axis))

    loads["w_qkv"].wait()
    third = width // 256
    for number in range(3 * third):
        columns = slice(number * 256, (number + 1) * 256)
        part = dot(ref["normed"][...], ref["w_qkv_held"][:, columns])
        if number < third:
            part = part + row_of("bias_query", columns)
            part = part.astype(LOW) * LOW(HEAD_DIM ** (-0.5))
        elif number >= 2 * third:
            part = part + row_of("bias_value", slice((number - 2 * third) * 256, (number - 2 * third + 1) * 256))
        ref["qkv"][:, columns] = part.astype(LOW)
    ref["normed_one"][...] = ref["normed"][...]

    row_ids = lax.broadcasted_iota(jnp.int32, (ROWS_SEQ, ROWS_SEQ), 0)
    lane_ids = lax.broadcasted_iota(jnp.int32, (ROWS_SEQ, ROWS_SEQ), 1)
    earlier = (row_ids < lane_ids).astype(FULL).astype(LOW)

    def one_hot(count, row):
        ids = lax.broadcasted_iota(jnp.int32, (count, ROWS_SEQ), 0)
        return jnp.where(ids == row, 1.0, 0.0)

    def picked(slot, position, quarter):
        offset = position - quarter * quarter_len
        inside = (slot >= 0) & (offset >= 0) & (offset < quarter_len)
        kinds = one_hot(8, jnp.where(inside, slot, -1))
        ranks = jnp.sum(kinds * dot(kinds.astype(LOW), earlier), axis=0, keepdims=True).astype(jnp.int32)
        chosen = one_hot(IMG_SEQ * CAP, jnp.where(inside, slot * CAP + ranks, -1))
        return chosen.astype(LOW), jnp.where(inside, slot * PLACES + offset, -1)

    for quarter in range(4):
        chosen, _ = picked(ref["slot"][...], ref["position"][...], quarter)
        ref["chosen"][quarter] = chosen

    slots = one_hot(8, ref["slot"][...] + 1).astype(LOW)
    ref["allowed"][...] = jnp.where(dot_tn(slots, slots) > 0.5, 0.0, NEGATIVE)

    ref["cot_wide"][...] = jnp.zeros_like(ref["cot_wide"])
    loads["cotangent"].wait()
    for image in range(4 * IMG_SEQ):
        ref["cot_wide"][image, 0:quarter_len, :] = ref["cotangent_held"][image]
    for number, axis in enumerate(PEERS + ("self",)):
        if axis == "self":
            source = my_pos
        else:
            source = peer(axis)[1]
            remote(ref["places"].at[source], ref["places"].at[source], "place", number, axis).wait_recv()
        slot = ref["places"][source, 0:1, :]
        position = ref["places"][source, 1:2, :]
        chosen, place = picked(slot, position, my_pos)
        filled = one_hot(IMG_SEQ * PLACES, place).astype(LOW)
        placing = dot_nt(filled, chosen)
        placing_low = placing.astype(LOW)
        ref["placing"][number] = placing_low
        cot = ref["cot_wide"][pl.ds(source * IMG_SEQ, IMG_SEQ)].reshape(IMG_SEQ * PLACES, -1)
        back = dot_tn(placing_low, cot).astype(LOW)
        if axis == "self":
            ref["back_in"][my_pos] = back
        else:
            ref["back_out"][number] = back
            begin(remote(ref["back_out"].at[number], ref["back_in"].at[my_pos], "back", number, axis))
    ref["vec_own"][...] = jnp.zeros_like(ref["vec_own"])

    lane = lax.broadcasted_iota(jnp.int32, (1, 2 * HEAD_DIM), 1)
    sides_full = [(lane < HEAD_DIM).astype(FULL), (lane >= HEAD_DIM).astype(FULL)]
    sides = [side.astype(LOW) for side in sides_full]

    def head_columns(pair, first):
        return pl.ds(first + pair * 2 * HEAD_DIM, 2 * HEAD_DIM)

    def attend(pair, carry):
        queries = ref["qkv"][:, head_columns(pair, 0)]
        keys = ref["qkv"][:, head_columns(pair, width)]
        values = ref["qkv"][:, head_columns(pair, 2 * width)]
        total = None
        for side in range(2):
            scores = dot_nt(queries * sides[side], keys) + ref["allowed"][...]
            powers = jnp.exp(scores - jnp.max(scores, axis=-1, keepdims=True))
            probs = powers / jnp.sum(powers, axis=-1, keepdims=True)
            ref["probs"][pair * 2 + side] = probs
            part = dot(probs.astype(LOW), values) * sides_full[side]
            total = part if total is None else total + part
        ref["attended"][:, head_columns(pair, 0)] = total.astype(LOW)
        return carry

    for pair in range(HEADS // 2):
        attend(pair, 0)

    loads["w_out"].wait()
    for number in range(third):
        columns = slice(number * 256, (number + 1) * 256)
        ref["residual"][:, columns] = (
            ref["tokens"][:, columns].astype(FULL)
            + dot(ref["attended"][...], ref["w_out_held"][:, columns])
            + row_of("bias_out", columns)
        )

    def second_norm(step, carry):
        rows = pl.ds(pl.multiple_of(step * 64, 64), 64)
        xhat, _ = normalised(ref["residual"][rows, :])
        ref["normed"][rows, :] = (xhat * row_of("ln2_gain") + row_of("ln2_bias")).astype(LOW)
        return carry

    lax.fori_loop(0, 4, second_norm, 0, unroll=4)
    ref["left_up"][...] = ref["normed"][...].T

    loads["w_proj"].wait()
    for number, axis in enumerate(PEERS):
        remote(ref["back_out"].at[number], ref["back_in"].at[my_pos], "back", number, axis).wait_recv()
    chosen_all = ref["chosen"][...].reshape(4 * IMG_SEQ * CAP, ROWS_SEQ)
    returned = ref["back_in"][...].reshape(4 * IMG_SEQ * CAP, -1)
    delta_proj = dot_tn(chosen_all, returned)
    ref["vec_own"][BIAS_PROJ : BIAS_PROJ + 1, : delta_proj.shape[1]] = jnp.sum(delta_proj, axis=0, keepdims=True)
    ref["right_proj"][...] = delta_proj.astype(LOW)
    for number in range(third):
        columns = slice(number * 256, (number + 1) * 256)
        part = dot_nt(ref["right_proj"][...], ref["w_proj_held"][columns, :])
        ref["delta_block"][:, columns] = part
        part = part.astype(LOW)
        ref["right_down"][:, columns] = part
        ref["vec_own"][BIAS_DOWN : BIAS_DOWN + 1, columns] = jnp.sum(part.astype(FULL), axis=0, keepdims=True)

    loads["w_up"].wait()
    loads["w_down"].wait()

    def chunk_of(slot):
        high = 1 - me["zh"] if slot < 2 else me["zh"]
        low = 1 - me["zl"] if slot % 2 == 0 else me["zl"]
        return high, low, high * 2 + low

    def chunk_columns(slot, start=0, wide=width):
        return pl.ds(pl.multiple_of(chunk_of(slot)[2] * width + start, 128), wide)

    def feed(slot):
        columns = chunk_columns(slot)
        up = dot(ref["normed"][...], ref["w_up_held"][:, columns]) + ref["bias_up"][:, columns]
        square = up * up
        bent = jnp.tanh(GELU_COEF * (up + 0.044715 * up * square))
        half = 0.5 * (1.0 + bent)
        slope = half + 0.5 * up * (1.0 - bent * bent) * (GELU_COEF * (1.0 + 0.134145 * square))
        hidden = (up * half).astype(LOW)
        ref["left_down"][columns, :] = hidden.T
        back = dot_nt(ref["right_down"][...], ref["w_down_held"][columns, :])
        delta_up = (back * slope).astype(LOW)
        ref["right_up"][:, columns] = delta_up
        for copy in swap_copies("feed%d" % slot):
            begin(copy)
        ref["bias_up_sum"][:, columns] = jnp.sum(delta_up.astype(FULL), axis=0, keepdims=True)
        out = dot(hidden, ref["w_down_held"][columns, :])
        delta = dot_nt(delta_up, ref["w_up_held"][:, columns])
        if slot == 0:
            ref["mlp_out"][...] = out
            ref["delta_normed"][...] = delta
        else:
            ref["mlp_out"][...] += out
            ref["delta_normed"][...] += delta

    swaps = ("early", "feed0", "feed1", "feed2", "feed3", "proj", "out", "qkv")

    def swap_copies(which):
        other = 1 - core
        if which == "early":
            pairs = ((ref["left_up"], ref["left_in_up"]), (ref["right_down"], ref["right_in_down"]))
        elif which.startswith("feed"):
            slot = int(which[4:])
            _, _, chunk = chunk_of(slot)
            left = ref["left_down"].reshape(8, 2, 192, ROWS_SEQ)
            right = ref["right_up"].at[:, chunk_columns(slot, other * (width // 2), width // 2)]
            pairs = (
                (left.at[pl.ds(chunk * 2, 2), other], ref["left_in_down"].at[pl.ds(chunk * 2, 2)]),
                (right, ref["right_in_up"].at[slot]),
            )
        else:
            wide = ref["right_" + which].shape[1] // 2
            right = ref["right_" + which].at[:, pl.ds(pl.multiple_of(other * wide, 128), wide)]
            pairs = ((ref["left_" + which], ref["left_in_" + which]), (right, ref["right_in_" + which]))
        spot = swaps.index(which)
        return [remote(source, target, "core", (spot, part), "core") for part, (source, target) in enumerate(pairs)]

    def swap(which):
        for copy in swap_copies(which):
            begin(copy)

    def swapped(which):
        for copy in swap_copies(which):
            copy.wait_recv()

    job_names = tuple(JOBS)

    def job_final(job):
        matrix, slot, first, wide, _ = JOBS[job]
        final = ref["final_" + matrix]
        if slot is not None:
            final = final.at[chunk_of(slot)[2]]
        return final, pl.ds(first, wide)

    def job_target(job, stage):
        _, slot, _, _, dims = JOBS[job]
        if slot is None or stage > 3 or dims[stage] not in ("zl", "zh"):
            return job
        return "up%d%s" % (slot ^ (1 if dims[stage] == "zl" else 2), job[3:])

    def job_index(job, stage, part, mine):
        dims = JOBS[job][4]
        pick, land = [], []
        for axis in AXES:
            if axis in dims[:stage]:
                pick.append(me[axis])
            elif axis == dims[stage]:
                pick.append(me[axis] if mine else 1 - me[axis])
            elif axis == "zh" and part:
                pick.append(1 - me[axis] if part == "a" else me[axis])
                land.append(pick[-1])
            else:
                pick.append(slice(None))
                land.append(slice(None))
        return tuple(pick), tuple(land)

    def job_copy(job, stage, part):
        dims = JOBS[job][4]
        target = job_target(job, stage)
        spot = stage if part != "b" else 6
        send_sem = ref["job_send"].at[job_names.index(job), spot]
        recv_sem = ref["job_recv"].at[job_names.index(target), spot]
        if stage < 4:
            pick, land = job_index(job, stage, part, False)
            source = ref["partial_" + job].at[pick]
            place = ref["landed_%s_%d" % (target, stage)]
            place = place.at[land] if land else place
            axis = dims[stage]
        else:
            final, columns = job_final(job)
            if stage == 4:
                source = place = final.at[core, me["y"], :, columns]
            else:
                source = place = final.at[core, :, :, columns]
            axis = "y" if stage == 4 else "core"
        return pltpu.make_async_remote_copy(
            src_ref=source,
            dst_ref=place,
            send_sem=send_sem,
            recv_sem=recv_sem,
            device_id=peer(axis),
            device_id_type=MESH_ID,
        )

    def first_parts(job):
        return ("a", "b") if JOBS[job][0] == "down" else ("",)

    def needs(job, stage):
        if stage == 0:
            return ()
        if stage == 1:
            return tuple((0, part) for part in first_parts(job) if part != "b" or JOBS[job][4][1] != "zh")
        if stage == 2:
            return ((1, ""),) + tuple((0, part) for part in first_parts(job))
        return ((stage - 1, ""),)

    arrived, sent = set(), set()

    def send(job, stage, part=""):
        sent.add((job, stage, part))
        begin(job_copy(job, stage, part))

    def arrive(job, stage, part):
        matrix, slot, _, _, dims = JOBS[job]
        source = job_copy(job_target(job, stage), stage, part)
        source.wait_recv()
        if stage < 4:
            partial, landed = ref["partial_" + job], ref["landed_%s_%d" % (job, stage)]
            pick, land = job_index(job, stage, part, True)
            free = [spot for spot, index in enumerate(pick) if isinstance(index, slice)]
            for code in range(2 ** len(free)):
                here, there = list(pick), list(land)
                for order, spot in enumerate(free):
                    bit = (code >> (len(free) - 1 - order)) % 2
                    here[spot] = bit
                    there[[place for place, axis in enumerate(AXES) if axis not in dims[: stage + 1]].index(spot)] = bit
                sums = partial[tuple(here)] + (landed[tuple(there)] if there else landed[...])
                if stage < 3:
                    partial[tuple(here)] = sums
                else:
                    final, columns = job_final(job)
                    final[core, me["y"], :, columns] = sums
        arrived.add((job, stage, part))
        for later in range(1, 6):
            ready = all((job,) + need in arrived for need in needs(job, later))
            if (job, later, "") not in sent and ready:
                send(job, later)
        if stage == 5:
            final, columns = job_final(job)
            _, _, first, wide, _ = JOBS[job]
            out = ref["grad_" + matrix]
            for side in range(2):
                if matrix == "down":
                    place = out.at[side, :, :, columns]
                else:
                    start = side * ref["final_" + matrix].shape[-1] + first
                    if slot is not None:
                        place = out.at[:, :, chunk_columns(slot, start, wide)]
                    else:
                        place = out.at[:, :, pl.ds(start, wide)]
                store = pltpu.make_async_copy(
                    final.at[side, :, :, columns], place, ref["store"].at[job_names.index(job), side]
                )
                store.start()
                stores.append(store)

    stores = []

    def keep(name, number):
        store = pltpu.make_async_copy(ref[name + "_held"], ref[name], ref["keep"].at[number])
        store.start()
        stores.append(store)

    def multiply_feed(slot):
        if slot == 0:
            swapped("early")
        swapped("feed%d" % slot)
        high, low, chunk = chunk_of(slot)
        for side in range(2):
            block = chunk * 2 + side
            rows = pl.ds(pl.multiple_of(block * 384 + core * 192, 192), 192)
            total = dot(ref["left_down"][rows, :], ref["right_down"][...]) + dot(
                ref["left_in_down"][block], ref["right_in_down"][...]
            )
            total = total.astype(LOW)
            for job, (matrix, _, first, wide, _) in JOBS.items():
                if matrix == "down":
                    for half in range(2):
                        ref["partial_" + job][high, low, side, half] = total[
                            half * 96 : (half + 1) * 96, first : first + wide
                        ]
        if slot % 2 == 0:
            for job in JOBS:
                if JOBS[job][0] == "down":
                    send(job, 0, "ab"[slot // 2])
        for block in range(2):
            rows = slice(block * 384, (block + 1) * 384)
            total = dot(
                ref["left_up"][rows, :], ref["right_up"][:, chunk_columns(slot, core * (width // 2), width // 2)]
            ) + dot(ref["left_in_up"][rows, :], ref["right_in_up"][slot])
            total = total.astype(LOW)
            for job, (matrix, own, first, wide, _) in JOBS.items():
                if matrix == "up" and own == slot:
                    for part in range(8):
                        ref["partial_" + job][block, part // 4, (part // 2) % 2, part % 2] = total[
                            part * 48 : (part + 1) * 48, first : first + wide
                        ]
        for job, (matrix, own, _, _, _) in JOBS.items():
            if matrix == "up" and own == slot:
                send(job, 0)

    def multiply(job):
        matrix, _, first, wide, _ = JOBS[job]
        wide_half = ref["right_" + matrix].shape[1] // 2
        columns = pl.ds(pl.multiple_of(core * wide_half + first, 128), wide)
        for block in range(2):
            rows = slice(block * 384, (block + 1) * 384)
            total = dot(ref["left_" + matrix][rows, :], ref["right_" + matrix][:, columns]) + dot(
                ref["left_in_" + matrix][rows, :], ref["right_in_" + matrix][:, first : first + wide]
            )
            total = total.astype(LOW)
            for part in range(8):
                ref["partial_" + job][block, part // 4, (part // 2) % 2, part % 2] = total[part * 48 : (part + 1) * 48]
        send(job, 0)

    def vec_copy(stage):
        return remote(ref["vec_held"].at[stage], ref["vec_in"].at[stage], "vec", stage, VEC_STEPS[stage])

    def arrive_vec(stage):
        vec_copy(stage).wait_recv()
        sums = ref["vec_held"][stage] + ref["vec_in"][stage]
        if stage < 4:
            ref["vec_held"][stage + 1] = sums
            begin(vec_copy(stage + 1))
        else:
            ref["vec_sums"][...] = sums

    swap("early")

    def project():
        for number in range(third):
            columns = slice(number * 256, (number + 1) * 256)
            ref["block_low"][:, columns] = (
                ref["residual"][:, columns] + ref["mlp_out"][:, columns] + row_of("bias_down", columns)
            ).astype(LOW)
        ref["left_proj"][...] = ref["block_low"][...].T
        swap("proj")
        projected = (dot(ref["block_low"][...], ref["w_proj_held"][...]) + ref["bias_proj"][...]).astype(LOW)
        outgoing = dot(chosen_all, projected).astype(LOW)
        ref["grid_out"][...] = outgoing.reshape(4, IMG_SEQ * CAP, -1)
        for number, axis in enumerate(PEERS):
            begin(remote(ref["grid_out"].at[peer(axis)[1]], ref["grid_in"].at[number], "grid", number, axis))

    def second_back():
        sums = [jnp.zeros((1, width), FULL)] * 3
        for step in range(4):
            rows = slice(step * 64, (step + 1) * 64)
            delta = ref["delta_normed"][rows, :]
            row_term, gains = norm_rows_back(delta, ref["residual"][rows, :], row_of("ln2_gain"))
            total = ref["delta_block"][rows, :] + row_term
            low = total.astype(LOW)
            ref["delta_block"][rows, :] = total
            ref["right_out"][rows, :] = low
            news = (gains, delta, low.astype(FULL))
            sums = [old + jnp.sum(new, axis=0, keepdims=True) for old, new in zip(sums, news)]
        for spot, total in zip((LN2_GAIN, LN2_BIAS, BIAS_OUT), sums):
            ref["vec_own"][spot : spot + 1, :] = total
        ref["left_out"][...] = ref["attended"][...].T
        swap("out")

    def attended_back():
        for number in range(third):
            columns = slice(number * 256, (number + 1) * 256)
            ref["delta_attended"][:, columns] = dot_nt(ref["right_out"][...], ref["w_out_held"][columns, :]).astype(LOW)
        ref["left_qkv"][...] = ref["normed_one"][...].T

    def attend_back(pair):
        queries = ref["qkv"][:, head_columns(pair, 0)]
        keys = ref["qkv"][:, head_columns(pair, width)]
        values = ref["qkv"][:, head_columns(pair, 2 * width)]
        delta = ref["delta_attended"][:, head_columns(pair, 0)]
        totals = [None, None, None]
        for side in range(2):
            probs = ref["probs"][pair * 2 + side]
            delta_probs = dot_nt(delta * sides[side], values)
            delta_scores = probs * (delta_probs - jnp.sum(delta_probs * probs, axis=-1, keepdims=True))
            delta_scores = delta_scores.astype(LOW)
            parts = (
                dot(delta_scores, keys) * (HEAD_DIM ** (-0.5)),
                dot_tn(delta_scores, queries),
                dot_tn(probs.astype(LOW), delta),
            )
            for spot, part in enumerate(parts):
                part = part * sides_full[side]
                totals[spot] = part if totals[spot] is None else totals[spot] + part
        for spot, total in enumerate(totals):
            ref["right_qkv"][:, head_columns(pair, spot * width)] = total.astype(LOW)
        if pair == HEADS // 2 - 1:
            swap("qkv")

    def delta_first():
        for number in range(third):
            columns = slice(number * 256, (number + 1) * 256)
            ref["delta_normed"][:, columns] = dot_nt(ref["right_qkv"][...], ref["w_qkv_held"][columns, :])
        for spot, first in ((BIAS_Q, 0), (BIAS_V, 2 * width)):
            ref["vec_own"][spot : spot + 1, :] = jnp.sum(
                ref["right_qkv"][:, first : first + width].astype(FULL), axis=0, keepdims=True
            )

    def first_back():
        sums = [jnp.zeros((1, width), FULL)] * 2
        for step in range(4):
            rows = slice(step * 64, (step + 1) * 64)
            delta = ref["delta_normed"][rows, :]
            row_term, gains = norm_rows_back(delta, ref["tokens"][rows, :].astype(FULL), row_of("ln1_gain"))
            ref["grad_tokens_held"][rows, :] = (ref["delta_block"][rows, :] + row_term).astype(LOW)
            sums = [old + jnp.sum(new, axis=0, keepdims=True) for old, new in zip(sums, (gains, delta))]
        for spot, total in zip((LN1_GAIN, LN1_BIAS), sums):
            ref["vec_own"][spot : spot + 1, :] = total
        for number in range(ff // width):
            ref["vec_own"][BIAS_UP + number : BIAS_UP + number + 1, :] = ref["bias_up_sum"][
                :, number * width : (number + 1) * width
            ]
        mask_sum = jnp.zeros((8, ref["cot_wide"].shape[2]), FULL)
        for number, axis in enumerate(PEERS + ("self",)):
            source = my_pos if axis == "self" else peer(axis)[1]
            cot = ref["cot_wide"][pl.ds(source * IMG_SEQ, IMG_SEQ)].reshape(IMG_SEQ * PLACES, -1)
            seen = dot_nt(jnp.ones((8, IMG_SEQ * CAP), LOW), ref["placing"][number])
            mask_sum = mask_sum + dot((1.0 - seen).astype(LOW), cot)
        ref["vec_own"][MASK : MASK + 1, : mask_sum.shape[1]] = mask_sum[0:1]
        ref["vec_held"][0] = ref["vec_own"][...]
        begin(vec_copy(0))
        keep("grad_tokens", 0)

    def decode():
        for number, axis in enumerate(PEERS + ("self",)):
            if axis == "self":
                source = my_pos
                arrived_rows = ref["grid_out"][my_pos]
            else:
                source = peer(axis)[1]
                remote(ref["grid_out"].at[source], ref["grid_in"].at[number], "grid", number, axis).wait_recv()
                arrived_rows = ref["grid_in"][number]
            placing = ref["placing"][number]
            visible = jnp.sum(placing.astype(FULL), axis=1, keepdims=True)
            filled = jnp.where(visible > 0.5, dot(placing, arrived_rows), row_of("mask_token").astype(FULL)).astype(LOW)
            for image in range(IMG_SEQ):
                ref["decoder_input_held"][source * IMG_SEQ + image] = filled[
                    image * PLACES : image * PLACES + quarter_len
                ]
        keep("decoder_input", 1)

    segments = {
        "project": project,
        "second_back": second_back,
        "attended_back": attended_back,
        "delta_first": delta_first,
        "first_back": first_back,
        "decode": decode,
    }
    for slot in range(4):
        segments["feed%d" % slot] = functools.partial(feed, slot)
        segments["multiply_feed%d" % slot] = functools.partial(multiply_feed, slot)
    for pair in range(HEADS // 2):
        segments["attend_back%d" % pair] = functools.partial(attend_back, pair)
    for matrix in ("proj", "out", "qkv"):
        segments["swapped_" + matrix] = functools.partial(swapped, matrix)
    for job in JOBS:
        segments["multiply_" + job] = functools.partial(multiply, job)
    for step in PLAN:
        if step[0] == "do":
            segments[step[1]]()
        elif step[0] == "vec":
            arrive_vec(step[1])
        else:
            arrive(*step)
    for store in stores:
        store.wait()
    for copy in started:
        copy.wait_send()


def finish_kernel(names, *refs):
    ref = dict(zip(names, refs))
    loads, stores = [], []
    for number in range(7):
        load = pltpu.make_async_copy(ref["in%d" % number], ref["low%d" % number], ref["load"].at[number])
        load.start()
        loads.append(load)
    sums = ref["sums"]
    for spot, number in zip(
        (LN1_GAIN, LN1_BIAS, BIAS_Q, BIAS_V, BIAS_OUT, LN2_GAIN, LN2_BIAS, BIAS_DOWN, BIAS_PROJ, MASK), range(10)
    ):
        target = ref["vec%d" % number]
        target[...] = sums[spot, : target.shape[0]]
    wide = sums.shape[1]
    for number in range(ref["vec10"].shape[1] // wide):
        ref["vec10"][:, number * wide : (number + 1) * wide] = sums[BIAS_UP + number : BIAS_UP + number + 1, :]
    for number in range(7):
        loads[number].wait()
        source = ref["low%d" % number]
        if number < 5:
            source = ref["full%d" % number]
            source[...] = ref["low%d" % number][...].astype(FULL)
        store = pltpu.make_async_copy(source, ref["out%d" % number], ref["store"].at[number])
        store.start()
        stores.append(store)
    for store in stores:
        store.wait()


def layer_device(
    tokens,
    image_slot,
    patch_position,
    ln1_gain,
    ln1_bias,
    w_qkv,
    bias_query,
    bias_value,
    w_out,
    bias_out,
    ln2_gain,
    ln2_bias,
    w_up,
    bias_up,
    w_down,
    bias_down,
    w_proj,
    bias_proj,
    mask_token,
    cotangent,
):
    rows, width = tokens.shape
    ff = w_up.shape[1]
    out_width = w_proj.shape[1]
    row = lambda vec: vec.reshape(1, -1)
    vmem = pl.BlockSpec(memory_space=pltpu.VMEM)
    hbm = pl.BlockSpec(memory_space=pl.ANY)
    inputs = {
        "tokens": tokens,
        "slot": row(image_slot),
        "position": row(patch_position),
        "ln1_gain": ln1_gain,
        "ln1_bias": ln1_bias,
        "bias_query": bias_query,
        "bias_value": bias_value,
        "bias_out": bias_out,
        "ln2_gain": ln2_gain,
        "ln2_bias": ln2_bias,
        "bias_up": row(bias_up),
        "bias_down": bias_down,
        "bias_proj": row(bias_proj),
        "mask_token": mask_token,
        "cotangent": cotangent,
        "w_qkv": w_qkv,
        "w_out": w_out,
        "w_proj": w_proj,
        "w_up": w_up,
        "w_down": w_down,
    }
    lefts = {"down": ff, "up": width, "proj": width, "out": width, "qkv": width}
    rights = {"down": width, "up": ff, "proj": out_width, "out": width, "qkv": 3 * width}
    outs = {}
    for name in MATRICES:
        block = (2, 2, 96) if name == "down" else (2, 48)
        outs["grad_" + name] = jax.ShapeDtypeStruct(block + (rights[name],), LOW)
    outs["decoder_input"] = jax.ShapeDtypeStruct(cotangent.shape, LOW)
    outs["grad_tokens"] = jax.ShapeDtypeStruct(tokens.shape, LOW)
    outs["vec_sums"] = jax.ShapeDtypeStruct((16, width), FULL)
    dma = pltpu.SemaphoreType.DMA
    room = {
        "w_qkv_held": (w_qkv.shape, LOW),
        "w_out_held": (w_out.shape, LOW),
        "w_proj_held": (w_proj.shape, LOW),
        "w_up_held": (w_up.shape, LOW),
        "w_down_held": (w_down.shape, LOW),
        "cotangent_held": (cotangent.shape, LOW),
        "decoder_input_held": (cotangent.shape, LOW),
        "grad_tokens_held": (tokens.shape, LOW),
        "places": ((4, 8, rows), jnp.int32),
        "chosen": ((4, IMG_SEQ * CAP, rows), LOW),
        "placing": ((4, IMG_SEQ * PLACES, IMG_SEQ * CAP), LOW),
        "allowed": ((rows, rows), FULL),
        "cot_wide": ((4 * IMG_SEQ, PLACES, out_width), LOW),
        "back_out": ((3, IMG_SEQ * CAP, out_width), LOW),
        "back_in": ((4, IMG_SEQ * CAP, out_width), LOW),
        "grid_out": ((4, IMG_SEQ * CAP, out_width), LOW),
        "grid_in": ((3, IMG_SEQ * CAP, out_width), LOW),
        "normed": ((rows, width), LOW),
        "normed_one": ((rows, width), LOW),
        "qkv": ((rows, 3 * width), LOW),
        "probs": ((HEADS, rows, rows), FULL),
        "attended": ((rows, width), LOW),
        "residual": ((rows, width), FULL),
        "delta_block": ((rows, width), FULL),
        "mlp_out": ((rows, width), FULL),
        "delta_normed": ((rows, width), FULL),
        "block_low": ((rows, width), LOW),
        "delta_attended": ((rows, width), LOW),
        "bias_up_sum": ((1, ff), FULL),
        "vec_own": ((16, width), FULL),
        "vec_held": ((5, 16, width), FULL),
        "vec_in": ((5, 16, width), FULL),
        "left_in_down": ((8, 192, rows), LOW),
        "right_in_down": ((rows, width), LOW),
        "right_in_up": ((4, rows, width // 2), LOW),
        "final_down": ((2, 2, 96, width), LOW),
        "final_up": ((4, 2, 2, 48, width // 2), LOW),
    }
    for name in MATRICES:
        room["left_" + name] = ((lefts[name], rows), LOW)
        room["right_" + name] = ((rows, rights[name]), LOW)
        if name != "down":
            room["left_in_" + name] = ((lefts[name], rows), LOW)
        if name in ("proj", "out", "qkv"):
            room["right_in_" + name] = ((rows, rights[name] // 2), LOW)
            room["final_" + name] = ((2, 2, 48, rights[name] // 2), LOW)
    for job, (name, _, _, wide, _) in JOBS.items():
        block = (96 if name == "down" else 48, wide)
        room["partial_" + job] = ((2, 2, 2, 2) + block, LOW)
        for stage in range(4):
            room["landed_%s_%d" % (job, stage)] = ((2,) * (3 - stage) + block, LOW)
    scratch = {name: pltpu.VMEM(shape, dtype) for name, (shape, dtype) in room.items()}
    scratch["load"] = dma((6,))
    scratch["keep"] = dma((2,))
    scratch["store"] = dma((len(JOBS), 2))
    for kind, shape in (
        ("place", (3,)),
        ("back", (3,)),
        ("grid", (3,)),
        ("core", (8, 2)),
        ("job", (len(JOBS), 7)),
        ("vec", (5,)),
    ):
        scratch[kind + "_send"] = dma(shape)
        scratch[kind + "_recv"] = dma(shape)
    names = tuple(inputs) + tuple(outs) + tuple(scratch)
    found = pl.pallas_call(
        functools.partial(layer_kernel, names),
        out_shape=list(outs.values()),
        in_specs=[hbm if name.startswith("w_") or name == "cotangent" else vmem for name in inputs],
        out_specs=[vmem if name == "vec_sums" else hbm for name in outs],
        scratch_shapes=list(scratch.values()),
        compiler_params=pltpu.CompilerParams(
            collective_id=0, has_side_effects=True, vmem_limit_bytes=63 * 2**20
        ),
        name="layer",
    )(*inputs.values())
    found = dict(zip(outs, found))
    sources = [found["grad_" + name].reshape(-1, rights[name]) for name in MATRICES]
    sources += [found["decoder_input"], found["grad_tokens"]]
    operands = {"in%d" % number: source for number, source in enumerate(sources)}
    operands["sums"] = found["vec_sums"]
    results = {}
    for number, source in enumerate(sources):
        results["out%d" % number] = jax.ShapeDtypeStruct(source.shape, FULL if number < 5 else LOW)
    for number, wide in enumerate([width] * 8 + [out_width] * 2):
        results["vec%d" % number] = jax.ShapeDtypeStruct((wide,), FULL)
    results["vec10"] = jax.ShapeDtypeStruct((1, ff), FULL)
    held = {"low%d" % number: pltpu.VMEM(source.shape, LOW) for number, source in enumerate(sources)}
    held.update({"full%d" % number: pltpu.VMEM(source.shape, FULL) for number, source in enumerate(sources[:5])})
    held["load"] = dma((7,))
    held["store"] = dma((7,))
    done = pl.pallas_call(
        functools.partial(finish_kernel, tuple(operands) + tuple(results) + tuple(held)),
        out_shape=list(results.values()),
        in_specs=[hbm] * 7 + [vmem],
        out_specs=[hbm] * 7 + [vmem] * 11,
        scratch_shapes=list(held.values()),
        compiler_params=pltpu.CompilerParams(vmem_limit_bytes=60 * 2**20),
        name="finish",
    )(*operands.values())
    down, up, proj, out, qkv, decoder_input, grad_tokens = done[:7]
    gain1, bias1, b_query, b_value, b_out, gain2, bias2, b_down, b_proj, mask, b_up = done[7:]
    b_up = b_up.reshape(-1)
    return (
        decoder_input,
        grad_tokens,
        gain1,
        bias1,
        qkv,
        b_query,
        b_value,
        out,
        b_out,
        gain2,
        bias2,
        up,
        b_up,
        down,
        b_down,
        proj,
        b_proj,
        mask,
    )


def solution(mesh):
    placed = (
        P(("img", "pos"), None),
        P(("img", "pos")),
        P(("img", "pos")),
        P(),
        P(),
        P(),
        P(),
        P(),
        P(),
        P(),
        P(),
        P(),
        P(),
        P(),
        P(),
        P(),
        P(),
        P(),
        P(),
        P("img", "pos", None),
    )
    fits = mesh.shape["img"] == 8 and mesh.shape["pos"] == 4
    return jax.shard_map(
        layer_device if fits else general_device,
        mesh=mesh,
        in_specs=placed,
        out_specs=(
            P("img", "pos", None),
            P(("img", "pos"), None),
            P(),
            P(),
            P("img", None),
            P(),
            P(),
            P("img", None),
            P(),
            P(),
            P(),
            P("img", None),
            P(),
            P("img", None),
            P(),
            P("img", None),
            P(),
            P(),
        ),
        check_vma=False,
    )
```

```python
import functools

import jax
import jax.numpy as jnp
from jax import lax
from jax.experimental import pallas as pl
from jax.experimental.pallas import tpu as pltpu
from jax.sharding import PartitionSpec as P

HEADS = 12
HEAD_DIM = 64
ROWS_SEQ = 256
IMG_SEQ = 5
POSITIONS = 196
CAP = 16


EPSILON = 1e-05
NEGATIVE = -1e30
GELU_COEF = 0.7978845608028654


def layer_norm(values, gain_vec, shift_vec):
    centre = jnp.mean(values, axis=-1, keepdims=True)
    centred = values - centre
    return (
        centred
        * lax.rsqrt(jnp.mean(centred * centred, axis=-1, keepdims=True) + EPSILON)
        * gain_vec
        + shift_vec
    )


def gelu_tanh(values):
    return (
        0.5 * values * (1.0 + jnp.tanh(GELU_COEF * (values + 0.044715 * values * values * values)))
    )


def matmul_rows(left, right):
    return jnp.dot(left, right, preferred_element_type=jnp.float32)


def column_sums(values):
    return jnp.sum(values.astype(jnp.float32), axis=0)


def reduce_matrices(members):
    img_count = lax.axis_size("img")
    pos_count = lax.axis_size("pos")
    pieces = [member.reshape(img_count, pos_count, -1) for member in members]
    bucket = jnp.concatenate(pieces, axis=2)
    flat_bucket = bucket.reshape(img_count * pos_count, -1)
    share = lax.psum_scatter(flat_bucket, ("img", "pos"), scatter_dimension=0, tiled=True).reshape(
        1, 1, -1
    )
    summed = lax.all_gather(share.astype(jnp.bfloat16), "pos", axis=1, tiled=True).astype(
        share.dtype
    )
    results = []
    offset = 0
    for member in members:
        extent = member.size // (img_count * pos_count)
        block = summed[0, :, offset : offset + extent]
        results.append(block.reshape(member.shape[0] // img_count, member.shape[1]))
        offset = offset + extent
    return results


def reduce_vectors(members):
    return lax.psum(tuple(members), ("img", "pos"))


def general_device(
    tokens,
    image_slot,
    patch_position,
    ln1_gain,
    ln1_bias,
    w_qkv,
    bias_query,
    bias_value,
    w_out,
    bias_out,
    ln2_gain,
    ln2_bias,
    w_up,
    bias_up,
    w_down,
    bias_down,
    w_proj,
    bias_proj,
    mask_token,
    cotangent,
):
    seq_count = tokens.shape[0] // ROWS_SEQ
    width = w_out.shape[0]
    out_width = w_proj.shape[1]
    pos_count = lax.axis_size("pos")
    quarter_len = POSITIONS // pos_count
    score_scale = HEAD_DIM ** (-0.5)
    head_shape = (seq_count, ROWS_SEQ, HEADS, HEAD_DIM)
    rows_f = tokens.astype(jnp.float32)
    normed_low = layer_norm(rows_f, ln1_gain, ln1_bias).astype(jnp.bfloat16)
    qkv_all = matmul_rows(normed_low, w_qkv)
    queries = (qkv_all[:, :width] + bias_query).astype(jnp.bfloat16).reshape(head_shape)
    keys_h = qkv_all[:, width : 2 * width].astype(jnp.bfloat16).reshape(head_shape)
    values_h = (qkv_all[:, 2 * width :] + bias_value).astype(jnp.bfloat16).reshape(head_shape)
    slot_rows = image_slot.reshape(seq_count, ROWS_SEQ)
    allowed = slot_rows[:, None, :, None] == slot_rows[:, None, None, :]
    raw_scores = (
        jnp.einsum("sqhd,skhd->shqk", queries, keys_h, preferred_element_type=jnp.float32)
        * score_scale
    )
    scores = jnp.where(allowed, raw_scores, NEGATIVE)
    top_score = jnp.max(scores, axis=-1, keepdims=True)
    log_total = top_score + jnp.log(jnp.sum(jnp.exp(scores - top_score), axis=-1, keepdims=True))
    attn_probs = jnp.exp(scores - log_total)
    probs_low = attn_probs.astype(jnp.bfloat16)
    attended = jnp.einsum(
        "shqk,skhd->sqhd", probs_low, values_h, preferred_element_type=jnp.float32
    )
    attended = attended.reshape(-1, width).astype(jnp.bfloat16)
    residual = rows_f + matmul_rows(attended, w_out) + bias_out
    normed_mlp = layer_norm(residual, ln2_gain, ln2_bias).astype(jnp.bfloat16)
    up_proj = matmul_rows(normed_mlp, w_up) + bias_up
    hidden = gelu_tanh(up_proj).astype(jnp.bfloat16)
    block_out = residual + matmul_rows(hidden, w_down) + bias_down
    block_low = block_out.astype(jnp.bfloat16)
    projected = (matmul_rows(block_low, w_proj) + bias_proj).astype(jnp.bfloat16)
    row_index = jnp.arange(ROWS_SEQ, dtype=jnp.int32)
    pos_rows = patch_position.reshape(seq_count, ROWS_SEQ)
    live = slot_rows >= 0
    bucket_id = jnp.where(live, slot_rows * pos_count + pos_rows // quarter_len, -1)
    earlier = (bucket_id[:, :, None] == bucket_id[:, None, :]) & (
        row_index[None, :, None] > row_index[None, None, :]
    )
    rank_in = jnp.sum(earlier.astype(jnp.int32), axis=2)
    target = jnp.where(live, bucket_id * CAP + rank_in, -1)
    slot_index = jnp.arange(IMG_SEQ * pos_count * CAP, dtype=jnp.int32)
    selected = slot_index[None, :, None] == target[:, None, :]
    select_low = selected.astype(jnp.bfloat16)
    outgoing = jnp.einsum(
        "sjr,src->sjc",
        select_low,
        projected.reshape(seq_count, ROWS_SEQ, out_width),
        preferred_element_type=jnp.float32,
    ).astype(jnp.bfloat16)
    outgoing = outgoing.reshape(seq_count * IMG_SEQ, pos_count, CAP, out_width)
    slot_place = (
        jnp.sum(jnp.where(selected, (pos_rows % quarter_len + 1)[:, None, :], 0), axis=2) - 1
    )
    slot_place = slot_place.reshape(seq_count * IMG_SEQ, pos_count, CAP)
    arrived, arrived_place = (
        lax.all_to_all(outgoing, "pos", split_axis=1, concat_axis=0, tiled=True),
        lax.all_to_all(slot_place, "pos", split_axis=1, concat_axis=0, tiled=True),
    )
    arrived = arrived[:, 0]
    arrived_place = arrived_place[:, 0]
    placing = jnp.arange(quarter_len, dtype=jnp.int32)[None, :, None] == arrived_place[:, None, :]
    placing_low = placing.astype(jnp.bfloat16)
    visible = jnp.any(placing, axis=2)
    filled = jnp.einsum("gqj,gjc->gqc", placing_low, arrived, preferred_element_type=jnp.float32)
    decoder_input = jnp.where(
        visible[:, :, None], filled, mask_token.astype(jnp.float32)[None, None, :]
    )
    decoder_input = decoder_input.astype(jnp.bfloat16)
    grad_mask = jnp.sum(
        jnp.where(visible[:, :, None], 0.0, cotangent.astype(jnp.float32)), axis=(0, 1)
    )
    back_slots = jnp.einsum(
        "gqj,gqc->gjc", placing_low, cotangent, preferred_element_type=jnp.float32
    ).astype(jnp.bfloat16)
    returned = lax.all_to_all(back_slots[:, None], "pos", split_axis=0, concat_axis=1, tiled=True)
    delta_proj = (
        jnp.einsum(
            "sjr,sjc->src",
            select_low,
            returned.reshape(seq_count, -1, out_width),
            preferred_element_type=jnp.float32,
        )
        .reshape(-1, out_width)
        .astype(jnp.bfloat16)
    )
    grad_proj = jnp.einsum("rd,rc->dc", block_low, delta_proj, preferred_element_type=jnp.float32)
    grad_bproj = column_sums(delta_proj)
    delta_block = jnp.einsum("rc,dc->rd", delta_proj, w_proj, preferred_element_type=jnp.float32)
    delta_down = delta_block.astype(jnp.bfloat16)
    grad_down = jnp.einsum("rf,rd->fd", hidden, delta_down, preferred_element_type=jnp.float32)
    grad_bdown = column_sums(delta_down)
    delta_hidden = jnp.einsum("rd,fd->rf", delta_down, w_down, preferred_element_type=jnp.float32)
    gelu_back = jax.vjp(gelu_tanh, up_proj)[1]
    delta_up = gelu_back(delta_hidden)[0].astype(jnp.bfloat16)
    grad_up = jnp.einsum("rd,rf->df", normed_mlp, delta_up, preferred_element_type=jnp.float32)
    grad_bup = column_sums(delta_up)
    delta_normed = jnp.einsum("rf,df->rd", delta_up, w_up, preferred_element_type=jnp.float32)
    norm_back = jax.vjp(layer_norm, residual, ln2_gain, ln2_bias)[1]
    delta_resid_norm, grad_gain_two, grad_shift_two = norm_back(delta_normed)
    delta_residual = delta_block + delta_resid_norm
    mlp_mats = reduce_matrices((grad_proj, grad_down, grad_up))
    mlp_vecs = reduce_vectors(
        (grad_bproj, grad_bdown, grad_bup, grad_gain_two, grad_shift_two, grad_mask)
    )
    delta_branch = delta_residual.astype(jnp.bfloat16)
    grad_out = jnp.einsum("re,rd->ed", attended, delta_branch, preferred_element_type=jnp.float32)
    grad_bout = column_sums(delta_branch)
    delta_attended = jnp.einsum(
        "rd,ed->re", delta_branch, w_out, preferred_element_type=jnp.float32
    )
    delta_attended = delta_attended.astype(jnp.bfloat16).reshape(head_shape)
    delta_values = jnp.einsum(
        "shqk,sqhd->skhd", probs_low, delta_attended, preferred_element_type=jnp.float32
    ).astype(jnp.bfloat16)
    delta_probs = jnp.einsum(
        "sqhd,skhd->shqk", delta_attended, values_h, preferred_element_type=jnp.float32
    )
    delta_scores = attn_probs * (
        delta_probs - jnp.sum(delta_probs * attn_probs, axis=-1, keepdims=True)
    )
    delta_scores = delta_scores.astype(jnp.bfloat16)
    delta_queries = (
        (
            jnp.einsum("shqk,skhd->sqhd", delta_scores, keys_h, preferred_element_type=jnp.float32)
            * score_scale
        )
        .astype(jnp.bfloat16)
        .reshape(-1, width)
    )
    delta_keys = (
        (
            jnp.einsum("shqk,sqhd->skhd", delta_scores, queries, preferred_element_type=jnp.float32)
            * score_scale
        )
        .astype(jnp.bfloat16)
        .reshape(-1, width)
    )
    delta_values = delta_values.reshape(-1, width)
    delta_qkv = jnp.concatenate([delta_queries, delta_keys, delta_values], axis=1)
    grad_qkv = jnp.einsum("rd,re->de", normed_low, delta_qkv, preferred_element_type=jnp.float32)
    grad_bquery = column_sums(delta_queries)
    grad_bvalue = column_sums(delta_values)
    delta_first = jnp.einsum("re,de->rd", delta_qkv, w_qkv, preferred_element_type=jnp.float32)
    first_back = jax.vjp(layer_norm, rows_f, ln1_gain, ln1_bias)[1]
    delta_rows, grad_gain_one, grad_shift_one = first_back(delta_first)
    grad_tokens = (delta_residual + delta_rows).astype(jnp.bfloat16)
    attn_mats = reduce_matrices((grad_qkv, grad_out))
    attn_vecs = reduce_vectors((grad_bquery, grad_bvalue, grad_bout, grad_gain_one, grad_shift_one))
    return (
        decoder_input,
        grad_tokens,
        attn_vecs[3],
        attn_vecs[4],
        attn_mats[0],
        attn_vecs[0],
        attn_vecs[1],
        attn_mats[1],
        attn_vecs[2],
        mlp_vecs[3],
        mlp_vecs[4],
        mlp_mats[2],
        mlp_vecs[2],
        mlp_mats[1],
        mlp_vecs[1],
        mlp_mats[0],
        mlp_vecs[0],
        mlp_vecs[5],
    )


MESH_ID = pl.DeviceIdType.MESH
LOW = jnp.bfloat16
FULL = jnp.float32

AXES = ("zh", "zl", "x", "y")
MATRICES = ("down", "up", "proj", "out", "qkv")
JOBS = {
    "down0": ("down", None, 0, 256, ("zl", "zh", "y")),
    "down1": ("down", None, 256, 256, ("zl", "y", "zh")),
    "down2": ("down", None, 512, 256, ("zl", "y", "zh")),
    "up0a": ("up", 0, 0, 256, ("y", "x", "zl", "zh")),
    "up0b": ("up", 0, 256, 128, ("zl", "zh", "y", "x")),
    "up1a": ("up", 1, 0, 256, ("y", "x", "zl", "zh")),
    "up1b": ("up", 1, 256, 128, ("zl", "zh", "y", "x")),
    "up2a": ("up", 2, 0, 256, ("y", "x", "zl", "zh")),
    "up2b": ("up", 2, 256, 128, ("zl", "zh", "y", "x")),
    "up3a": ("up", 3, 0, 256, ("y", "x", "zl", "zh")),
    "up3b": ("up", 3, 256, 128, ("zl", "zh", "y", "x")),
    "proj0": ("proj", None, 0, 256, ("zl", "x", "y", "zh")),
    "out0": ("out", None, 0, 384, ("y", "x", "zl", "zh")),
    "qkv0": ("qkv", None, 0, 256, ("y", "zl", "x", "zh")),
    "qkv1": ("qkv", None, 256, 256, ("x", "y", "zl", "zh")),
    "qkv2": ("qkv", None, 512, 256, ("y", "x", "zl", "zh")),
    "qkv3": ("qkv", None, 768, 256, ("x", "y", "zl", "zh")),
    "qkv4": ("qkv", None, 1024, 128, ("x", "y", "zl", "zh")),
}
PLAN = (
    ("do", "feed0"),
    ("do", "feed1"),
    ("do", "feed2"),
    ("do", "feed3"),
    ("do", "project"),
    ("do", "delta"),
    ("do", "feed_back0"),
    ("do", "feed_back1"),
    ("do", "feed_back2"),
    ("do", "feed_back3"),
    ("do", "swapped_proj_left"),
    ("do", "swapped_proj_right"),
    ("do", "multiply_proj0"),
    ("do", "multiply_up0"),
    ("do", "multiply_up1"),
    ("do", "multiply_up2"),
    ("do", "multiply_up3"),
    ("do", "second_back"),
    ("do", "attended_back"),
    ("do", "transposes"),
    ("do", "attend_back0"),
    ("do", "attend_back1"),
    ("do", "attend_back2"),
    ("proj0", 0, ""),
    ("do", "attend_back3"),
    ("up0a", 0, ""),
    ("do", "attend_back4"),
    ("do", "attend_back5"),
    ("up1b", 0, ""),
    ("do", "swapped_out_left"),
    ("do", "swapped_out_right"),
    ("do", "multiply_out0"),
    ("do", "pass_delta"),
    ("do", "delta_first"),
    ("do", "first_back"),
    ("up0b", 0, ""),
    ("up1a", 0, ""),
    ("do", "swapped_qkv_left"),
    ("do", "swapped_qkv_right"),
    ("do", "multiply_qkv0"),
    ("do", "multiply_qkv1"),
    ("do", "multiply_qkv2"),
    ("do", "multiply_qkv3"),
    ("do", "multiply_qkv4"),
    ("up3b", 0, ""),
    ("vec", 0),
    ("do", "decode"),
    ("up2b", 0, ""),
    ("up2a", 0, ""),
    ("do", "multiply_down0"),
    ("do", "multiply_down1"),
    ("do", "multiply_down2"),
    ("do", "multiply_down3"),
    ("up3b", 1, ""),
    ("proj0", 1, ""),
    ("up3a", 0, ""),
    ("up2b", 1, ""),
    ("down0", 0, "a"),
    ("up0a", 1, ""),
    ("up1b", 1, ""),
    ("down1", 0, "a"),
    ("up1a", 1, ""),
    ("up0b", 1, ""),
    ("down2", 0, "a"),
    ("out0", 0, ""),
    ("down0", 0, "b"),
    ("qkv1", 0, ""),
    ("down1", 0, "b"),
    ("qkv0", 0, ""),
    ("down2", 0, "b"),
    ("qkv3", 0, ""),
    ("qkv4", 0, ""),
    ("qkv2", 0, ""),
    ("vec", 1),
    ("up1a", 2, ""),
    ("up3b", 2, ""),
    ("up0a", 2, ""),
    ("proj0", 2, ""),
    ("up2b", 2, ""),
    ("up2a", 1, ""),
    ("down0", 1, ""),
    ("up1b", 2, ""),
    ("up0b", 2, ""),
    ("qkv0", 1, ""),
    ("up3a", 1, ""),
    ("qkv1", 1, ""),
    ("up3a", 2, ""),
    ("up3a", 3, ""),
    ("down1", 1, ""),
    ("up2a", 2, ""),
    ("up2a", 3, ""),
    ("out0", 1, ""),
    ("proj0", 3, ""),
    ("qkv1", 2, ""),
    ("down2", 1, ""),
    ("qkv2", 1, ""),
    ("up3b", 3, ""),
    ("up2b", 3, ""),
    ("up1b", 3, ""),
    ("up1a", 3, ""),
    ("up0b", 3, ""),
    ("qkv3", 1, ""),
    ("qkv0", 2, ""),
    ("out0", 2, ""),
    ("qkv4", 1, ""),
    ("down1", 2, ""),
    ("vec", 2),
    ("up0a", 3, ""),
    ("down0", 2, ""),
    ("up3a", 4, ""),
    ("qkv1", 3, ""),
    ("qkv2", 2, ""),
    ("up2a", 4, ""),
    ("proj0", 4, ""),
    ("up3b", 4, ""),
    ("qkv3", 2, ""),
    ("up2b", 4, ""),
    ("up1b", 4, ""),
    ("up3a", 5, ""),
    ("up1a", 4, ""),
    ("down2", 2, ""),
    ("up0b", 4, ""),
    ("up2a", 5, ""),
    ("proj0", 5, ""),
    ("qkv4", 2, ""),
    ("up3b", 5, ""),
    ("qkv0", 3, ""),
    ("down1", 4, ""),
    ("up2b", 5, ""),
    ("vec", 3),
    ("up1b", 5, ""),
    ("up0a", 4, ""),
    ("up1a", 5, ""),
    ("up0b", 5, ""),
    ("out0", 3, ""),
    ("down0", 4, ""),
    ("qkv1", 4, ""),
    ("down1", 5, ""),
    ("qkv2", 3, ""),
    ("up0a", 5, ""),
    ("down2", 4, ""),
    ("qkv3", 3, ""),
    ("qkv0", 4, ""),
    ("down0", 5, ""),
    ("qkv4", 3, ""),
    ("qkv1", 5, ""),
    ("out0", 4, ""),
    ("qkv2", 4, ""),
    ("vec", 4),
    ("down2", 5, ""),
    ("qkv0", 5, ""),
    ("qkv3", 4, ""),
    ("qkv4", 4, ""),
    ("out0", 5, ""),
    ("qkv2", 5, ""),
    ("vec", 5),
    ("qkv3", 5, ""),
    ("qkv4", 5, ""),
)
VEC_STEPS = ("core", "x", "y", "zl", "zh", "core")
PEERS = ("diagonal", "y", "core")
PLACES = 64
INPUTS = (
    "slot", "position", "ln1_gain", "ln1_bias", "tokens", "w_qkv", "cotangent", "bias_query", "bias_value", "w_out",
    "bias_out", "ln2_gain", "ln2_bias", "bias_up", "w_up", "w_down", "bias_down", "w_proj", "bias_proj", "mask_token",
)
LN1_GAIN, LN1_BIAS, BIAS_Q, BIAS_V, BIAS_OUT, LN2_GAIN, LN2_BIAS, BIAS_DOWN, BIAS_UP, BIAS_PROJ, MASK = (
    0, 1, 2, 3, 4, 5, 6, 7, 8, 12, 13,
)


def axes_of(matrix):
    return ("zh", "zl", "y") if matrix == "down" else AXES


def device_coords():
    img = lax.axis_index("img")
    pos = lax.axis_index("pos")
    return {"zh": img // 4, "zl": (img // 2) % 2, "x": img % 2, "y": pos // 2, "core": pos % 2}


def device_of(where):
    return (where["zh"] * 4 + where["zl"] * 2 + where["x"], where["y"] * 2 + where["core"])


def block_rows(name):
    return 96 if name == "down" else 48


def dot(left, right):
    return jnp.dot(left, right, preferred_element_type=FULL)


def dot_nt(left, right):
    return lax.dot_general(left, right, (((1,), (1,)), ((), ())), preferred_element_type=FULL)


def dot_tn(left, right):
    return lax.dot_general(left, right, (((0,), (0,)), ((), ())), preferred_element_type=FULL)


def normalised(values):
    centred = values - jnp.mean(values, axis=-1, keepdims=True)
    rstd = lax.rsqrt(jnp.mean(centred * centred, axis=-1, keepdims=True) + EPSILON)
    return centred * rstd, rstd


def norm_rows_back(delta, values, gain):
    xhat, rstd = normalised(values)
    scaled = delta * gain
    rows = rstd * (
        scaled
        - jnp.mean(scaled, axis=-1, keepdims=True)
        - xhat * jnp.mean(scaled * xhat, axis=-1, keepdims=True)
    )
    return rows, delta * xhat


def layer_kernel(names, *refs):
    ref = dict(zip(names, refs))

    def row_of(name, columns=slice(None)):
        return ref[name + "_held"][...].reshape(1, -1)[:, columns]

    me = device_coords()
    core = me["core"]
    my_pos = me["y"] * 2 + core
    width = ref["tokens_held"].shape[1]
    ff = ref["w_up"].shape[1]
    quarter_len = POSITIONS // 4

    def peer(axis):
        if axis == "diagonal":
            return device_of({**me, "y": 1 - me["y"], "core": 1 - core})
        if axis == "across":
            return device_of({**me, "x": 1 - me["x"], "core": 1 - core})
        return device_of({**me, axis: 1 - me[axis]})

    started = []

    def remote(source, target, kind, spot, axis):
        return pltpu.make_async_remote_copy(
            src_ref=source,
            dst_ref=target,
            send_sem=ref[kind + "_send"].at[spot],
            recv_sem=ref[kind + "_recv"].at[spot],
            device_id=peer(axis),
            device_id_type=MESH_ID,
        )

    def begin(copy):
        copy.start()
        started.append(copy)

    barrier = pltpu.get_barrier_semaphore()
    for axis in AXES + ("core", "diagonal", "across"):
        pl.semaphore_signal(barrier, inc=1, device_id=peer(axis), device_id_type=MESH_ID)

    loads = {}
    for number, name in enumerate(INPUTS):
        loads[name] = pltpu.make_async_copy(ref[name], ref[name + "_held"], ref["load"].at[number])
        loads[name].start()

    def loaded(*which):
        for name in which:
            loads[name].wait()

    loaded("slot", "position", "tokens", "ln1_gain", "ln1_bias")
    ref["places"][my_pos, 0:1, :] = row_of("slot")
    ref["places"][my_pos, 1:2, :] = row_of("position")

    def first_norm(step, carry):
        rows = pl.ds(pl.multiple_of(step * 64, 64), 64)
        xhat, _ = normalised(ref["tokens_held"][rows, :].astype(FULL))
        ref["normed"][rows, :] = (xhat * row_of("ln1_gain") + row_of("ln1_bias")).astype(LOW)
        return carry

    lax.fori_loop(0, 4, first_norm, 0, unroll=4)

    loaded("w_qkv", "bias_query", "bias_value")
    third = width // 256
    for number in range(3 * third):
        columns = slice(number * 256, (number + 1) * 256)
        if number == 6:
            pl.semaphore_wait(barrier, 7)
            for spot, axis in enumerate(PEERS):
                begin(remote(ref["places"].at[my_pos], ref["places"].at[my_pos], "place", spot, axis))
        part = dot(ref["normed"][...], ref["w_qkv_held"][:, columns])
        if number < third:
            part = part + row_of("bias_query", columns)
            part = part.astype(LOW) * LOW(HEAD_DIM ** (-0.5))
        elif number >= 2 * third:
            part = part + row_of("bias_value", slice((number - 2 * third) * 256, (number - 2 * third + 1) * 256))
        ref["qkv"][:, columns] = part.astype(LOW)
    ref["normed_one"][...] = ref["normed"][...]

    row_ids = lax.broadcasted_iota(jnp.int32, (ROWS_SEQ, ROWS_SEQ), 0)
    lane_ids = lax.broadcasted_iota(jnp.int32, (ROWS_SEQ, ROWS_SEQ), 1)
    earlier = (row_ids < lane_ids).astype(FULL).astype(LOW)

    def one_hot(count, row):
        ids = lax.broadcasted_iota(jnp.int32, (count, ROWS_SEQ), 0)
        return jnp.where(ids == row, 1.0, 0.0)

    def picked(slot, position, quarter):
        offset = position - quarter * quarter_len
        inside = (slot >= 0) & (offset >= 0) & (offset < quarter_len)
        kinds = one_hot(8, jnp.where(inside, slot, -1))
        ranks = jnp.sum(kinds * dot(kinds.astype(LOW), earlier), axis=0, keepdims=True).astype(jnp.int32)
        chosen = one_hot(IMG_SEQ * CAP, jnp.where(inside, slot * CAP + ranks, -1))
        return chosen.astype(LOW), jnp.where(inside, slot * PLACES + offset, -1)

    for quarter in range(4):
        chosen, _ = picked(row_of("slot"), row_of("position"), quarter)
        ref["chosen"][quarter] = chosen

    slots = one_hot(8, row_of("slot") + 1).astype(LOW)
    ref["allowed"][...] = jnp.where(dot_tn(slots, slots) > 0.5, 0.0, NEGATIVE)

    lane = lax.broadcasted_iota(jnp.int32, (1, 2 * HEAD_DIM), 1)
    sides_full = [(lane < HEAD_DIM).astype(FULL), (lane >= HEAD_DIM).astype(FULL)]
    sides = [side.astype(LOW) for side in sides_full]

    def head_columns(pair, first):
        return pl.ds(first + pair * 2 * HEAD_DIM, 2 * HEAD_DIM)

    def attend(pair, carry):
        queries = ref["qkv"][:, head_columns(pair, 0)]
        keys = ref["qkv"][:, head_columns(pair, width)]
        values = ref["qkv"][:, head_columns(pair, 2 * width)]
        total = None
        for side in range(2):
            scores = dot_nt(queries * sides[side], keys) + ref["allowed"][...]
            powers = jnp.exp(scores - jnp.max(scores, axis=-1, keepdims=True))
            probs = powers / jnp.sum(powers, axis=-1, keepdims=True)
            ref["probs"][pair * 2 + side] = probs
            part = dot(probs.astype(LOW), values) * sides_full[side]
            total = part if total is None else total + part
        ref["attended"][:, head_columns(pair, 0)] = total.astype(LOW)
        return carry

    for pair in range(HEADS // 2):
        attend(pair, 0)

    ref["cot_wide"][...] = jnp.zeros_like(ref["cot_wide"])
    loaded("cotangent")
    for image in range(4 * IMG_SEQ):
        ref["cot_wide"][image, 0:quarter_len, :] = ref["cotangent_held"][image]
    for number, axis in enumerate(PEERS):
        source = peer(axis)[1]
        remote(ref["places"].at[source], ref["places"].at[source], "place", number, axis).wait_recv()
    for number, axis in enumerate(PEERS + ("self",)):
        source = my_pos if axis == "self" else peer(axis)[1]
        slot = ref["places"][source, 0:1, :]
        position = ref["places"][source, 1:2, :]
        chosen, place = picked(slot, position, my_pos)
        filled = one_hot(IMG_SEQ * PLACES, place).astype(LOW)
        placing = dot_nt(filled, chosen).astype(LOW)
        ref["placing"][number] = placing
        cot = ref["cot_wide"][pl.ds(source * IMG_SEQ, IMG_SEQ)].reshape(IMG_SEQ * PLACES, -1)
        back = dot_tn(placing, cot).astype(LOW)
        if axis == "self":
            ref["back_in"][my_pos] = back
        else:
            ref["back_out"][number] = back
    for number, axis in enumerate(PEERS):
        begin(remote(ref["back_out"].at[number], ref["back_in"].at[my_pos], "back", number, axis))
    ref["vec_own"][...] = jnp.zeros_like(ref["vec_own"])

    loaded("w_out", "bias_out")
    for number in range(third):
        columns = slice(number * 256, (number + 1) * 256)
        ref["residual"][:, columns] = (
            ref["tokens_held"][:, columns].astype(FULL)
            + dot(ref["attended"][...], ref["w_out_held"][:, columns])
            + row_of("bias_out", columns)
        )

    def second_norm(step, carry):
        rows = pl.ds(pl.multiple_of(step * 64, 64), 64)
        xhat, _ = normalised(ref["residual"][rows, :])
        ref["normed"][rows, :] = (xhat * row_of("ln2_gain") + row_of("ln2_bias")).astype(LOW)
        return carry

    loaded("ln2_gain", "ln2_bias")
    lax.fori_loop(0, 4, second_norm, 0, unroll=4)
    ref["left_up"][...] = ref["normed"][...].T

    def delta():
        for number, axis in enumerate(PEERS):
            remote(ref["back_out"].at[number], ref["back_in"].at[my_pos], "back", number, axis).wait_recv()
        chosen_all = ref["chosen"][...].reshape(4 * IMG_SEQ * CAP, ROWS_SEQ)
        returned = ref["back_in"][...].reshape(4 * IMG_SEQ * CAP, -1)
        delta_proj = dot_tn(chosen_all, returned)
        ref["vec_own"][BIAS_PROJ : BIAS_PROJ + 1, : delta_proj.shape[1]] = jnp.sum(delta_proj, axis=0, keepdims=True)
        ref["right_proj"][...] = delta_proj.astype(LOW)
        for number in range(third):
            columns = slice(number * 256, (number + 1) * 256)
            part = dot_nt(ref["right_proj"][...], ref["w_proj_held"][columns, :])
            ref["delta_block"][:, columns] = part
            part = part.astype(LOW)
            ref["right_down"][:, columns] = part
            ref["vec_own"][BIAS_DOWN : BIAS_DOWN + 1, columns] = jnp.sum(part.astype(FULL), axis=0, keepdims=True)
        for which in ("delta_side", "delta_across", "side2", "across2", "side3", "across3", "delta", "proj_right"):
            swap(which)

    def pass_delta():
        for which, later in (("delta_side", "on_side"), ("delta_across", "on_across")):
            swapped(which)
            swap(later)

    loaded("w_up", "bias_up")
    ref["bias_up_row"][...] = row_of("bias_up")

    def chunk_of(slot):
        high = 1 - me["zh"] if slot < 2 else me["zh"]
        low = 1 - me["zl"] if slot % 2 == 0 else me["zl"]
        return high, low, high * 2 + low

    def chunk_columns(slot, start=0, wide=width):
        return pl.ds(pl.multiple_of(chunk_of(slot)[2] * width + start, 128), wide)

    def feed(slot):
        columns = chunk_columns(slot)
        up = dot(ref["normed"][...], ref["w_up_held"][:, columns]) + ref["bias_up_row"][:, columns]
        square = up * up
        bent = jnp.tanh(GELU_COEF * (up + 0.044715 * up * square))
        half = 0.5 * (1.0 + bent)
        ref["slope"][slot] = half + 0.5 * up * (1.0 - bent * bent) * (GELU_COEF * (1.0 + 0.134145 * square))
        hidden = (up * half).astype(LOW)
        ref["left_down"][columns, :] = hidden.T
        swap("hidden%d" % slot)
        if slot < 2:
            swap("side%d" % slot)
            swap("across%d" % slot)
        if slot == 0:
            loaded("w_down", "bias_down")
        out = dot(hidden, ref["w_down_held"][columns, :])
        if slot == 0:
            ref["mlp_out"][...] = out
        else:
            ref["mlp_out"][...] += out

    def feed_back(slot):
        columns = chunk_columns(slot)
        back = dot_nt(ref["right_down"][...], ref["w_down_held"][columns, :])
        delta_up = (back * ref["slope"][slot]).astype(LOW)
        ref["right_up"][:, columns] = delta_up
        swap("feed%d" % slot)
        ref["bias_up_sum"][:, columns] = jnp.sum(delta_up.astype(FULL), axis=0, keepdims=True)
        delta = dot_nt(delta_up, ref["w_up_held"][:, columns])
        if slot == 0:
            ref["delta_normed"][...] = delta
        else:
            ref["delta_normed"][...] += delta

    swaps = ("norm", "delta", "proj_left", "proj_right", "out_left", "out_right", "qkv_left", "qkv_right")
    swaps += tuple("hidden%d" % slot for slot in range(4)) + tuple("feed%d" % slot for slot in range(4))
    swaps += tuple("side%d" % slot for slot in range(4)) + tuple("across%d" % slot for slot in range(4))
    swaps += ("delta_side", "delta_across", "on_side", "on_across")

    def swap_copy(which):
        other = 1 - core
        axis = "core"
        half = width // 2
        if which == "norm":
            source, target = ref["left_up"], ref["left_in_up"]
        elif which == "delta":
            source, target = ref["right_down"], ref["right_in_down"].at[0]
        elif which == "delta_side":
            source, target = ref["right_down"].at[:, pl.ds(0, half)], ref["right_in_down"].at[1, :, pl.ds(0, half)]
            axis = "x"
        elif which == "delta_across":
            source, target = ref["right_down"].at[:, pl.ds(half, half)], ref["right_in_down"].at[2, :, pl.ds(half, half)]
            axis = "across"
        elif which == "on_side":
            source = ref["right_in_down"].at[1, :, pl.ds(0, half)]
            target = ref["right_in_down"].at[2, :, pl.ds(0, half)]
        elif which == "on_across":
            source = ref["right_in_down"].at[2, :, pl.ds(half, half)]
            target = ref["right_in_down"].at[1, :, pl.ds(half, half)]
        elif which[:-1] in ("hidden", "side", "across"):
            chunk = chunk_of(int(which[-1]))[2]
            blocks = ref["left_down"].reshape(8, 2, 192, ROWS_SEQ)
            if which.startswith("hidden"):
                source, target = blocks.at[chunk * 2 + me["x"], other], ref["left_in_down"].at[0, chunk]
            elif which.startswith("side"):
                source, target = blocks.at[chunk * 2 + 1 - me["x"], core], ref["left_in_down"].at[1, chunk]
                axis = "x"
            else:
                source, target = blocks.at[chunk * 2 + 1 - me["x"], other], ref["left_in_down"].at[2, chunk]
                axis = "across"
        elif which.startswith("feed"):
            slot = int(which[4:])
            source = ref["right_up"].at[:, chunk_columns(slot, other * half, half)]
            target = ref["right_in_up"].at[slot]
        else:
            matrix, side = which.split("_")
            if side == "left":
                source, target = ref["left_" + matrix], ref["left_in_" + matrix]
            else:
                wide = ref["right_" + matrix].shape[1] // 2
                source = ref["right_" + matrix].at[:, pl.ds(pl.multiple_of(other * wide, 128), wide)]
                target = ref["right_in_" + matrix]
        return remote(source, target, "core", swaps.index(which), axis)

    def swap(which):
        begin(swap_copy(which))

    def swapped(which):
        swap_copy(which).wait_recv()

    job_names = tuple(JOBS)

    def job_final(job):
        matrix, slot, first, wide, _ = JOBS[job]
        final = ref["final_" + matrix]
        if slot is not None:
            final = final.at[chunk_of(slot)[2]]
        return final, pl.ds(first, wide)

    def job_target(job, stage):
        _, slot, _, _, dims = JOBS[job]
        if slot is None or stage > 3 or dims[stage] not in ("zl", "zh"):
            return job
        return "up%d%s" % (slot ^ (1 if dims[stage] == "zl" else 2), job[3:])

    def job_index(job, stage, part, mine):
        dims = JOBS[job][4]
        pick, land = [], []
        for axis in axes_of(JOBS[job][0]):
            if axis in dims[:stage]:
                pick.append(me[axis])
            elif axis == dims[stage]:
                pick.append(me[axis] if mine else 1 - me[axis])
            elif axis == "zh" and part:
                pick.append(1 - me[axis] if part == "a" else me[axis])
                land.append(pick[-1])
            else:
                pick.append(slice(None))
                land.append(slice(None))
        return tuple(pick), tuple(land)

    def job_copy(job, stage, part):
        dims = JOBS[job][4]
        target = job_target(job, stage)
        spot = stage if part != "b" else 6
        send_sem = ref["job_send"].at[job_names.index(job), spot]
        recv_sem = ref["job_recv"].at[job_names.index(target), spot]
        if stage < 4:
            pick, land = job_index(job, stage, part, False)
            source = ref["partial_" + job].at[pick]
            place = ref["landed_%s_%d" % (target, stage)]
            place = place.at[land] if land else place
            axis = dims[stage]
        else:
            final, columns = job_final(job)
            if stage == 4:
                source = place = final.at[core, me["y"], :, columns]
            else:
                source = place = final.at[core, :, :, columns]
            axis = "y" if stage == 4 else "core"
        return pltpu.make_async_remote_copy(
            src_ref=source,
            dst_ref=place,
            send_sem=send_sem,
            recv_sem=recv_sem,
            device_id=peer(axis),
            device_id_type=MESH_ID,
        )

    def first_parts(job):
        return ("a", "b") if JOBS[job][0] == "down" else ("",)

    def needs(job, stage):
        dims = JOBS[job][4]
        firsts = tuple((0, part) for part in first_parts(job))
        if stage == 1:
            return tuple(first for first in firsts if first[1] != "b" or dims[:2] != ("zl", "zh"))
        if stage == 2:
            return ((1, ""),) + firsts
        if stage == 4:
            return ((len(dims) - 1, ""),) + firsts
        return ((stage - 1, ""),)

    arrived, sent = set(), set()

    def send(job, stage, part=""):
        sent.add((job, stage, part))
        begin(job_copy(job, stage, part))

    def arrive(job, stage, part):
        matrix, slot, _, _, dims = JOBS[job]
        axes = axes_of(matrix)
        last = len(dims) - 1
        source = job_copy(job_target(job, stage), stage, part)
        source.wait_recv()
        if stage < 4:
            partial, landed = ref["partial_" + job], ref["landed_%s_%d" % (job, stage)]
            pick, land = job_index(job, stage, part, True)
            free = [spot for spot, index in enumerate(pick) if isinstance(index, slice)]
            for code in range(2 ** len(free)):
                here, there = list(pick), list(land)
                for order, spot in enumerate(free):
                    bit = (code >> (len(free) - 1 - order)) % 2
                    here[spot] = bit
                    there[[place for place, axis in enumerate(axes) if axis not in dims[: stage + 1]].index(spot)] = bit
                sums = partial[tuple(here)] + (landed[tuple(there)] if there else landed[...])
                if stage < last:
                    partial[tuple(here)] = sums
                else:
                    final, columns = job_final(job)
                    final[core, me["y"], :, columns] = sums
        arrived.add((job, stage, part))
        for later in list(range(1, last + 1)) + [4, 5]:
            ready = all((job,) + need in arrived for need in needs(job, later))
            if (job, later, "") not in sent and ready:
                send(job, later)
        if stage == 5:
            final, columns = job_final(job)
            _, _, first, wide, _ = JOBS[job]
            out = ref["grad_" + matrix]
            for side in range(2):
                if matrix == "down":
                    place = out.at[side, :, :, columns]
                else:
                    start = side * ref["final_" + matrix].shape[-1] + first
                    if slot is not None:
                        place = out.at[:, :, chunk_columns(slot, start, wide)]
                    else:
                        place = out.at[:, :, pl.ds(start, wide)]
                store = pltpu.make_async_copy(
                    final.at[side, :, :, columns], place, ref["store"].at[job_names.index(job), side]
                )
                store.start()
                stores.append(store)

    stores = []

    def multiply_down(slot):
        if slot == 0:
            for which in ("delta", "on_side", "on_across"):
                swapped(which)
        for which in ("hidden", "side", "across"):
            swapped(which + str(slot))
        high, low, chunk = chunk_of(slot)
        rows = pl.ds(pl.multiple_of((chunk * 2 + me["x"]) * 384 + core * 192, 192), 192)
        total = dot(ref["left_down"][rows, :], ref["right_down"][...])
        for number in range(3):
            total = total + dot(ref["left_in_down"][number, chunk], ref["right_in_down"][number])
        total = total.astype(LOW)
        for job, (matrix, _, first, wide, _) in JOBS.items():
            if matrix == "down":
                for half in range(2):
                    ref["partial_" + job][high, low, half] = total[half * 96 : (half + 1) * 96, first : first + wide]
        if slot % 2 == 1:
            for job in JOBS:
                if JOBS[job][0] == "down":
                    send(job, 0, "ab"[slot // 2])

    def multiply_up(slot):
        if slot == 0:
            swapped("norm")
        swapped("feed%d" % slot)
        for block in range(2):
            rows = slice(block * 384, (block + 1) * 384)
            total = dot(
                ref["left_up"][rows, :], ref["right_up"][:, chunk_columns(slot, core * (width // 2), width // 2)]
            ) + dot(ref["left_in_up"][rows, :], ref["right_in_up"][slot])
            total = total.astype(LOW)
            for job, (matrix, own, first, wide, _) in JOBS.items():
                if matrix == "up" and own == slot:
                    for part in range(8):
                        ref["partial_" + job][block, part // 4, (part // 2) % 2, part % 2] = total[
                            part * 48 : (part + 1) * 48, first : first + wide
                        ]
        for job, (matrix, own, _, _, _) in JOBS.items():
            if matrix == "up" and own == slot:
                send(job, 0)

    def multiply(job):
        matrix, _, first, wide, _ = JOBS[job]
        wide_half = ref["right_" + matrix].shape[1] // 2
        columns = pl.ds(pl.multiple_of(core * wide_half + first, 128), wide)
        for block in range(2):
            rows = slice(block * 384, (block + 1) * 384)
            total = dot(ref["left_" + matrix][rows, :], ref["right_" + matrix][:, columns]) + dot(
                ref["left_in_" + matrix][rows, :], ref["right_in_" + matrix][:, first : first + wide]
            )
            total = total.astype(LOW)
            for part in range(8):
                ref["partial_" + job][block, part // 4, (part // 2) % 2, part % 2] = total[part * 48 : (part + 1) * 48]
        send(job, 0)

    def vec_rows(side):
        return pl.ds(pl.multiple_of(side * 8, 8), 8)

    def vec_copy(stage):
        source = ref["vec_own"].at[vec_rows(1 - core)] if stage == 0 else ref["vec_held"].at[stage]
        return remote(source, ref["vec_in"].at[stage], "vec", stage, VEC_STEPS[stage])

    def arrive_vec(stage):
        vec_copy(stage).wait_recv()
        if stage == 5:
            ref["vec_sums"][vec_rows(1 - core), :] = ref["vec_in"][5]
            return
        own = ref["vec_own"][vec_rows(core), :] if stage == 0 else ref["vec_held"][stage]
        ref["vec_held"][stage + 1] = own + ref["vec_in"][stage]
        begin(vec_copy(stage + 1))
        if stage == 4:
            ref["vec_sums"][vec_rows(core), :] = ref["vec_held"][5]

    swap("norm")

    def project():
        for number in range(third):
            columns = slice(number * 256, (number + 1) * 256)
            ref["block_low"][:, columns] = (
                ref["residual"][:, columns] + ref["mlp_out"][:, columns] + row_of("bias_down", columns)
            ).astype(LOW)
        ref["left_proj"][...] = ref["block_low"][...].T
        swap("proj_left")
        loaded("w_proj", "bias_proj")
        projected = (dot(ref["block_low"][...], ref["w_proj_held"][...]) + row_of("bias_proj")).astype(LOW)
        outgoing = dot(ref["chosen"][...].reshape(4 * IMG_SEQ * CAP, ROWS_SEQ), projected).astype(LOW)
        ref["grid_out"][...] = outgoing.reshape(4, IMG_SEQ * CAP, -1)
        for number, axis in enumerate(PEERS):
            begin(remote(ref["grid_out"].at[peer(axis)[1]], ref["grid_in"].at[number], "grid", number, axis))

    def second_back():
        sums = [jnp.zeros((1, width), FULL)] * 3
        for step in range(4):
            rows = slice(step * 64, (step + 1) * 64)
            delta = ref["delta_normed"][rows, :]
            row_term, gains = norm_rows_back(delta, ref["residual"][rows, :], row_of("ln2_gain"))
            total = ref["delta_block"][rows, :] + row_term
            low = total.astype(LOW)
            ref["delta_block"][rows, :] = total
            ref["right_out"][rows, :] = low
            news = (gains, delta, low.astype(FULL))
            sums = [old + jnp.sum(new, axis=0, keepdims=True) for old, new in zip(sums, news)]
        for spot, total in zip((LN2_GAIN, LN2_BIAS, BIAS_OUT), sums):
            ref["vec_own"][spot : spot + 1, :] = total
        swap("out_right")

    def attended_back():
        for number in range(third):
            columns = slice(number * 256, (number + 1) * 256)
            ref["delta_attended"][:, columns] = dot_nt(ref["right_out"][...], ref["w_out_held"][columns, :]).astype(LOW)

    def transposes():
        ref["left_out"][...] = ref["attended"][...].T
        swap("out_left")
        ref["left_qkv"][...] = ref["normed_one"][...].T
        swap("qkv_left")

    def attend_back(pair):
        queries = ref["qkv"][:, head_columns(pair, 0)]
        keys = ref["qkv"][:, head_columns(pair, width)]
        values = ref["qkv"][:, head_columns(pair, 2 * width)]
        delta = ref["delta_attended"][:, head_columns(pair, 0)]
        totals = [None, None, None]
        for side in range(2):
            probs = ref["probs"][pair * 2 + side]
            delta_probs = dot_nt(delta * sides[side], values)
            delta_scores = probs * (delta_probs - jnp.sum(delta_probs * probs, axis=-1, keepdims=True))
            delta_scores = delta_scores.astype(LOW)
            parts = (
                dot(delta_scores, keys) * (HEAD_DIM ** (-0.5)),
                dot_tn(delta_scores, queries),
                dot_tn(probs.astype(LOW), delta),
            )
            for spot, part in enumerate(parts):
                part = part * sides_full[side]
                totals[spot] = part if totals[spot] is None else totals[spot] + part
        for spot, total in enumerate(totals):
            ref["right_qkv"][:, head_columns(pair, spot * width)] = total.astype(LOW)
        if pair == HEADS // 2 - 1:
            swap("qkv_right")

    def delta_first():
        for number in range(third):
            columns = slice(number * 256, (number + 1) * 256)
            ref["delta_normed"][:, columns] = dot_nt(ref["right_qkv"][...], ref["w_qkv_held"][columns, :])
        for spot, first in ((BIAS_Q, 0), (BIAS_V, 2 * width)):
            ref["vec_own"][spot : spot + 1, :] = jnp.sum(
                ref["right_qkv"][:, first : first + width].astype(FULL), axis=0, keepdims=True
            )

    def first_back():
        sums = [jnp.zeros((1, width), FULL)] * 2
        for step in range(4):
            rows = slice(step * 64, (step + 1) * 64)
            delta = ref["delta_normed"][rows, :]
            row_term, gains = norm_rows_back(delta, ref["tokens_held"][rows, :].astype(FULL), row_of("ln1_gain"))
            ref["grad_tokens"][rows, :] = (ref["delta_block"][rows, :] + row_term).astype(LOW)
            sums = [old + jnp.sum(new, axis=0, keepdims=True) for old, new in zip(sums, (gains, delta))]
        for spot, total in zip((LN1_GAIN, LN1_BIAS), sums):
            ref["vec_own"][spot : spot + 1, :] = total
        for number in range(ff // width):
            ref["vec_own"][BIAS_UP + number : BIAS_UP + number + 1, :] = ref["bias_up_sum"][
                :, number * width : (number + 1) * width
            ]
        mask_sum = jnp.zeros((8, ref["cot_wide"].shape[2]), FULL)
        for number, axis in enumerate(PEERS + ("self",)):
            source = my_pos if axis == "self" else peer(axis)[1]
            cot = ref["cot_wide"][pl.ds(source * IMG_SEQ, IMG_SEQ)].reshape(IMG_SEQ * PLACES, -1)
            seen = dot_nt(jnp.ones((8, IMG_SEQ * CAP), LOW), ref["placing"][number])
            mask_sum = mask_sum + dot((1.0 - seen).astype(LOW), cot)
        ref["vec_own"][MASK : MASK + 1, : mask_sum.shape[1]] = mask_sum[0:1]
        begin(vec_copy(0))

    def decode():
        loaded("mask_token")
        for number, axis in enumerate(PEERS + ("self",)):
            if axis == "self":
                source = my_pos
                arrived_rows = ref["grid_out"][my_pos]
            else:
                source = peer(axis)[1]
                remote(ref["grid_out"].at[source], ref["grid_in"].at[number], "grid", number, axis).wait_recv()
                arrived_rows = ref["grid_in"][number]
            placing = ref["placing"][number]
            visible = jnp.sum(placing.astype(FULL), axis=1, keepdims=True)
            filled = jnp.where(visible > 0.5, dot(placing, arrived_rows), row_of("mask_token").astype(FULL)).astype(LOW)
            for image in range(IMG_SEQ):
                ref["decoder_input"][source * IMG_SEQ + image] = filled[
                    image * PLACES : image * PLACES + quarter_len
                ]

    segments = {
        "project": project,
        "delta": delta,
        "pass_delta": pass_delta,
        "transposes": transposes,
        "second_back": second_back,
        "attended_back": attended_back,
        "delta_first": delta_first,
        "first_back": first_back,
        "decode": decode,
    }
    for slot in range(4):
        segments["feed%d" % slot] = functools.partial(feed, slot)
        segments["feed_back%d" % slot] = functools.partial(feed_back, slot)
        segments["multiply_down%d" % slot] = functools.partial(multiply_down, slot)
        segments["multiply_up%d" % slot] = functools.partial(multiply_up, slot)
    for pair in range(HEADS // 2):
        segments["attend_back%d" % pair] = functools.partial(attend_back, pair)
    for which in swaps[2:8]:
        segments["swapped_" + which] = functools.partial(swapped, which)
    for job in JOBS:
        if JOBS[job][0] not in ("down", "up"):
            segments["multiply_" + job] = functools.partial(multiply, job)
    for step in PLAN:
        if step[0] == "do":
            segments[step[1]]()
        elif step[0] == "vec":
            arrive_vec(step[1])
        else:
            arrive(*step)
    for store in stores:
        store.wait()
    for copy in started:
        copy.wait_send()


def finish_kernel(names, *refs):
    ref = dict(zip(names, refs))
    stores = []
    for number in (5, 6, 1, 0, 4, 3, 2):
        source = ref["in%d" % number]
        if number < 5:
            source = ref["full%d" % number]
            source[...] = ref["in%d" % number][...].astype(FULL)
        store = pltpu.make_async_copy(source, ref["out%d" % number], ref["store"].at[number])
        store.start()
        stores.append(store)
    sums = ref["sums"]
    for spot, number in zip(
        (LN1_GAIN, LN1_BIAS, BIAS_Q, BIAS_V, BIAS_OUT, LN2_GAIN, LN2_BIAS, BIAS_DOWN, BIAS_PROJ, MASK), range(10)
    ):
        target = ref["vec%d" % number]
        target[...] = sums[spot, : target.shape[0]]
    wide = sums.shape[1]
    for number in range(ref["vec10"].shape[1] // wide):
        ref["vec10"][:, number * wide : (number + 1) * wide] = sums[BIAS_UP + number : BIAS_UP + number + 1, :]
    for store in stores:
        store.wait()


def layer_device(
    tokens,
    image_slot,
    patch_position,
    ln1_gain,
    ln1_bias,
    w_qkv,
    bias_query,
    bias_value,
    w_out,
    bias_out,
    ln2_gain,
    ln2_bias,
    w_up,
    bias_up,
    w_down,
    bias_down,
    w_proj,
    bias_proj,
    mask_token,
    cotangent,
):
    rows, width = tokens.shape
    ff = w_up.shape[1]
    out_width = w_proj.shape[1]
    vmem = pl.BlockSpec(memory_space=pltpu.VMEM)
    hbm = pl.BlockSpec(memory_space=pl.ANY)
    inputs = {
        "tokens": tokens,
        "slot": image_slot,
        "position": patch_position,
        "ln1_gain": ln1_gain,
        "ln1_bias": ln1_bias,
        "bias_query": bias_query,
        "bias_value": bias_value,
        "bias_out": bias_out,
        "ln2_gain": ln2_gain,
        "ln2_bias": ln2_bias,
        "bias_up": bias_up,
        "bias_down": bias_down,
        "bias_proj": bias_proj,
        "mask_token": mask_token,
        "cotangent": cotangent,
        "w_qkv": w_qkv,
        "w_out": w_out,
        "w_proj": w_proj,
        "w_up": w_up,
        "w_down": w_down,
    }
    lefts = {"down": ff, "up": width, "proj": width, "out": width, "qkv": width}
    rights = {"down": width, "up": ff, "proj": out_width, "out": width, "qkv": 3 * width}
    outs = {}
    for name in MATRICES:
        block = (2, 2, 96) if name == "down" else (2, 48)
        outs["grad_" + name] = pltpu.VMEM(block + (rights[name],), LOW)
    outs["decoder_input"] = pltpu.VMEM(cotangent.shape, LOW)
    outs["grad_tokens"] = pltpu.VMEM(tokens.shape, LOW)
    outs["vec_sums"] = pltpu.VMEM((16, width), FULL)
    dma = pltpu.SemaphoreType.DMA
    room = {name + "_held": (array.shape, array.dtype) for name, array in inputs.items()}
    room |= {
        "slope": ((4, rows, width), FULL),
        "bias_up_row": ((1, ff), FULL),
        "places": ((4, 8, rows), jnp.int32),
        "chosen": ((4, IMG_SEQ * CAP, rows), LOW),
        "placing": ((4, IMG_SEQ * PLACES, IMG_SEQ * CAP), LOW),
        "allowed": ((rows, rows), FULL),
        "cot_wide": ((4 * IMG_SEQ, PLACES, out_width), LOW),
        "back_out": ((3, IMG_SEQ * CAP, out_width), LOW),
        "back_in": ((4, IMG_SEQ * CAP, out_width), LOW),
        "grid_out": ((4, IMG_SEQ * CAP, out_width), LOW),
        "grid_in": ((3, IMG_SEQ * CAP, out_width), LOW),
        "normed": ((rows, width), LOW),
        "normed_one": ((rows, width), LOW),
        "qkv": ((rows, 3 * width), LOW),
        "probs": ((HEADS, rows, rows), FULL),
        "attended": ((rows, width), LOW),
        "residual": ((rows, width), FULL),
        "delta_block": ((rows, width), FULL),
        "mlp_out": ((rows, width), FULL),
        "delta_normed": ((rows, width), FULL),
        "block_low": ((rows, width), LOW),
        "delta_attended": ((rows, width), LOW),
        "bias_up_sum": ((1, ff), FULL),
        "vec_own": ((16, width), FULL),
        "vec_held": ((6, 8, width), FULL),
        "vec_in": ((6, 8, width), FULL),
        "left_in_down": ((3, 4, 192, rows), LOW),
        "right_in_down": ((3, rows, width), LOW),
        "right_in_up": ((4, rows, width // 2), LOW),
        "final_down": ((2, 2, 96, width), LOW),
        "final_up": ((4, 2, 2, 48, width // 2), LOW),
    }
    for name in MATRICES:
        room["left_" + name] = ((lefts[name], rows), LOW)
        room["right_" + name] = ((rows, rights[name]), LOW)
        if name != "down":
            room["left_in_" + name] = ((lefts[name], rows), LOW)
        if name in ("proj", "out", "qkv"):
            room["right_in_" + name] = ((rows, rights[name] // 2), LOW)
            room["final_" + name] = ((2, 2, 48, rights[name] // 2), LOW)
    for job, (name, _, _, wide, _) in JOBS.items():
        block = (96 if name == "down" else 48, wide)
        count = len(axes_of(name))
        room["partial_" + job] = ((2,) * count + block, LOW)
        for stage in range(count):
            room["landed_%s_%d" % (job, stage)] = ((2,) * (count - 1 - stage) + block, LOW)
    scratch = {name: pltpu.VMEM(shape, dtype) for name, (shape, dtype) in room.items()}
    scratch["load"] = dma((len(inputs),))
    scratch["store"] = dma((len(JOBS), 2))
    for kind, shape in (
        ("place", (3,)),
        ("back", (3,)),
        ("grid", (3,)),
        ("core", (28,)),
        ("job", (len(JOBS), 7)),
        ("vec", (6,)),
    ):
        scratch[kind + "_send"] = dma(shape)
        scratch[kind + "_recv"] = dma(shape)
    names = tuple(inputs) + tuple(outs) + tuple(scratch)
    found = pl.pallas_call(
        functools.partial(layer_kernel, names),
        out_shape=list(outs.values()),
        in_specs=[hbm] * len(inputs),
        out_specs=[vmem] * len(outs),
        scratch_shapes=list(scratch.values()),
        compiler_params=pltpu.CompilerParams(
            collective_id=0, has_side_effects=True, vmem_limit_bytes=59 * 2**20
        ),
        name="layer",
    )(*inputs.values())
    found = dict(zip(outs, found))
    sources = [found["grad_" + name].reshape(-1, rights[name]) for name in MATRICES]
    sources += [found["decoder_input"], found["grad_tokens"]]
    operands = {"in%d" % number: source for number, source in enumerate(sources)}
    operands["sums"] = found["vec_sums"]
    results = {}
    for number, source in enumerate(sources):
        results["out%d" % number] = jax.ShapeDtypeStruct(source.shape, FULL if number < 5 else LOW)
    for number, wide in enumerate([width] * 8 + [out_width] * 2):
        results["vec%d" % number] = jax.ShapeDtypeStruct((wide,), FULL)
    results["vec10"] = jax.ShapeDtypeStruct((1, ff), FULL)
    held = {"full%d" % number: pltpu.VMEM(source.shape, FULL) for number, source in enumerate(sources[:5])}
    held["store"] = dma((7,))
    done = pl.pallas_call(
        functools.partial(finish_kernel, tuple(operands) + tuple(results) + tuple(held)),
        out_shape=list(results.values()),
        in_specs=[vmem] * 8,
        out_specs=[hbm] * 7 + [vmem] * 11,
        scratch_shapes=list(held.values()),
        compiler_params=pltpu.CompilerParams(vmem_limit_bytes=24 * 2**20),
        name="finish",
    )(*operands.values())
    down, up, proj, out, qkv, decoder_input, grad_tokens = done[:7]
    gain1, bias1, b_query, b_value, b_out, gain2, bias2, b_down, b_proj, mask, b_up = done[7:]
    b_up = b_up.reshape(-1)
    return (
        decoder_input,
        grad_tokens,
        gain1,
        bias1,
        qkv,
        b_query,
        b_value,
        out,
        b_out,
        gain2,
        bias2,
        up,
        b_up,
        down,
        b_down,
        proj,
        b_proj,
        mask,
    )


def solution(mesh):
    placed = (
        P(("img", "pos"), None),
        P(("img", "pos")),
        P(("img", "pos")),
        P(),
        P(),
        P(),
        P(),
        P(),
        P(),
        P(),
        P(),
        P(),
        P(),
        P(),
        P(),
        P(),
        P(),
        P(),
        P(),
        P("img", "pos", None),
    )
    fits = mesh.shape["img"] == 8 and mesh.shape["pos"] == 4
    return jax.shard_map(
        layer_device if fits else general_device,
        mesh=mesh,
        in_specs=placed,
        out_specs=(
            P("img", "pos", None),
            P(("img", "pos"), None),
            P(),
            P(),
            P("img", None),
            P(),
            P(),
            P("img", None),
            P(),
            P(),
            P(),
            P("img", None),
            P(),
            P("img", None),
            P(),
            P("img", None),
            P(),
            P(),
        ),
        check_vma=False,
    )
```

```python
import functools

import jax
import jax.numpy as jnp
from jax import lax
from jax.experimental import pallas as pl
from jax.experimental.pallas import tpu as pltpu
from jax.sharding import PartitionSpec as P

HEADS = 12
HEAD_DIM = 64
ROWS_SEQ = 256
IMG_SEQ = 5
POSITIONS = 196
CAP = 16


EPSILON = 1e-05
NEGATIVE = -1e30
GELU_COEF = 0.7978845608028654


def layer_norm(values, gain_vec, shift_vec):
    centre = jnp.mean(values, axis=-1, keepdims=True)
    centred = values - centre
    return (
        centred
        * lax.rsqrt(jnp.mean(centred * centred, axis=-1, keepdims=True) + EPSILON)
        * gain_vec
        + shift_vec
    )


def gelu_tanh(values):
    return (
        0.5 * values * (1.0 + jnp.tanh(GELU_COEF * (values + 0.044715 * values * values * values)))
    )


def matmul_rows(left, right):
    return jnp.dot(left, right, preferred_element_type=jnp.float32)


def column_sums(values):
    return jnp.sum(values.astype(jnp.float32), axis=0)


def reduce_matrices(members):
    img_count = lax.axis_size("img")
    pos_count = lax.axis_size("pos")
    pieces = [member.reshape(img_count, pos_count, -1) for member in members]
    bucket = jnp.concatenate(pieces, axis=2)
    flat_bucket = bucket.reshape(img_count * pos_count, -1)
    share = lax.psum_scatter(flat_bucket, ("img", "pos"), scatter_dimension=0, tiled=True).reshape(
        1, 1, -1
    )
    summed = lax.all_gather(share.astype(jnp.bfloat16), "pos", axis=1, tiled=True).astype(
        share.dtype
    )
    results = []
    offset = 0
    for member in members:
        extent = member.size // (img_count * pos_count)
        block = summed[0, :, offset : offset + extent]
        results.append(block.reshape(member.shape[0] // img_count, member.shape[1]))
        offset = offset + extent
    return results


def reduce_vectors(members):
    return lax.psum(tuple(members), ("img", "pos"))


def general_device(
    tokens,
    image_slot,
    patch_position,
    ln1_gain,
    ln1_bias,
    w_qkv,
    bias_query,
    bias_value,
    w_out,
    bias_out,
    ln2_gain,
    ln2_bias,
    w_up,
    bias_up,
    w_down,
    bias_down,
    w_proj,
    bias_proj,
    mask_token,
    cotangent,
):
    seq_count = tokens.shape[0] // ROWS_SEQ
    width = w_out.shape[0]
    out_width = w_proj.shape[1]
    pos_count = lax.axis_size("pos")
    quarter_len = POSITIONS // pos_count
    score_scale = HEAD_DIM ** (-0.5)
    head_shape = (seq_count, ROWS_SEQ, HEADS, HEAD_DIM)
    rows_f = tokens.astype(jnp.float32)
    normed_low = layer_norm(rows_f, ln1_gain, ln1_bias).astype(jnp.bfloat16)
    qkv_all = matmul_rows(normed_low, w_qkv)
    queries = (qkv_all[:, :width] + bias_query).astype(jnp.bfloat16).reshape(head_shape)
    keys_h = qkv_all[:, width : 2 * width].astype(jnp.bfloat16).reshape(head_shape)
    values_h = (qkv_all[:, 2 * width :] + bias_value).astype(jnp.bfloat16).reshape(head_shape)
    slot_rows = image_slot.reshape(seq_count, ROWS_SEQ)
    allowed = slot_rows[:, None, :, None] == slot_rows[:, None, None, :]
    raw_scores = (
        jnp.einsum("sqhd,skhd->shqk", queries, keys_h, preferred_element_type=jnp.float32)
        * score_scale
    )
    scores = jnp.where(allowed, raw_scores, NEGATIVE)
    top_score = jnp.max(scores, axis=-1, keepdims=True)
    log_total = top_score + jnp.log(jnp.sum(jnp.exp(scores - top_score), axis=-1, keepdims=True))
    attn_probs = jnp.exp(scores - log_total)
    probs_low = attn_probs.astype(jnp.bfloat16)
    attended = jnp.einsum(
        "shqk,skhd->sqhd", probs_low, values_h, preferred_element_type=jnp.float32
    )
    attended = attended.reshape(-1, width).astype(jnp.bfloat16)
    residual = rows_f + matmul_rows(attended, w_out) + bias_out
    normed_mlp = layer_norm(residual, ln2_gain, ln2_bias).astype(jnp.bfloat16)
    up_proj = matmul_rows(normed_mlp, w_up) + bias_up
    hidden = gelu_tanh(up_proj).astype(jnp.bfloat16)
    block_out = residual + matmul_rows(hidden, w_down) + bias_down
    block_low = block_out.astype(jnp.bfloat16)
    projected = (matmul_rows(block_low, w_proj) + bias_proj).astype(jnp.bfloat16)
    row_index = jnp.arange(ROWS_SEQ, dtype=jnp.int32)
    pos_rows = patch_position.reshape(seq_count, ROWS_SEQ)
    live = slot_rows >= 0
    bucket_id = jnp.where(live, slot_rows * pos_count + pos_rows // quarter_len, -1)
    earlier = (bucket_id[:, :, None] == bucket_id[:, None, :]) & (
        row_index[None, :, None] > row_index[None, None, :]
    )
    rank_in = jnp.sum(earlier.astype(jnp.int32), axis=2)
    target = jnp.where(live, bucket_id * CAP + rank_in, -1)
    slot_index = jnp.arange(IMG_SEQ * pos_count * CAP, dtype=jnp.int32)
    selected = slot_index[None, :, None] == target[:, None, :]
    select_low = selected.astype(jnp.bfloat16)
    outgoing = jnp.einsum(
        "sjr,src->sjc",
        select_low,
        projected.reshape(seq_count, ROWS_SEQ, out_width),
        preferred_element_type=jnp.float32,
    ).astype(jnp.bfloat16)
    outgoing = outgoing.reshape(seq_count * IMG_SEQ, pos_count, CAP, out_width)
    slot_place = (
        jnp.sum(jnp.where(selected, (pos_rows % quarter_len + 1)[:, None, :], 0), axis=2) - 1
    )
    slot_place = slot_place.reshape(seq_count * IMG_SEQ, pos_count, CAP)
    arrived, arrived_place = (
        lax.all_to_all(outgoing, "pos", split_axis=1, concat_axis=0, tiled=True),
        lax.all_to_all(slot_place, "pos", split_axis=1, concat_axis=0, tiled=True),
    )
    arrived = arrived[:, 0]
    arrived_place = arrived_place[:, 0]
    placing = jnp.arange(quarter_len, dtype=jnp.int32)[None, :, None] == arrived_place[:, None, :]
    placing_low = placing.astype(jnp.bfloat16)
    visible = jnp.any(placing, axis=2)
    filled = jnp.einsum("gqj,gjc->gqc", placing_low, arrived, preferred_element_type=jnp.float32)
    decoder_input = jnp.where(
        visible[:, :, None], filled, mask_token.astype(jnp.float32)[None, None, :]
    )
    decoder_input = decoder_input.astype(jnp.bfloat16)
    grad_mask = jnp.sum(
        jnp.where(visible[:, :, None], 0.0, cotangent.astype(jnp.float32)), axis=(0, 1)
    )
    back_slots = jnp.einsum(
        "gqj,gqc->gjc", placing_low, cotangent, preferred_element_type=jnp.float32
    ).astype(jnp.bfloat16)
    returned = lax.all_to_all(back_slots[:, None], "pos", split_axis=0, concat_axis=1, tiled=True)
    delta_proj = (
        jnp.einsum(
            "sjr,sjc->src",
            select_low,
            returned.reshape(seq_count, -1, out_width),
            preferred_element_type=jnp.float32,
        )
        .reshape(-1, out_width)
        .astype(jnp.bfloat16)
    )
    grad_proj = jnp.einsum("rd,rc->dc", block_low, delta_proj, preferred_element_type=jnp.float32)
    grad_bproj = column_sums(delta_proj)
    delta_block = jnp.einsum("rc,dc->rd", delta_proj, w_proj, preferred_element_type=jnp.float32)
    delta_down = delta_block.astype(jnp.bfloat16)
    grad_down = jnp.einsum("rf,rd->fd", hidden, delta_down, preferred_element_type=jnp.float32)
    grad_bdown = column_sums(delta_down)
    delta_hidden = jnp.einsum("rd,fd->rf", delta_down, w_down, preferred_element_type=jnp.float32)
    gelu_back = jax.vjp(gelu_tanh, up_proj)[1]
    delta_up = gelu_back(delta_hidden)[0].astype(jnp.bfloat16)
    grad_up = jnp.einsum("rd,rf->df", normed_mlp, delta_up, preferred_element_type=jnp.float32)
    grad_bup = column_sums(delta_up)
    delta_normed = jnp.einsum("rf,df->rd", delta_up, w_up, preferred_element_type=jnp.float32)
    norm_back = jax.vjp(layer_norm, residual, ln2_gain, ln2_bias)[1]
    delta_resid_norm, grad_gain_two, grad_shift_two = norm_back(delta_normed)
    delta_residual = delta_block + delta_resid_norm
    mlp_mats = reduce_matrices((grad_proj, grad_down, grad_up))
    mlp_vecs = reduce_vectors(
        (grad_bproj, grad_bdown, grad_bup, grad_gain_two, grad_shift_two, grad_mask)
    )
    delta_branch = delta_residual.astype(jnp.bfloat16)
    grad_out = jnp.einsum("re,rd->ed", attended, delta_branch, preferred_element_type=jnp.float32)
    grad_bout = column_sums(delta_branch)
    delta_attended = jnp.einsum(
        "rd,ed->re", delta_branch, w_out, preferred_element_type=jnp.float32
    )
    delta_attended = delta_attended.astype(jnp.bfloat16).reshape(head_shape)
    delta_values = jnp.einsum(
        "shqk,sqhd->skhd", probs_low, delta_attended, preferred_element_type=jnp.float32
    ).astype(jnp.bfloat16)
    delta_probs = jnp.einsum(
        "sqhd,skhd->shqk", delta_attended, values_h, preferred_element_type=jnp.float32
    )
    delta_scores = attn_probs * (
        delta_probs - jnp.sum(delta_probs * attn_probs, axis=-1, keepdims=True)
    )
    delta_scores = delta_scores.astype(jnp.bfloat16)
    delta_queries = (
        (
            jnp.einsum("shqk,skhd->sqhd", delta_scores, keys_h, preferred_element_type=jnp.float32)
            * score_scale
        )
        .astype(jnp.bfloat16)
        .reshape(-1, width)
    )
    delta_keys = (
        (
            jnp.einsum("shqk,sqhd->skhd", delta_scores, queries, preferred_element_type=jnp.float32)
            * score_scale
        )
        .astype(jnp.bfloat16)
        .reshape(-1, width)
    )
    delta_values = delta_values.reshape(-1, width)
    delta_qkv = jnp.concatenate([delta_queries, delta_keys, delta_values], axis=1)
    grad_qkv = jnp.einsum("rd,re->de", normed_low, delta_qkv, preferred_element_type=jnp.float32)
    grad_bquery = column_sums(delta_queries)
    grad_bvalue = column_sums(delta_values)
    delta_first = jnp.einsum("re,de->rd", delta_qkv, w_qkv, preferred_element_type=jnp.float32)
    first_back = jax.vjp(layer_norm, rows_f, ln1_gain, ln1_bias)[1]
    delta_rows, grad_gain_one, grad_shift_one = first_back(delta_first)
    grad_tokens = (delta_residual + delta_rows).astype(jnp.bfloat16)
    attn_mats = reduce_matrices((grad_qkv, grad_out))
    attn_vecs = reduce_vectors((grad_bquery, grad_bvalue, grad_bout, grad_gain_one, grad_shift_one))
    return (
        decoder_input,
        grad_tokens,
        attn_vecs[3],
        attn_vecs[4],
        attn_mats[0],
        attn_vecs[0],
        attn_vecs[1],
        attn_mats[1],
        attn_vecs[2],
        mlp_vecs[3],
        mlp_vecs[4],
        mlp_mats[2],
        mlp_vecs[2],
        mlp_mats[1],
        mlp_vecs[1],
        mlp_mats[0],
        mlp_vecs[0],
        mlp_vecs[5],
    )


MESH_ID = pl.DeviceIdType.MESH
LOW = jnp.bfloat16
FULL = jnp.float32

AXES = ("zh", "zl", "x", "y")
MATRICES = ("down", "up", "proj", "out", "qkv")
JOBS = {
    "down0": ("down", None, 0, 256, ("y", "zl", "zh")),
    "down1": ("down", None, 256, 256, ("y", "zl", "zh")),
    "down2": ("down", None, 512, 256, ("zl", "zh", "y")),
    "up0a": ("up", 0, 0, 256, ("y", "zl", "zh", "x")),
    "up0b": ("up", 0, 256, 128, ("zl", "x", "zh", "y")),
    "up1a": ("up", 1, 0, 384, ("x", "zl", "y", "zh")),
    "up2a": ("up", 2, 0, 384, ("zl", "y", "zh", "x")),
    "up3a": ("up", 3, 0, 384, ("y", "zl", "zh", "x")),
    "proj0": ("proj", None, 0, 256, ("zl", "y", "x", "zh")),
    "out0": ("out", None, 0, 384, ("x", "y", "zl", "zh")),
    "qkv0": ("qkv", None, 0, 256, ("y", "x", "zl", "zh")),
    "qkv1": ("qkv", None, 256, 256, ("y", "zl", "zh", "x")),
    "qkv2": ("qkv", None, 512, 256, ("x", "y", "zl", "zh")),
    "qkv3": ("qkv", None, 768, 256, ("x", "y", "zl", "zh")),
    "qkv4": ("qkv", None, 1024, 128, ("x", "y", "zl", "zh")),
}
PLAN = (
    ("do", "feed0"),
    ("do", "feed1"),
    ("do", "feed2"),
    ("do", "feed3"),
    ("do", "project"),
    ("do", "delta_rows"),
    ("do", "delta"),
    ("do", "feed_back0"),
    ("do", "feed_back1"),
    ("do", "swapped_proj_left"),
    ("do", "swapped_proj_right"),
    ("do", "multiply_proj0"),
    ("do", "feed_back2"),
    ("do", "multiply_up0"),
    ("do", "feed_back3"),
    ("do", "second_back"),
    ("do", "attended_back"),
    ("do", "attend_back0"),
    ("do", "multiply_up1"),
    ("do", "multiply_up3"),
    ("do", "multiply_up2"),
    ("do", "transposes"),
    ("proj0", 0, ""),
    ("do", "attend_back1"),
    ("do", "attend_back2"),
    ("up0a", 0, ""),
    ("do", "attend_back3"),
    ("up0b", 0, ""),
    ("do", "attend_back4"),
    ("do", "attend_back5"),
    ("do", "delta_first"),
    ("do", "pass_delta"),
    ("do", "decode"),
    ("do", "swapped_out_left"),
    ("do", "swapped_out_right"),
    ("do", "multiply_out0"),
    ("do", "multiply_down0"),
    ("do", "multiply_down1"),
    ("up3a", 0, ""),
    ("do", "swapped_qkv_left"),
    ("do", "swapped_qkv_right"),
    ("do", "multiply_qkv0"),
    ("do", "multiply_qkv1"),
    ("do", "multiply_qkv2"),
    ("do", "multiply_qkv3"),
    ("do", "multiply_qkv4"),
    ("up2a", 0, ""),
    ("proj0", 1, ""),
    ("do", "first_back"),
    ("up0a", 1, ""),
    ("down0", 0, "a"),
    ("down2", 0, "a"),
    ("vec", 0),
    ("do", "multiply_down2"),
    ("do", "multiply_down3"),
    ("down1", 0, "a"),
    ("up3a", 1, ""),
    ("qkv0", 0, ""),
    ("up0a", 2, ""),
    ("down2", 0, "b"),
    ("up1a", 0, ""),
    ("up0b", 1, ""),
    ("qkv1", 0, ""),
    ("up3a", 2, ""),
    ("up2a", 1, ""),
    ("up1a", 1, ""),
    ("out0", 0, ""),
    ("down2", 1, ""),
    ("down0", 0, "b"),
    ("up0b", 2, ""),
    ("qkv1", 1, ""),
    ("down1", 0, "b"),
    ("qkv2", 0, ""),
    ("up1a", 2, ""),
    ("down0", 1, ""),
    ("up2a", 2, ""),
    ("out0", 1, ""),
    ("qkv3", 0, ""),
    ("qkv1", 2, ""),
    ("down1", 1, ""),
    ("down2", 2, ""),
    ("up0b", 3, ""),
    ("qkv4", 0, ""),
    ("qkv2", 1, ""),
    ("proj0", 2, ""),
    ("up1a", 3, ""),
    ("vec", 1),
    ("out0", 2, ""),
    ("qkv3", 1, ""),
    ("down0", 2, ""),
    ("qkv0", 1, ""),
    ("qkv2", 2, ""),
    ("down2", 4, ""),
    ("up0a", 3, ""),
    ("up0b", 4, ""),
    ("up3a", 3, ""),
    ("down1", 2, ""),
    ("qkv4", 1, ""),
    ("up2a", 3, ""),
    ("down2", 5, ""),
    ("up0b", 5, ""),
    ("up1a", 4, ""),
    ("qkv1", 3, ""),
    ("proj0", 3, ""),
    ("qkv3", 2, ""),
    ("vec", 2),
    ("qkv0", 2, ""),
    ("down0", 4, ""),
    ("up1a", 5, ""),
    ("out0", 3, ""),
    ("up0a", 4, ""),
    ("qkv4", 2, ""),
    ("up3a", 4, ""),
    ("down0", 5, ""),
    ("qkv2", 3, ""),
    ("vec", 3),
    ("up0a", 5, ""),
    ("down1", 4, ""),
    ("qkv3", 3, ""),
    ("up3a", 5, ""),
    ("up2a", 4, ""),
    ("qkv1", 4, ""),
    ("qkv0", 3, ""),
    ("down1", 5, ""),
    ("proj0", 4, ""),
    ("qkv4", 3, ""),
    ("up2a", 5, ""),
    ("out0", 4, ""),
    ("qkv1", 5, ""),
    ("qkv2", 4, ""),
    ("proj0", 5, ""),
    ("qkv3", 4, ""),
    ("vec", 4),
    ("qkv0", 4, ""),
    ("out0", 5, ""),
    ("qkv4", 4, ""),
    ("qkv2", 5, ""),
    ("qkv3", 5, ""),
    ("vec", 5),
    ("qkv0", 5, ""),
    ("qkv4", 5, ""),
)
VEC_STEPS = ("core", "x", "y", "zl", "zh", "core")
PEERS = ("diagonal", "y", "core")
PLACES = 64
INPUTS = (
    "slot", "position", "ln1_gain", "ln1_bias", "tokens", "w_qkv", "cotangent", "bias_query", "bias_value", "w_out",
    "bias_out", "ln2_gain", "ln2_bias", "bias_up", "w_up", "w_down", "bias_down", "w_proj", "bias_proj", "mask_token",
)
LN1_GAIN, LN1_BIAS, BIAS_Q, BIAS_V, BIAS_OUT, LN2_GAIN, LN2_BIAS, BIAS_DOWN, BIAS_UP, BIAS_PROJ, MASK = (
    0, 1, 2, 3, 4, 5, 6, 7, 8, 12, 13,
)


def axes_of(matrix):
    return ("zh", "zl", "y") if matrix == "down" else AXES


def device_coords():
    img = lax.axis_index("img")
    pos = lax.axis_index("pos")
    return {"zh": img // 4, "zl": (img // 2) % 2, "x": img % 2, "y": pos // 2, "core": pos % 2}


def device_of(where):
    return (where["zh"] * 4 + where["zl"] * 2 + where["x"], where["y"] * 2 + where["core"])


def block_rows(name):
    return 96 if name == "down" else 48


def dot(left, right):
    return jnp.dot(left, right, preferred_element_type=FULL)


def dot_nt(left, right):
    return lax.dot_general(left, right, (((1,), (1,)), ((), ())), preferred_element_type=FULL)


def dot_tn(left, right):
    return lax.dot_general(left, right, (((0,), (0,)), ((), ())), preferred_element_type=FULL)


def normalised(values):
    centred = values - jnp.mean(values, axis=-1, keepdims=True)
    rstd = lax.rsqrt(jnp.mean(centred * centred, axis=-1, keepdims=True) + EPSILON)
    return centred * rstd, rstd


def norm_rows_back(delta, values, gain):
    xhat, rstd = normalised(values)
    scaled = delta * gain
    rows = rstd * (
        scaled
        - jnp.mean(scaled, axis=-1, keepdims=True)
        - xhat * jnp.mean(scaled * xhat, axis=-1, keepdims=True)
    )
    return rows, delta * xhat


def layer_kernel(names, *refs):
    ref = dict(zip(names, refs))

    def row_of(name, columns=slice(None)):
        return ref[name + "_held"][...].reshape(1, -1)[:, columns]

    me = device_coords()
    core = me["core"]
    my_pos = me["y"] * 2 + core
    width = ref["tokens_held"].shape[1]
    ff = ref["w_up"].shape[1]
    quarter_len = POSITIONS // 4

    def peer(axis):
        if axis == "diagonal":
            return device_of({**me, "y": 1 - me["y"], "core": 1 - core})
        if axis == "across":
            return device_of({**me, "x": 1 - me["x"], "core": 1 - core})
        return device_of({**me, axis: 1 - me[axis]})

    leaving = {}

    def remote(source, target, kind, spot, axis, leave=None):
        leave = ref["small_send"].at[spot] if leave is None else leave
        return pltpu.make_async_remote_copy(
            src_ref=source,
            dst_ref=target,
            send_sem=leave,
            recv_sem=ref[kind + "_recv"].at[spot],
            device_id=peer(axis),
            device_id_type=MESH_ID,
        )

    def begin(copy, use):
        if use in leaving:
            leaving.pop(use).wait_send()
        copy.start()
        leaving[use] = copy

    barrier = pltpu.get_barrier_semaphore()
    for axis in AXES + ("core", "diagonal", "across"):
        pl.semaphore_signal(barrier, inc=1, device_id=peer(axis), device_id_type=MESH_ID)

    loads = {}
    for number, name in enumerate(INPUTS):
        loads[name] = pltpu.make_async_copy(ref[name], ref[name + "_held"], ref["load"].at[number])
        loads[name].start()

    def loaded(*which):
        for name in which:
            loads[name].wait()

    loaded("slot", "position", "tokens", "ln1_gain", "ln1_bias")
    ref["places"][my_pos, 0:1, :] = row_of("slot")
    ref["places"][my_pos, 1:2, :] = row_of("position")

    def first_norm(step, carry):
        rows = pl.ds(pl.multiple_of(step * 64, 64), 64)
        xhat, _ = normalised(ref["tokens_held"][rows, :].astype(FULL))
        ref["normed"][rows, :] = (xhat * row_of("ln1_gain") + row_of("ln1_bias")).astype(LOW)
        return carry

    lax.fori_loop(0, 4, first_norm, 0, unroll=4)

    loaded("w_qkv", "bias_query", "bias_value")
    third = width // 256
    for number in range(3 * third):
        columns = slice(number * 256, (number + 1) * 256)
        if number == 6:
            pl.semaphore_wait(barrier, 7)
            for spot, axis in enumerate(PEERS):
                begin(remote(ref["places"].at[my_pos], ref["places"].at[my_pos], "place", spot, axis), spot)
        part = dot(ref["normed"][...], ref["w_qkv_held"][:, columns])
        if number < third:
            part = part + row_of("bias_query", columns)
            part = part.astype(LOW) * LOW(HEAD_DIM ** (-0.5))
        elif number >= 2 * third:
            part = part + row_of("bias_value", slice((number - 2 * third) * 256, (number - 2 * third + 1) * 256))
        ref["qkv"][:, columns] = part.astype(LOW)
    ref["normed_one"][...] = ref["normed"][...]

    row_ids = lax.broadcasted_iota(jnp.int32, (ROWS_SEQ, ROWS_SEQ), 0)
    lane_ids = lax.broadcasted_iota(jnp.int32, (ROWS_SEQ, ROWS_SEQ), 1)
    earlier = (row_ids < lane_ids).astype(FULL).astype(LOW)

    def one_hot(count, row):
        ids = lax.broadcasted_iota(jnp.int32, (count, ROWS_SEQ), 0)
        return jnp.where(ids == row, 1.0, 0.0)

    def picked(slot, position, quarter):
        offset = position - quarter * quarter_len
        inside = (slot >= 0) & (offset >= 0) & (offset < quarter_len)
        kinds = one_hot(8, jnp.where(inside, slot, -1))
        ranks = jnp.sum(kinds * dot(kinds.astype(LOW), earlier), axis=0, keepdims=True).astype(jnp.int32)
        chosen = one_hot(IMG_SEQ * CAP, jnp.where(inside, slot * CAP + ranks, -1))
        return chosen.astype(LOW), jnp.where(inside, slot * PLACES + offset, -1)

    for quarter in range(4):
        chosen, _ = picked(row_of("slot"), row_of("position"), quarter)
        ref["chosen"][quarter] = chosen

    slots = one_hot(8, row_of("slot") + 1).astype(LOW)
    ref["allowed"][...] = jnp.where(dot_tn(slots, slots) > 0.5, 0.0, NEGATIVE)

    lane = lax.broadcasted_iota(jnp.int32, (1, 2 * HEAD_DIM), 1)
    sides_full = [(lane < HEAD_DIM).astype(FULL), (lane >= HEAD_DIM).astype(FULL)]
    sides = [side.astype(LOW) for side in sides_full]

    def head_columns(pair, first):
        return pl.ds(first + pair * 2 * HEAD_DIM, 2 * HEAD_DIM)

    def attend(pair, carry):
        queries = ref["qkv"][:, head_columns(pair, 0)]
        keys = ref["qkv"][:, head_columns(pair, width)]
        values = ref["qkv"][:, head_columns(pair, 2 * width)]
        total = None
        for side in range(2):
            scores = dot_nt(queries * sides[side], keys) + ref["allowed"][...]
            powers = jnp.exp(scores - jnp.max(scores, axis=-1, keepdims=True))
            probs = powers / jnp.sum(powers, axis=-1, keepdims=True)
            ref["probs"][pair * 2 + side] = probs
            part = dot(probs.astype(LOW), values) * sides_full[side]
            total = part if total is None else total + part
        ref["attended"][:, head_columns(pair, 0)] = total.astype(LOW)
        return carry

    for pair in range(HEADS // 2):
        attend(pair, 0)

    ref["cot_wide"][...] = jnp.zeros_like(ref["cot_wide"])
    loaded("cotangent")
    for image in range(4 * IMG_SEQ):
        ref["cot_wide"][image, 0:quarter_len, :] = ref["cotangent_held"][image]
    for number, axis in enumerate(PEERS):
        source = peer(axis)[1]
        remote(ref["places"].at[source], ref["places"].at[source], "place", number, axis).wait_recv()
    for number, axis in enumerate(PEERS + ("self",)):
        source = my_pos if axis == "self" else peer(axis)[1]
        slot = ref["places"][source, 0:1, :]
        position = ref["places"][source, 1:2, :]
        chosen, place = picked(slot, position, my_pos)
        filled = one_hot(IMG_SEQ * PLACES, place).astype(LOW)
        placing = dot_nt(filled, chosen).astype(LOW)
        ref["placing"][number] = placing
        cot = ref["cot_wide"][pl.ds(source * IMG_SEQ, IMG_SEQ)].reshape(IMG_SEQ * PLACES, -1)
        back = dot_tn(placing, cot).astype(LOW)
        if axis == "self":
            ref["back_in"][my_pos] = back
        else:
            ref["back_out"][number] = back
    for number, axis in enumerate(PEERS):
        begin(remote(ref["back_out"].at[number], ref["back_in"].at[my_pos], "back", number, axis), number)
    ref["vec_own"][...] = jnp.zeros_like(ref["vec_own"])

    loaded("w_out", "bias_out")
    for number in range(third):
        columns = slice(number * 256, (number + 1) * 256)
        ref["residual"][:, columns] = (
            ref["tokens_held"][:, columns].astype(FULL)
            + dot(ref["attended"][...], ref["w_out_held"][:, columns])
            + row_of("bias_out", columns)
        )

    def second_norm(step, carry):
        rows = pl.ds(pl.multiple_of(step * 64, 64), 64)
        xhat, _ = normalised(ref["residual"][rows, :])
        ref["normed"][rows, :] = (xhat * row_of("ln2_gain") + row_of("ln2_bias")).astype(LOW)
        return carry

    loaded("ln2_gain", "ln2_bias")
    lax.fori_loop(0, 4, second_norm, 0, unroll=4)
    ref["left_up"][...] = ref["normed"][...].T

    def delta_rows():
        for number, axis in enumerate(PEERS):
            remote(ref["back_out"].at[number], ref["back_in"].at[my_pos], "back", number, axis).wait_recv()
        chosen_all = ref["chosen"][...].reshape(4 * IMG_SEQ * CAP, ROWS_SEQ)
        returned = ref["back_in"][...].reshape(4 * IMG_SEQ * CAP, -1)
        delta_proj = dot_tn(chosen_all, returned)
        ref["vec_own"][BIAS_PROJ : BIAS_PROJ + 1, : delta_proj.shape[1]] = jnp.sum(delta_proj, axis=0, keepdims=True)
        ref["right_proj"][...] = delta_proj.astype(LOW)
        swap("proj_right")

    def delta():
        for number in range(third):
            columns = slice(number * 256, (number + 1) * 256)
            part = dot_nt(ref["right_proj"][...], ref["w_proj_held"][columns, :])
            ref["delta_block"][:, columns] = part
            part = part.astype(LOW)
            ref["right_down"][:, columns] = part
            ref["vec_own"][BIAS_DOWN : BIAS_DOWN + 1, columns] = jnp.sum(part.astype(FULL), axis=0, keepdims=True)
        for which in ("delta_side", "delta_across", "side2", "across2", "side3", "across3", "delta"):
            swap(which)

    def pass_delta():
        for which, later in (("delta_side", "on_side"), ("delta_across", "on_across")):
            swapped(which)
            swap(later)

    loaded("w_up", "bias_up")
    ref["bias_up_row"][...] = row_of("bias_up")

    def chunk_columns(slot, start=0, wide=width):
        if isinstance(start, int):
            return pl.ds(slot * width + start, wide)
        return pl.ds(pl.multiple_of(slot * width + start, 128), wide)

    def feed(slot):
        columns = chunk_columns(slot)
        up = dot(ref["normed"][...], ref["w_up_held"][:, columns]) + ref["bias_up_row"][:, columns]
        square = up * up
        bent = jnp.tanh(GELU_COEF * (up + 0.044715 * up * square))
        half = 0.5 * (1.0 + bent)
        ref["slope"][slot] = half + 0.5 * up * (1.0 - bent * bent) * (GELU_COEF * (1.0 + 0.134145 * square))
        hidden = (up * half).astype(LOW)
        ref["left_down"][columns, :] = hidden.T
        swap("hidden%d" % slot)
        if slot < 2:
            swap("side%d" % slot)
            swap("across%d" % slot)
        if slot == 0:
            loaded("w_down", "bias_down")
        out = dot(hidden, ref["w_down_held"][columns, :])
        if slot == 0:
            ref["mlp_out"][...] = out
        else:
            ref["mlp_out"][...] += out

    def feed_back(slot):
        columns = chunk_columns(slot)
        back = dot_nt(ref["right_down"][...], ref["w_down_held"][columns, :])
        delta_up = (back * ref["slope"][slot]).astype(LOW)
        ref["right_up"][:, columns] = delta_up
        swap("feed%d" % slot)
        ref["bias_up_sum"][:, columns] = jnp.sum(delta_up.astype(FULL), axis=0, keepdims=True)
        delta = dot_nt(delta_up, ref["w_up_held"][:, columns])
        if slot == 0:
            ref["delta_normed"][...] = delta
        else:
            ref["delta_normed"][...] += delta

    swaps = ("norm", "delta", "proj_left", "proj_right", "out_left", "out_right", "qkv_left", "qkv_right")
    swaps += tuple("hidden%d" % slot for slot in range(4)) + tuple("feed%d" % slot for slot in range(4))
    swaps += tuple("side%d" % slot for slot in range(4)) + tuple("across%d" % slot for slot in range(4))
    swaps += ("delta_side", "delta_across", "on_side", "on_across")

    def swap_copy(which):
        other = 1 - core
        axis = "core"
        half = width // 2
        if which == "norm":
            source, target = ref["left_up"], ref["left_in_up"]
        elif which == "delta":
            source, target = ref["right_down"], ref["right_in_down"].at[0]
        elif which == "delta_side":
            source, target = ref["right_down"].at[:, pl.ds(0, half)], ref["right_in_down"].at[1, :, pl.ds(0, half)]
            axis = "x"
        elif which == "delta_across":
            source, target = ref["right_down"].at[:, pl.ds(half, half)], ref["right_in_down"].at[2, :, pl.ds(half, half)]
            axis = "across"
        elif which == "on_side":
            source = ref["right_in_down"].at[1, :, pl.ds(0, half)]
            target = ref["right_in_down"].at[2, :, pl.ds(0, half)]
        elif which == "on_across":
            source = ref["right_in_down"].at[2, :, pl.ds(half, half)]
            target = ref["right_in_down"].at[1, :, pl.ds(half, half)]
        elif which[:-1] in ("hidden", "side", "across"):
            chunk = int(which[-1])
            blocks = ref["left_down"].reshape(8, 2, 192, ROWS_SEQ)
            if which.startswith("hidden"):
                source, target = blocks.at[chunk * 2 + me["x"], other], ref["left_in_down"].at[0, chunk]
            elif which.startswith("side"):
                source, target = blocks.at[chunk * 2 + 1 - me["x"], core], ref["left_in_down"].at[1, chunk]
                axis = "x"
            else:
                source, target = blocks.at[chunk * 2 + 1 - me["x"], other], ref["left_in_down"].at[2, chunk]
                axis = "across"
        elif which.startswith("feed"):
            slot = int(which[4:])
            source = ref["right_up"].at[:, chunk_columns(slot, other * half, half)]
            target = ref["right_in_up"].at[slot]
        else:
            matrix, side = which.split("_")
            if side == "left":
                source, target = ref["left_" + matrix], ref["left_in_" + matrix]
            else:
                wide = ref["right_" + matrix].shape[1] // 2
                source = ref["right_" + matrix].at[:, pl.ds(pl.multiple_of(other * wide, 128), wide)]
                target = ref["right_in_" + matrix]
        leave = swap_leave[which] if which in swap_leave else 0
        return remote(source, target, "core", swaps.index(which), axis, ref["core_send"].at[leave])

    swap_leave = {}

    def swap(which):
        far = which[:-1] in ("side", "across") or which.startswith("delta_")
        many = sum(spot < 6 if not far else spot >= 6 for spot in swap_leave.values())
        swap_leave[which] = 6 + many if far else many % 6
        begin(swap_copy(which), ("core", swap_leave[which]))

    def swapped(which):
        swap_copy(which).wait_recv()

    job_names = tuple(JOBS)

    def job_final(job):
        matrix, slot, first, wide, _ = JOBS[job]
        final = ref["final_" + matrix]
        if slot is not None:
            final = final.at[slot]
        return final, pl.ds(first, wide)

    def job_index(job, stage, part, mine):
        dims = JOBS[job][4]
        pick, land = [], []
        for axis in axes_of(JOBS[job][0]):
            if axis in dims[:stage]:
                pick.append(me[axis])
            elif axis == dims[stage]:
                pick.append(me[axis] if mine else 1 - me[axis])
            elif axis == "zh" and part:
                pick.append("ab".index(part))
                land.append(pick[-1])
            else:
                pick.append(slice(None))
                land.append(slice(None))
        return tuple(pick), tuple(land)

    def job_send_spot(job, stage, part):
        spot = job_names.index(job)
        return 2 * len(job_names) + spot if part == "b" else 2 * spot + stage % 2

    def job_copy(job, stage, part):
        dims = JOBS[job][4]
        spot = stage if part != "b" else 3
        send_sem = ref["job_send"].at[job_send_spot(job, stage, part)]
        recv_sem = ref["job_recv"].at[job_names.index(job), spot]
        if stage < 4:
            pick, land = job_index(job, stage, part, False)
            source = ref["partial_" + job].at[pick]
            place = ref["landed_%s_%d" % (job, stage)]
            place = place.at[land] if land else place
            axis = dims[stage]
        else:
            final, columns = job_final(job)
            if stage == 4:
                source = place = final.at[core, me["y"], :, columns]
            else:
                source = place = final.at[core, :, :, columns]
            axis = "y" if stage == 4 else "core"
        return pltpu.make_async_remote_copy(
            src_ref=source,
            dst_ref=place,
            send_sem=send_sem,
            recv_sem=recv_sem,
            device_id=peer(axis),
            device_id_type=MESH_ID,
        )

    def first_parts(job):
        return ("a", "b") if JOBS[job][0] == "down" else ("",)

    def needs(job, stage):
        dims = JOBS[job][4]
        firsts = tuple((0, part) for part in first_parts(job))
        if stage == 1:
            return firsts
        if stage == 2:
            return ((1, ""),) + firsts
        if stage == 4:
            return ((len(dims) - 1, ""),) + firsts
        return ((stage - 1, ""),)

    arrived, sent = set(), set()

    def send(job, stage, part=""):
        sent.add((job, stage, part))
        begin(job_copy(job, stage, part), ("job", job_send_spot(job, stage, part)))

    def arrive(job, stage, part):
        matrix, slot, _, _, dims = JOBS[job]
        axes = axes_of(matrix)
        last = len(dims) - 1
        job_copy(job, stage, part).wait_recv()
        if stage < 4:
            partial, landed = ref["partial_" + job], ref["landed_%s_%d" % (job, stage)]
            pick, land = job_index(job, stage, part, True)
            free = [spot for spot, index in enumerate(pick) if isinstance(index, slice)]
            for code in range(2 ** len(free)):
                here, there = list(pick), list(land)
                for order, spot in enumerate(free):
                    bit = (code >> (len(free) - 1 - order)) % 2
                    here[spot] = bit
                    there[[place for place, axis in enumerate(axes) if axis not in dims[: stage + 1]].index(spot)] = bit
                sums = partial[tuple(here)] + (landed[tuple(there)] if there else landed[...])
                if stage < last:
                    partial[tuple(here)] = sums
                else:
                    final, columns = job_final(job)
                    final[core, me["y"], :, columns] = sums
        arrived.add((job, stage, part))
        for later in list(range(1, last + 1)) + [4, 5]:
            ready = all((job,) + need in arrived for need in needs(job, later))
            if (job, later, "") not in sent and ready:
                send(job, later)
        if stage == 5:
            final, columns = job_final(job)
            _, _, first, wide, _ = JOBS[job]
            out = ref["grad_" + matrix]
            for side in range(2):
                if matrix == "down":
                    out[side, :, :, columns] = final[side, :, :, columns]
                else:
                    start = side * ref["final_" + matrix].shape[-1] + first
                    place = pl.ds(start, wide) if slot is None else chunk_columns(slot, start, wide)
                    out[:, :, place] = final[side, :, :, columns]

    def multiply_down(slot):
        if slot == 0:
            for which in ("delta", "on_side", "on_across"):
                swapped(which)
        for which in ("hidden", "side", "across"):
            swapped(which + str(slot))
        rows = pl.ds(pl.multiple_of((slot * 2 + me["x"]) * 384 + core * 192, 192), 192)
        total = dot(ref["left_down"][rows, :], ref["right_down"][...])
        for number in range(3):
            total = total + dot(ref["left_in_down"][number, slot], ref["right_in_down"][number])
        total = total.astype(LOW)
        for job, (matrix, _, first, wide, _) in JOBS.items():
            if matrix == "down":
                for half in range(2):
                    ref["partial_" + job][slot // 2, slot % 2, half] = total[half * 96 : (half + 1) * 96, first : first + wide]
        if slot % 2 == 1:
            for job in JOBS:
                if JOBS[job][0] == "down":
                    send(job, 0, "ab"[slot // 2])

    def multiply_up(slot):
        if slot == 0:
            swapped("norm")
        swapped("feed%d" % slot)
        for block in range(2):
            rows = slice(block * 384, (block + 1) * 384)
            total = dot(
                ref["left_up"][rows, :], ref["right_up"][:, chunk_columns(slot, core * (width // 2), width // 2)]
            ) + dot(ref["left_in_up"][rows, :], ref["right_in_up"][slot])
            total = total.astype(LOW)
            for job, (matrix, own, first, wide, _) in JOBS.items():
                if matrix == "up" and own == slot:
                    for part in range(8):
                        ref["partial_" + job][block, part // 4, (part // 2) % 2, part % 2] = total[
                            part * 48 : (part + 1) * 48, first : first + wide
                        ]
        for job, (matrix, own, _, _, _) in JOBS.items():
            if matrix == "up" and own == slot:
                send(job, 0)

    def multiply(job):
        matrix, _, first, wide, _ = JOBS[job]
        wide_half = ref["right_" + matrix].shape[1] // 2
        columns = pl.ds(pl.multiple_of(core * wide_half + first, 128), wide)
        for block in range(2):
            rows = slice(block * 384, (block + 1) * 384)
            total = dot(ref["left_" + matrix][rows, :], ref["right_" + matrix][:, columns]) + dot(
                ref["left_in_" + matrix][rows, :], ref["right_in_" + matrix][:, first : first + wide]
            )
            total = total.astype(LOW)
            for part in range(8):
                ref["partial_" + job][block, part // 4, (part // 2) % 2, part % 2] = total[part * 48 : (part + 1) * 48]
        send(job, 0)

    def vec_rows(side):
        return pl.ds(pl.multiple_of(side * 8, 8), 8)

    def vec_copy(stage):
        source = ref["vec_own"].at[vec_rows(1 - core)] if stage == 0 else ref["vec_held"].at[stage]
        return remote(source, ref["vec_in"].at[stage], "vec", stage, VEC_STEPS[stage], ref["vec_send"].at[0])

    def arrive_vec(stage):
        vec_copy(stage).wait_recv()
        if stage == 5:
            ref["vec_sums"][vec_rows(1 - core), :] = ref["vec_in"][5]
            return
        own = ref["vec_own"][vec_rows(core), :] if stage == 0 else ref["vec_held"][stage]
        ref["vec_held"][stage + 1] = own + ref["vec_in"][stage]
        begin(vec_copy(stage + 1), "vec")
        if stage == 4:
            ref["vec_sums"][vec_rows(core), :] = ref["vec_held"][5]

    swap("norm")

    def project():
        for number in range(third):
            columns = slice(number * 256, (number + 1) * 256)
            ref["block_low"][:, columns] = (
                ref["residual"][:, columns] + ref["mlp_out"][:, columns] + row_of("bias_down", columns)
            ).astype(LOW)
        ref["left_proj"][...] = ref["block_low"][...].T
        swap("proj_left")
        loaded("w_proj", "bias_proj")
        projected = (dot(ref["block_low"][...], ref["w_proj_held"][...]) + row_of("bias_proj")).astype(LOW)
        outgoing = dot(ref["chosen"][...].reshape(4 * IMG_SEQ * CAP, ROWS_SEQ), projected).astype(LOW)
        ref["grid_out"][...] = outgoing.reshape(4, IMG_SEQ * CAP, -1)
        for number, axis in enumerate(PEERS):
            begin(remote(ref["grid_out"].at[peer(axis)[1]], ref["grid_in"].at[number], "grid", number, axis), number)

    def second_back():
        sums = [jnp.zeros((1, width), FULL)] * 3
        for step in range(4):
            rows = slice(step * 64, (step + 1) * 64)
            delta = ref["delta_normed"][rows, :]
            row_term, gains = norm_rows_back(delta, ref["residual"][rows, :], row_of("ln2_gain"))
            total = ref["delta_block"][rows, :] + row_term
            low = total.astype(LOW)
            ref["delta_block"][rows, :] = total
            ref["right_out"][rows, :] = low
            news = (gains, delta, low.astype(FULL))
            sums = [old + jnp.sum(new, axis=0, keepdims=True) for old, new in zip(sums, news)]
        for spot, total in zip((LN2_GAIN, LN2_BIAS, BIAS_OUT), sums):
            ref["vec_own"][spot : spot + 1, :] = total
        swap("out_right")

    def attended_back():
        for number in range(third):
            columns = slice(number * 256, (number + 1) * 256)
            ref["delta_attended"][:, columns] = dot_nt(ref["right_out"][...], ref["w_out_held"][columns, :]).astype(LOW)

    def transposes():
        ref["left_out"][...] = ref["attended"][...].T
        swap("out_left")
        ref["left_qkv"][...] = ref["normed_one"][...].T
        swap("qkv_left")

    def attend_back(pair):
        queries = ref["qkv"][:, head_columns(pair, 0)]
        keys = ref["qkv"][:, head_columns(pair, width)]
        values = ref["qkv"][:, head_columns(pair, 2 * width)]
        delta = ref["delta_attended"][:, head_columns(pair, 0)]
        totals = [None, None, None]
        for side in range(2):
            probs = ref["probs"][pair * 2 + side]
            delta_probs = dot_nt(delta * sides[side], values)
            delta_scores = probs * (delta_probs - jnp.sum(delta_probs * probs, axis=-1, keepdims=True))
            delta_scores = delta_scores.astype(LOW)
            parts = (
                dot(delta_scores, keys) * (HEAD_DIM ** (-0.5)),
                dot_tn(delta_scores, queries),
                dot_tn(probs.astype(LOW), delta),
            )
            for spot, part in enumerate(parts):
                part = part * sides_full[side]
                totals[spot] = part if totals[spot] is None else totals[spot] + part
        for spot, total in enumerate(totals):
            ref["right_qkv"][:, head_columns(pair, spot * width)] = total.astype(LOW)
        if pair == HEADS // 2 - 1:
            swap("qkv_right")

    def delta_first():
        for number in range(third):
            columns = slice(number * 256, (number + 1) * 256)
            ref["delta_normed"][:, columns] = dot_nt(ref["right_qkv"][...], ref["w_qkv_held"][columns, :])
        for spot, first in ((BIAS_Q, 0), (BIAS_V, 2 * width)):
            ref["vec_own"][spot : spot + 1, :] = jnp.sum(
                ref["right_qkv"][:, first : first + width].astype(FULL), axis=0, keepdims=True
            )

    def first_back():
        sums = [jnp.zeros((1, width), FULL)] * 2
        for step in range(4):
            rows = slice(step * 64, (step + 1) * 64)
            delta = ref["delta_normed"][rows, :]
            row_term, gains = norm_rows_back(delta, ref["tokens_held"][rows, :].astype(FULL), row_of("ln1_gain"))
            ref["grad_tokens"][rows, :] = (ref["delta_block"][rows, :] + row_term).astype(LOW)
            sums = [old + jnp.sum(new, axis=0, keepdims=True) for old, new in zip(sums, (gains, delta))]
        for spot, total in zip((LN1_GAIN, LN1_BIAS), sums):
            ref["vec_own"][spot : spot + 1, :] = total
        for number in range(ff // width):
            ref["vec_own"][BIAS_UP + number : BIAS_UP + number + 1, :] = ref["bias_up_sum"][
                :, number * width : (number + 1) * width
            ]
        mask_sum = jnp.zeros((8, ref["cot_wide"].shape[2]), FULL)
        for number, axis in enumerate(PEERS + ("self",)):
            source = my_pos if axis == "self" else peer(axis)[1]
            cot = ref["cot_wide"][pl.ds(source * IMG_SEQ, IMG_SEQ)].reshape(IMG_SEQ * PLACES, -1)
            seen = dot_nt(jnp.ones((8, IMG_SEQ * CAP), LOW), ref["placing"][number])
            mask_sum = mask_sum + dot((1.0 - seen).astype(LOW), cot)
        ref["vec_own"][MASK : MASK + 1, : mask_sum.shape[1]] = mask_sum[0:1]
        begin(vec_copy(0), "vec")

    def decode():
        loaded("mask_token")
        for number, axis in enumerate(PEERS + ("self",)):
            if axis == "self":
                source = my_pos
                arrived_rows = ref["grid_out"][my_pos]
            else:
                source = peer(axis)[1]
                remote(ref["grid_out"].at[source], ref["grid_in"].at[number], "grid", number, axis).wait_recv()
                arrived_rows = ref["grid_in"][number]
            placing = ref["placing"][number]
            visible = jnp.sum(placing.astype(FULL), axis=1, keepdims=True)
            filled = jnp.where(visible > 0.5, dot(placing, arrived_rows), row_of("mask_token").astype(FULL)).astype(LOW)
            for image in range(IMG_SEQ):
                ref["decoder_input"][source * IMG_SEQ + image] = filled[
                    image * PLACES : image * PLACES + quarter_len
                ]

    segments = {
        "project": project,
        "delta_rows": delta_rows,
        "delta": delta,
        "pass_delta": pass_delta,
        "transposes": transposes,
        "second_back": second_back,
        "attended_back": attended_back,
        "delta_first": delta_first,
        "first_back": first_back,
        "decode": decode,
    }
    for slot in range(4):
        segments["feed%d" % slot] = functools.partial(feed, slot)
        segments["feed_back%d" % slot] = functools.partial(feed_back, slot)
        segments["multiply_down%d" % slot] = functools.partial(multiply_down, slot)
        segments["multiply_up%d" % slot] = functools.partial(multiply_up, slot)
    for pair in range(HEADS // 2):
        segments["attend_back%d" % pair] = functools.partial(attend_back, pair)
    for which in swaps[2:8]:
        segments["swapped_" + which] = functools.partial(swapped, which)
    for job in JOBS:
        if JOBS[job][0] not in ("down", "up"):
            segments["multiply_" + job] = functools.partial(multiply, job)
    for step in PLAN:
        if step[0] == "do":
            segments[step[1]]()
        elif step[0] == "vec":
            arrive_vec(step[1])
        else:
            arrive(*step)
    for copy in leaving.values():
        copy.wait_send()


def finish_kernel(names, *refs):
    ref = dict(zip(names, refs))
    stores = []
    for number in (5, 6, 1, 0, 4, 3, 2):
        source = ref["in%d" % number]
        if number < 5:
            source = ref["full%d" % number]
            source[...] = ref["in%d" % number][...].astype(FULL)
        store = pltpu.make_async_copy(source, ref["out%d" % number], ref["store"].at[number])
        store.start()
        stores.append(store)
    sums = ref["sums"]
    for spot, number in zip(
        (LN1_GAIN, LN1_BIAS, BIAS_Q, BIAS_V, BIAS_OUT, LN2_GAIN, LN2_BIAS, BIAS_DOWN, BIAS_PROJ, MASK), range(10)
    ):
        target = ref["vec%d" % number]
        target[...] = sums[spot, : target.shape[0]]
    wide = sums.shape[1]
    for number in range(ref["vec10"].shape[1] // wide):
        ref["vec10"][:, number * wide : (number + 1) * wide] = sums[BIAS_UP + number : BIAS_UP + number + 1, :]
    for store in stores:
        store.wait()


def layer_device(
    tokens,
    image_slot,
    patch_position,
    ln1_gain,
    ln1_bias,
    w_qkv,
    bias_query,
    bias_value,
    w_out,
    bias_out,
    ln2_gain,
    ln2_bias,
    w_up,
    bias_up,
    w_down,
    bias_down,
    w_proj,
    bias_proj,
    mask_token,
    cotangent,
):
    rows, width = tokens.shape
    ff = w_up.shape[1]
    out_width = w_proj.shape[1]
    vmem = pl.BlockSpec(memory_space=pltpu.VMEM)
    hbm = pl.BlockSpec(memory_space=pl.ANY)
    inputs = {
        "tokens": tokens,
        "slot": image_slot,
        "position": patch_position,
        "ln1_gain": ln1_gain,
        "ln1_bias": ln1_bias,
        "bias_query": bias_query,
        "bias_value": bias_value,
        "bias_out": bias_out,
        "ln2_gain": ln2_gain,
        "ln2_bias": ln2_bias,
        "bias_up": bias_up,
        "bias_down": bias_down,
        "bias_proj": bias_proj,
        "mask_token": mask_token,
        "cotangent": cotangent,
        "w_qkv": w_qkv,
        "w_out": w_out,
        "w_proj": w_proj,
        "w_up": w_up,
        "w_down": w_down,
    }
    lefts = {"down": ff, "up": width, "proj": width, "out": width, "qkv": width}
    rights = {"down": width, "up": ff, "proj": out_width, "out": width, "qkv": 3 * width}
    outs = {}
    for name in MATRICES:
        block = (2, 2, 96) if name == "down" else (2, 48)
        outs["grad_" + name] = pltpu.VMEM(block + (rights[name],), LOW)
    outs["decoder_input"] = pltpu.VMEM(cotangent.shape, LOW)
    outs["grad_tokens"] = pltpu.VMEM(tokens.shape, LOW)
    outs["vec_sums"] = pltpu.VMEM((16, width), FULL)
    dma = pltpu.SemaphoreType.DMA
    room = {name + "_held": (array.shape, array.dtype) for name, array in inputs.items()}
    room |= {
        "slope": ((4, rows, width), FULL),
        "bias_up_row": ((1, ff), FULL),
        "places": ((4, 8, rows), jnp.int32),
        "chosen": ((4, IMG_SEQ * CAP, rows), LOW),
        "placing": ((4, IMG_SEQ * PLACES, IMG_SEQ * CAP), LOW),
        "allowed": ((rows, rows), FULL),
        "cot_wide": ((4 * IMG_SEQ, PLACES, out_width), LOW),
        "back_out": ((3, IMG_SEQ * CAP, out_width), LOW),
        "back_in": ((4, IMG_SEQ * CAP, out_width), LOW),
        "grid_out": ((4, IMG_SEQ * CAP, out_width), LOW),
        "grid_in": ((3, IMG_SEQ * CAP, out_width), LOW),
        "normed": ((rows, width), LOW),
        "normed_one": ((rows, width), LOW),
        "qkv": ((rows, 3 * width), LOW),
        "probs": ((HEADS, rows, rows), FULL),
        "attended": ((rows, width), LOW),
        "residual": ((rows, width), FULL),
        "delta_block": ((rows, width), FULL),
        "mlp_out": ((rows, width), FULL),
        "delta_normed": ((rows, width), FULL),
        "block_low": ((rows, width), LOW),
        "delta_attended": ((rows, width), LOW),
        "bias_up_sum": ((1, ff), FULL),
        "vec_own": ((16, width), FULL),
        "vec_held": ((6, 8, width), FULL),
        "vec_in": ((6, 8, width), FULL),
        "left_in_down": ((3, 4, 192, rows), LOW),
        "right_in_down": ((3, rows, width), LOW),
        "right_in_up": ((4, rows, width // 2), LOW),
        "final_down": ((2, 2, 96, width), LOW),
        "final_up": ((4, 2, 2, 48, width // 2), LOW),
    }
    for name in MATRICES:
        room["left_" + name] = ((lefts[name], rows), LOW)
        room["right_" + name] = ((rows, rights[name]), LOW)
        if name != "down":
            room["left_in_" + name] = ((lefts[name], rows), LOW)
        if name in ("proj", "out", "qkv"):
            room["right_in_" + name] = ((rows, rights[name] // 2), LOW)
            room["final_" + name] = ((2, 2, 48, rights[name] // 2), LOW)
    for job, (name, _, _, wide, _) in JOBS.items():
        block = (96 if name == "down" else 48, wide)
        count = len(axes_of(name))
        room["partial_" + job] = ((2,) * count + block, LOW)
        for stage in range(count):
            room["landed_%s_%d" % (job, stage)] = ((2,) * (count - 1 - stage) + block, LOW)
    scratch = {name: pltpu.VMEM(shape, dtype) for name, (shape, dtype) in room.items()}
    scratch["load"] = dma((len(inputs),))
    downs = sum(job[0] == "down" for job in JOBS.values())
    for kind, shape in (("small", (3,)), ("core", (16,)), ("job", (2 * len(JOBS) + downs,)), ("vec", (1,))):
        scratch[kind + "_send"] = dma(shape)
    for kind, shape in (
        ("place", (3,)),
        ("back", (3,)),
        ("grid", (3,)),
        ("core", (28,)),
        ("job", (len(JOBS), 6)),
        ("vec", (6,)),
    ):
        scratch[kind + "_recv"] = dma(shape)
    names = tuple(inputs) + tuple(outs) + tuple(scratch)
    found = pl.pallas_call(
        functools.partial(layer_kernel, names),
        out_shape=list(outs.values()),
        in_specs=[hbm] * len(inputs),
        out_specs=[vmem] * len(outs),
        scratch_shapes=list(scratch.values()),
        compiler_params=pltpu.CompilerParams(
            collective_id=0, has_side_effects=True, vmem_limit_bytes=59 * 2**20
        ),
        name="layer",
    )(*inputs.values())
    found = dict(zip(outs, found))
    sources = [found["grad_" + name].reshape(-1, rights[name]) for name in MATRICES]
    sources += [found["decoder_input"], found["grad_tokens"]]
    operands = {"in%d" % number: source for number, source in enumerate(sources)}
    operands["sums"] = found["vec_sums"]
    results = {}
    for number, source in enumerate(sources):
        results["out%d" % number] = jax.ShapeDtypeStruct(source.shape, FULL if number < 5 else LOW)
    for number, wide in enumerate([width] * 8 + [out_width] * 2):
        results["vec%d" % number] = jax.ShapeDtypeStruct((wide,), FULL)
    results["vec10"] = jax.ShapeDtypeStruct((1, ff), FULL)
    held = {"full%d" % number: pltpu.VMEM(source.shape, FULL) for number, source in enumerate(sources[:5])}
    held["store"] = dma((7,))
    done = pl.pallas_call(
        functools.partial(finish_kernel, tuple(operands) + tuple(results) + tuple(held)),
        out_shape=list(results.values()),
        in_specs=[vmem] * 8,
        out_specs=[hbm] * 7 + [vmem] * 11,
        scratch_shapes=list(held.values()),
        compiler_params=pltpu.CompilerParams(vmem_limit_bytes=24 * 2**20),
        name="finish",
    )(*operands.values())
    down, up, proj, out, qkv, decoder_input, grad_tokens = done[:7]
    gain1, bias1, b_query, b_value, b_out, gain2, bias2, b_down, b_proj, mask, b_up = done[7:]
    b_up = b_up.reshape(-1)
    return (
        decoder_input,
        grad_tokens,
        gain1,
        bias1,
        qkv,
        b_query,
        b_value,
        out,
        b_out,
        gain2,
        bias2,
        up,
        b_up,
        down,
        b_down,
        proj,
        b_proj,
        mask,
    )


def solution(mesh):
    placed = (
        P(("img", "pos"), None),
        P(("img", "pos")),
        P(("img", "pos")),
        P(),
        P(),
        P(),
        P(),
        P(),
        P(),
        P(),
        P(),
        P(),
        P(),
        P(),
        P(),
        P(),
        P(),
        P(),
        P(),
        P("img", "pos", None),
    )
    fits = mesh.shape["img"] == 8 and mesh.shape["pos"] == 4
    return jax.shard_map(
        layer_device if fits else general_device,
        mesh=mesh,
        in_specs=placed,
        out_specs=(
            P("img", "pos", None),
            P(("img", "pos"), None),
            P(),
            P(),
            P("img", None),
            P(),
            P(),
            P("img", None),
            P(),
            P(),
            P(),
            P("img", None),
            P(),
            P("img", None),
            P(),
            P("img", None),
            P(),
            P(),
        ),
        check_vma=False,
    )
```

```python
import functools

import jax
import jax.numpy as jnp
from jax import lax
from jax.experimental import pallas as pl
from jax.experimental.pallas import tpu as pltpu
from jax.sharding import PartitionSpec as P

HEADS = 12
HEAD_DIM = 64
ROWS_SEQ = 256
IMG_SEQ = 5
POSITIONS = 196
CAP = 16


EPSILON = 1e-05
NEGATIVE = -1e30
GELU_COEF = 0.7978845608028654


def layer_norm(values, gain_vec, shift_vec):
    centre = jnp.mean(values, axis=-1, keepdims=True)
    centred = values - centre
    return (
        centred
        * lax.rsqrt(jnp.mean(centred * centred, axis=-1, keepdims=True) + EPSILON)
        * gain_vec
        + shift_vec
    )


def gelu_tanh(values):
    return (
        0.5 * values * (1.0 + jnp.tanh(GELU_COEF * (values + 0.044715 * values * values * values)))
    )


def matmul_rows(left, right):
    return jnp.dot(left, right, preferred_element_type=jnp.float32)


def column_sums(values):
    return jnp.sum(values.astype(jnp.float32), axis=0)


def reduce_matrices(members):
    img_count = lax.axis_size("img")
    pos_count = lax.axis_size("pos")
    pieces = [member.reshape(img_count, pos_count, -1) for member in members]
    bucket = jnp.concatenate(pieces, axis=2)
    flat_bucket = bucket.reshape(img_count * pos_count, -1)
    share = lax.psum_scatter(flat_bucket, ("img", "pos"), scatter_dimension=0, tiled=True).reshape(
        1, 1, -1
    )
    summed = lax.all_gather(share.astype(jnp.bfloat16), "pos", axis=1, tiled=True).astype(
        share.dtype
    )
    results = []
    offset = 0
    for member in members:
        extent = member.size // (img_count * pos_count)
        block = summed[0, :, offset : offset + extent]
        results.append(block.reshape(member.shape[0] // img_count, member.shape[1]))
        offset = offset + extent
    return results


def reduce_vectors(members):
    return lax.psum(tuple(members), ("img", "pos"))


def general_device(
    tokens,
    image_slot,
    patch_position,
    ln1_gain,
    ln1_bias,
    w_qkv,
    bias_query,
    bias_value,
    w_out,
    bias_out,
    ln2_gain,
    ln2_bias,
    w_up,
    bias_up,
    w_down,
    bias_down,
    w_proj,
    bias_proj,
    mask_token,
    cotangent,
):
    seq_count = tokens.shape[0] // ROWS_SEQ
    width = w_out.shape[0]
    out_width = w_proj.shape[1]
    pos_count = lax.axis_size("pos")
    quarter_len = POSITIONS // pos_count
    score_scale = HEAD_DIM ** (-0.5)
    head_shape = (seq_count, ROWS_SEQ, HEADS, HEAD_DIM)
    rows_f = tokens.astype(jnp.float32)
    normed_low = layer_norm(rows_f, ln1_gain, ln1_bias).astype(jnp.bfloat16)
    qkv_all = matmul_rows(normed_low, w_qkv)
    queries = (qkv_all[:, :width] + bias_query).astype(jnp.bfloat16).reshape(head_shape)
    keys_h = qkv_all[:, width : 2 * width].astype(jnp.bfloat16).reshape(head_shape)
    values_h = (qkv_all[:, 2 * width :] + bias_value).astype(jnp.bfloat16).reshape(head_shape)
    slot_rows = image_slot.reshape(seq_count, ROWS_SEQ)
    allowed = slot_rows[:, None, :, None] == slot_rows[:, None, None, :]
    raw_scores = (
        jnp.einsum("sqhd,skhd->shqk", queries, keys_h, preferred_element_type=jnp.float32)
        * score_scale
    )
    scores = jnp.where(allowed, raw_scores, NEGATIVE)
    top_score = jnp.max(scores, axis=-1, keepdims=True)
    log_total = top_score + jnp.log(jnp.sum(jnp.exp(scores - top_score), axis=-1, keepdims=True))
    attn_probs = jnp.exp(scores - log_total)
    probs_low = attn_probs.astype(jnp.bfloat16)
    attended = jnp.einsum(
        "shqk,skhd->sqhd", probs_low, values_h, preferred_element_type=jnp.float32
    )
    attended = attended.reshape(-1, width).astype(jnp.bfloat16)
    residual = rows_f + matmul_rows(attended, w_out) + bias_out
    normed_mlp = layer_norm(residual, ln2_gain, ln2_bias).astype(jnp.bfloat16)
    up_proj = matmul_rows(normed_mlp, w_up) + bias_up
    hidden = gelu_tanh(up_proj).astype(jnp.bfloat16)
    block_out = residual + matmul_rows(hidden, w_down) + bias_down
    block_low = block_out.astype(jnp.bfloat16)
    projected = (matmul_rows(block_low, w_proj) + bias_proj).astype(jnp.bfloat16)
    row_index = jnp.arange(ROWS_SEQ, dtype=jnp.int32)
    pos_rows = patch_position.reshape(seq_count, ROWS_SEQ)
    live = slot_rows >= 0
    bucket_id = jnp.where(live, slot_rows * pos_count + pos_rows // quarter_len, -1)
    earlier = (bucket_id[:, :, None] == bucket_id[:, None, :]) & (
        row_index[None, :, None] > row_index[None, None, :]
    )
    rank_in = jnp.sum(earlier.astype(jnp.int32), axis=2)
    target = jnp.where(live, bucket_id * CAP + rank_in, -1)
    slot_index = jnp.arange(IMG_SEQ * pos_count * CAP, dtype=jnp.int32)
    selected = slot_index[None, :, None] == target[:, None, :]
    select_low = selected.astype(jnp.bfloat16)
    outgoing = jnp.einsum(
        "sjr,src->sjc",
        select_low,
        projected.reshape(seq_count, ROWS_SEQ, out_width),
        preferred_element_type=jnp.float32,
    ).astype(jnp.bfloat16)
    outgoing = outgoing.reshape(seq_count * IMG_SEQ, pos_count, CAP, out_width)
    slot_place = (
        jnp.sum(jnp.where(selected, (pos_rows % quarter_len + 1)[:, None, :], 0), axis=2) - 1
    )
    slot_place = slot_place.reshape(seq_count * IMG_SEQ, pos_count, CAP)
    arrived, arrived_place = (
        lax.all_to_all(outgoing, "pos", split_axis=1, concat_axis=0, tiled=True),
        lax.all_to_all(slot_place, "pos", split_axis=1, concat_axis=0, tiled=True),
    )
    arrived = arrived[:, 0]
    arrived_place = arrived_place[:, 0]
    placing = jnp.arange(quarter_len, dtype=jnp.int32)[None, :, None] == arrived_place[:, None, :]
    placing_low = placing.astype(jnp.bfloat16)
    visible = jnp.any(placing, axis=2)
    filled = jnp.einsum("gqj,gjc->gqc", placing_low, arrived, preferred_element_type=jnp.float32)
    decoder_input = jnp.where(
        visible[:, :, None], filled, mask_token.astype(jnp.float32)[None, None, :]
    )
    decoder_input = decoder_input.astype(jnp.bfloat16)
    grad_mask = jnp.sum(
        jnp.where(visible[:, :, None], 0.0, cotangent.astype(jnp.float32)), axis=(0, 1)
    )
    back_slots = jnp.einsum(
        "gqj,gqc->gjc", placing_low, cotangent, preferred_element_type=jnp.float32
    ).astype(jnp.bfloat16)
    returned = lax.all_to_all(back_slots[:, None], "pos", split_axis=0, concat_axis=1, tiled=True)
    delta_proj = (
        jnp.einsum(
            "sjr,sjc->src",
            select_low,
            returned.reshape(seq_count, -1, out_width),
            preferred_element_type=jnp.float32,
        )
        .reshape(-1, out_width)
        .astype(jnp.bfloat16)
    )
    grad_proj = jnp.einsum("rd,rc->dc", block_low, delta_proj, preferred_element_type=jnp.float32)
    grad_bproj = column_sums(delta_proj)
    delta_block = jnp.einsum("rc,dc->rd", delta_proj, w_proj, preferred_element_type=jnp.float32)
    delta_down = delta_block.astype(jnp.bfloat16)
    grad_down = jnp.einsum("rf,rd->fd", hidden, delta_down, preferred_element_type=jnp.float32)
    grad_bdown = column_sums(delta_down)
    delta_hidden = jnp.einsum("rd,fd->rf", delta_down, w_down, preferred_element_type=jnp.float32)
    gelu_back = jax.vjp(gelu_tanh, up_proj)[1]
    delta_up = gelu_back(delta_hidden)[0].astype(jnp.bfloat16)
    grad_up = jnp.einsum("rd,rf->df", normed_mlp, delta_up, preferred_element_type=jnp.float32)
    grad_bup = column_sums(delta_up)
    delta_normed = jnp.einsum("rf,df->rd", delta_up, w_up, preferred_element_type=jnp.float32)
    norm_back = jax.vjp(layer_norm, residual, ln2_gain, ln2_bias)[1]
    delta_resid_norm, grad_gain_two, grad_shift_two = norm_back(delta_normed)
    delta_residual = delta_block + delta_resid_norm
    mlp_mats = reduce_matrices((grad_proj, grad_down, grad_up))
    mlp_vecs = reduce_vectors(
        (grad_bproj, grad_bdown, grad_bup, grad_gain_two, grad_shift_two, grad_mask)
    )
    delta_branch = delta_residual.astype(jnp.bfloat16)
    grad_out = jnp.einsum("re,rd->ed", attended, delta_branch, preferred_element_type=jnp.float32)
    grad_bout = column_sums(delta_branch)
    delta_attended = jnp.einsum(
        "rd,ed->re", delta_branch, w_out, preferred_element_type=jnp.float32
    )
    delta_attended = delta_attended.astype(jnp.bfloat16).reshape(head_shape)
    delta_values = jnp.einsum(
        "shqk,sqhd->skhd", probs_low, delta_attended, preferred_element_type=jnp.float32
    ).astype(jnp.bfloat16)
    delta_probs = jnp.einsum(
        "sqhd,skhd->shqk", delta_attended, values_h, preferred_element_type=jnp.float32
    )
    delta_scores = attn_probs * (
        delta_probs - jnp.sum(delta_probs * attn_probs, axis=-1, keepdims=True)
    )
    delta_scores = delta_scores.astype(jnp.bfloat16)
    delta_queries = (
        (
            jnp.einsum("shqk,skhd->sqhd", delta_scores, keys_h, preferred_element_type=jnp.float32)
            * score_scale
        )
        .astype(jnp.bfloat16)
        .reshape(-1, width)
    )
    delta_keys = (
        (
            jnp.einsum("shqk,sqhd->skhd", delta_scores, queries, preferred_element_type=jnp.float32)
            * score_scale
        )
        .astype(jnp.bfloat16)
        .reshape(-1, width)
    )
    delta_values = delta_values.reshape(-1, width)
    delta_qkv = jnp.concatenate([delta_queries, delta_keys, delta_values], axis=1)
    grad_qkv = jnp.einsum("rd,re->de", normed_low, delta_qkv, preferred_element_type=jnp.float32)
    grad_bquery = column_sums(delta_queries)
    grad_bvalue = column_sums(delta_values)
    delta_first = jnp.einsum("re,de->rd", delta_qkv, w_qkv, preferred_element_type=jnp.float32)
    first_back = jax.vjp(layer_norm, rows_f, ln1_gain, ln1_bias)[1]
    delta_rows, grad_gain_one, grad_shift_one = first_back(delta_first)
    grad_tokens = (delta_residual + delta_rows).astype(jnp.bfloat16)
    attn_mats = reduce_matrices((grad_qkv, grad_out))
    attn_vecs = reduce_vectors((grad_bquery, grad_bvalue, grad_bout, grad_gain_one, grad_shift_one))
    return (
        decoder_input,
        grad_tokens,
        attn_vecs[3],
        attn_vecs[4],
        attn_mats[0],
        attn_vecs[0],
        attn_vecs[1],
        attn_mats[1],
        attn_vecs[2],
        mlp_vecs[3],
        mlp_vecs[4],
        mlp_mats[2],
        mlp_vecs[2],
        mlp_mats[1],
        mlp_vecs[1],
        mlp_mats[0],
        mlp_vecs[0],
        mlp_vecs[5],
    )


MESH_ID = pl.DeviceIdType.MESH
LOW = jnp.bfloat16
FULL = jnp.float32

AXES = ("zh", "zl", "x", "y")
MATRICES = ("down", "up", "proj", "out", "qkv")
JOBS = {
    "down0": ("down", None, 0, 256, ("zl", "y", "zh")),
    "down1": ("down", None, 256, 256, ("y", "zl", "zh")),
    "down2": ("down", None, 512, 256, ("zl", "zh", "y")),
    "up0a": ("up", 0, 0, 256, ("y", "zl", "zh", "x")),
    "up0b": ("up", 0, 256, 128, ("zl", "x", "zh", "y")),
    "up1a": ("up", 1, 0, 384, ("x", "y", "zl", "zh")),
    "up2a": ("up", 2, 0, 384, ("zl", "y", "zh", "x")),
    "up3a": ("up", 3, 0, 384, ("y", "zl", "zh", "x")),
    "proj0": ("proj", None, 0, 256, ("zl", "y", "x", "zh")),
    "out0": ("out", None, 0, 384, ("x", "y", "zl", "zh")),
    "qkv0": ("qkv", None, 0, 256, ("y", "x", "zl", "zh")),
    "qkv1": ("qkv", None, 256, 256, ("y", "zl", "zh", "x")),
    "qkv2": ("qkv", None, 512, 256, ("x", "y", "zl", "zh")),
    "qkv3": ("qkv", None, 768, 256, ("x", "y", "zl", "zh")),
    "qkv4": ("qkv", None, 1024, 128, ("x", "y", "zl", "zh")),
}
PLAN = (
    ("do", "feed0"),
    ("do", "feed1"),
    ("do", "feed2"),
    ("do", "feed3"),
    ("do", "project"),
    ("do", "delta_rows"),
    ("do", "delta"),
    ("do", "feed_back0"),
    ("do", "feed_back1"),
    ("do", "swapped_proj_left"),
    ("do", "swapped_proj_right"),
    ("do", "multiply_proj0"),
    ("do", "feed_back2"),
    ("do", "multiply_up0"),
    ("do", "feed_back3"),
    ("do", "second_back"),
    ("do", "attended_back"),
    ("do", "attend_back0"),
    ("do", "multiply_up1"),
    ("do", "multiply_up3"),
    ("do", "multiply_up2"),
    ("do", "transposes"),
    ("proj0", 0, ""),
    ("do", "attend_back1"),
    ("do", "attend_back2"),
    ("up0a", 0, ""),
    ("do", "attend_back3"),
    ("up0b", 0, ""),
    ("do", "attend_back4"),
    ("do", "attend_back5"),
    ("do", "delta_first"),
    ("do", "pass_delta"),
    ("do", "decode"),
    ("do", "swapped_out_left"),
    ("do", "swapped_out_right"),
    ("do", "multiply_out0"),
    ("do", "multiply_down0"),
    ("do", "multiply_down1"),
    ("up3a", 0, ""),
    ("do", "swapped_qkv_left"),
    ("do", "swapped_qkv_right"),
    ("do", "multiply_qkv0"),
    ("do", "multiply_qkv1"),
    ("do", "multiply_qkv2"),
    ("do", "multiply_qkv3"),
    ("do", "multiply_qkv4"),
    ("up2a", 0, ""),
    ("proj0", 1, ""),
    ("do", "first_back"),
    ("up0a", 1, ""),
    ("down1", 0, "a"),
    ("down0", 0, "a"),
    ("vec", 0),
    ("do", "multiply_down2"),
    ("do", "multiply_down3"),
    ("down2", 0, "a"),
    ("qkv0", 0, ""),
    ("up3a", 1, ""),
    ("up1a", 0, ""),
    ("up0b", 1, ""),
    ("qkv1", 0, ""),
    ("up0a", 2, ""),
    ("down0", 0, "b"),
    ("down2", 0, "b"),
    ("up2a", 1, ""),
    ("down1", 0, "b"),
    ("out0", 0, ""),
    ("up3a", 2, ""),
    ("qkv1", 1, ""),
    ("up0b", 2, ""),
    ("up1a", 1, ""),
    ("qkv2", 0, ""),
    ("down0", 1, ""),
    ("down2", 1, ""),
    ("down1", 1, ""),
    ("out0", 1, ""),
    ("up0b", 3, ""),
    ("qkv3", 0, ""),
    ("up2a", 2, ""),
    ("up1a", 2, ""),
    ("qkv2", 1, ""),
    ("qkv4", 0, ""),
    ("down2", 2, ""),
    ("qkv1", 2, ""),
    ("up0b", 4, ""),
    ("proj0", 2, ""),
    ("vec", 1),
    ("out0", 2, ""),
    ("up0b", 5, ""),
    ("down0", 2, ""),
    ("qkv3", 1, ""),
    ("qkv0", 1, ""),
    ("qkv4", 1, ""),
    ("qkv2", 2, ""),
    ("up0a", 3, ""),
    ("down1", 2, ""),
    ("down2", 4, ""),
    ("up3a", 3, ""),
    ("vec", 2),
    ("up2a", 3, ""),
    ("qkv1", 3, ""),
    ("up1a", 3, ""),
    ("qkv3", 2, ""),
    ("down0", 4, ""),
    ("down2", 5, ""),
    ("up0a", 4, ""),
    ("proj0", 3, ""),
    ("qkv0", 2, ""),
    ("qkv4", 2, ""),
    ("down1", 4, ""),
    ("down0", 5, ""),
    ("up0a", 5, ""),
    ("up3a", 4, ""),
    ("out0", 3, ""),
    ("vec", 3),
    ("up2a", 4, ""),
    ("down1", 5, ""),
    ("qkv2", 3, ""),
    ("qkv1", 4, ""),
    ("up3a", 5, ""),
    ("up1a", 4, ""),
    ("qkv3", 3, ""),
    ("up2a", 5, ""),
    ("proj0", 4, ""),
    ("qkv1", 5, ""),
    ("qkv0", 3, ""),
    ("out0", 4, ""),
    ("up1a", 5, ""),
    ("qkv4", 3, ""),
    ("qkv2", 4, ""),
    ("proj0", 5, ""),
    ("qkv3", 4, ""),
    ("vec", 4),
    ("out0", 5, ""),
    ("qkv2", 5, ""),
    ("qkv0", 4, ""),
    ("qkv4", 4, ""),
    ("qkv3", 5, ""),
    ("vec", 5),
    ("qkv0", 5, ""),
    ("qkv0", 6, ""),
    ("qkv4", 5, ""),
    ("qkv4", 6, ""),
)
DIRECT = ("qkv0", "qkv4",)
VEC_STEPS = ("core", "x", "y", "zl", "zh", "core")
PEERS = ("diagonal", "y", "core")
PLACES = 64
INPUTS = (
    "slot", "position", "ln1_gain", "ln1_bias", "tokens", "w_qkv", "cotangent", "bias_query", "bias_value", "w_out",
    "bias_out", "ln2_gain", "ln2_bias", "bias_up", "w_up", "w_down", "bias_down", "w_proj", "bias_proj", "mask_token",
)
LN1_GAIN, LN1_BIAS, BIAS_Q, BIAS_V, BIAS_OUT, LN2_GAIN, LN2_BIAS, BIAS_DOWN, BIAS_UP, BIAS_PROJ, MASK = (
    0, 1, 2, 3, 4, 5, 6, 7, 8, 12, 13,
)


def axes_of(matrix):
    return ("zh", "zl", "y") if matrix == "down" else AXES


def device_coords():
    img = lax.axis_index("img")
    pos = lax.axis_index("pos")
    return {"zh": img // 4, "zl": (img // 2) % 2, "x": img % 2, "y": pos // 2, "core": pos % 2}


def device_of(where):
    return (where["zh"] * 4 + where["zl"] * 2 + where["x"], where["y"] * 2 + where["core"])


def block_rows(name):
    return 96 if name == "down" else 48


def dot(left, right):
    return jnp.dot(left, right, preferred_element_type=FULL)


def dot_nt(left, right):
    return lax.dot_general(left, right, (((1,), (1,)), ((), ())), preferred_element_type=FULL)


def dot_tn(left, right):
    return lax.dot_general(left, right, (((0,), (0,)), ((), ())), preferred_element_type=FULL)


def normalised(values):
    centred = values - jnp.mean(values, axis=-1, keepdims=True)
    rstd = lax.rsqrt(jnp.mean(centred * centred, axis=-1, keepdims=True) + EPSILON)
    return centred * rstd, rstd


def norm_rows_back(delta, values, gain):
    xhat, rstd = normalised(values)
    scaled = delta * gain
    rows = rstd * (
        scaled
        - jnp.mean(scaled, axis=-1, keepdims=True)
        - xhat * jnp.mean(scaled * xhat, axis=-1, keepdims=True)
    )
    return rows, delta * xhat


def layer_kernel(names, *refs):
    ref = dict(zip(names, refs))

    def row_of(name, columns=slice(None)):
        return ref[name + "_held"][...].reshape(1, -1)[:, columns]

    me = device_coords()
    core = me["core"]
    my_pos = me["y"] * 2 + core
    width = ref["tokens_held"].shape[1]
    ff = ref["w_up"].shape[1]
    quarter_len = POSITIONS // 4

    def peer(axis):
        if axis == "diagonal":
            return device_of({**me, "y": 1 - me["y"], "core": 1 - core})
        if axis == "across":
            return device_of({**me, "x": 1 - me["x"], "core": 1 - core})
        return device_of({**me, axis: 1 - me[axis]})

    leaving = {}

    def remote(source, target, kind, spot, axis, leave=None):
        leave = ref["small_send"].at[spot] if leave is None else leave
        return pltpu.make_async_remote_copy(
            src_ref=source,
            dst_ref=target,
            send_sem=leave,
            recv_sem=ref[kind + "_recv"].at[spot],
            device_id=peer(axis),
            device_id_type=MESH_ID,
        )

    def begin(copy, use):
        if use in leaving:
            leaving.pop(use).wait_send()
        copy.start()
        leaving[use] = copy

    barrier = pltpu.get_barrier_semaphore()
    for axis in AXES + ("core", "diagonal", "across"):
        pl.semaphore_signal(barrier, inc=1, device_id=peer(axis), device_id_type=MESH_ID)

    loads = {}
    for number, name in enumerate(INPUTS):
        loads[name] = pltpu.make_async_copy(ref[name], ref[name + "_held"], ref["load"].at[number])
        loads[name].start()

    def loaded(*which):
        for name in which:
            loads[name].wait()

    loaded("slot", "position", "tokens", "ln1_gain", "ln1_bias")
    ref["places"][my_pos, 0:1, :] = row_of("slot")
    ref["places"][my_pos, 1:2, :] = row_of("position")

    def first_norm(step, carry):
        rows = pl.ds(pl.multiple_of(step * 64, 64), 64)
        xhat, _ = normalised(ref["tokens_held"][rows, :].astype(FULL))
        ref["normed"][rows, :] = (xhat * row_of("ln1_gain") + row_of("ln1_bias")).astype(LOW)
        return carry

    lax.fori_loop(0, 4, first_norm, 0, unroll=4)

    loaded("w_qkv", "bias_query", "bias_value")
    third = width // 256
    for number in range(3 * third):
        columns = slice(number * 256, (number + 1) * 256)
        if number == 6:
            pl.semaphore_wait(barrier, 7)
            for spot, axis in enumerate(PEERS):
                begin(remote(ref["places"].at[my_pos], ref["places"].at[my_pos], "place", spot, axis), spot)
        part = dot(ref["normed"][...], ref["w_qkv_held"][:, columns])
        if number < third:
            part = part + row_of("bias_query", columns)
            part = part.astype(LOW) * LOW(HEAD_DIM ** (-0.5))
        elif number >= 2 * third:
            part = part + row_of("bias_value", slice((number - 2 * third) * 256, (number - 2 * third + 1) * 256))
        ref["qkv"][:, columns] = part.astype(LOW)
    ref["normed_one"][...] = ref["normed"][...]

    row_ids = lax.broadcasted_iota(jnp.int32, (ROWS_SEQ, ROWS_SEQ), 0)
    lane_ids = lax.broadcasted_iota(jnp.int32, (ROWS_SEQ, ROWS_SEQ), 1)
    earlier = (row_ids < lane_ids).astype(FULL).astype(LOW)

    def one_hot(count, row):
        ids = lax.broadcasted_iota(jnp.int32, (count, ROWS_SEQ), 0)
        return jnp.where(ids == row, 1.0, 0.0)

    def picked(slot, position, quarter):
        offset = position - quarter * quarter_len
        inside = (slot >= 0) & (offset >= 0) & (offset < quarter_len)
        kinds = one_hot(8, jnp.where(inside, slot, -1))
        ranks = jnp.sum(kinds * dot(kinds.astype(LOW), earlier), axis=0, keepdims=True).astype(jnp.int32)
        chosen = one_hot(IMG_SEQ * CAP, jnp.where(inside, slot * CAP + ranks, -1))
        return chosen.astype(LOW), jnp.where(inside, slot * PLACES + offset, -1)

    for quarter in range(4):
        chosen, _ = picked(row_of("slot"), row_of("position"), quarter)
        ref["chosen"][quarter] = chosen

    slots = one_hot(8, row_of("slot") + 1).astype(LOW)
    ref["allowed"][...] = jnp.where(dot_tn(slots, slots) > 0.5, 0.0, NEGATIVE)

    lane = lax.broadcasted_iota(jnp.int32, (1, 2 * HEAD_DIM), 1)
    sides_full = [(lane < HEAD_DIM).astype(FULL), (lane >= HEAD_DIM).astype(FULL)]
    sides = [side.astype(LOW) for side in sides_full]

    def head_columns(pair, first):
        return pl.ds(first + pair * 2 * HEAD_DIM, 2 * HEAD_DIM)

    def attend(pair, carry):
        queries = ref["qkv"][:, head_columns(pair, 0)]
        keys = ref["qkv"][:, head_columns(pair, width)]
        values = ref["qkv"][:, head_columns(pair, 2 * width)]
        total = None
        for side in range(2):
            scores = dot_nt(queries * sides[side], keys) + ref["allowed"][...]
            powers = jnp.exp(scores - jnp.max(scores, axis=-1, keepdims=True))
            probs = powers / jnp.sum(powers, axis=-1, keepdims=True)
            ref["probs"][pair * 2 + side] = probs
            part = dot(probs.astype(LOW), values) * sides_full[side]
            total = part if total is None else total + part
        ref["attended"][:, head_columns(pair, 0)] = total.astype(LOW)
        return carry

    for pair in range(HEADS // 2):
        attend(pair, 0)

    ref["cot_wide"][...] = jnp.zeros_like(ref["cot_wide"])
    loaded("cotangent")
    for image in range(4 * IMG_SEQ):
        ref["cot_wide"][image, 0:quarter_len, :] = ref["cotangent_held"][image]
    for number, axis in enumerate(PEERS):
        source = peer(axis)[1]
        remote(ref["places"].at[source], ref["places"].at[source], "place", number, axis).wait_recv()
    for number, axis in enumerate(PEERS + ("self",)):
        source = my_pos if axis == "self" else peer(axis)[1]
        slot = ref["places"][source, 0:1, :]
        position = ref["places"][source, 1:2, :]
        chosen, place = picked(slot, position, my_pos)
        filled = one_hot(IMG_SEQ * PLACES, place).astype(LOW)
        placing = dot_nt(filled, chosen).astype(LOW)
        ref["placing"][number] = placing
        cot = ref["cot_wide"][pl.ds(source * IMG_SEQ, IMG_SEQ)].reshape(IMG_SEQ * PLACES, -1)
        back = dot_tn(placing, cot).astype(LOW)
        if axis == "self":
            ref["back_in"][my_pos] = back
        else:
            ref["back_out"][number] = back
    for number, axis in enumerate(PEERS):
        begin(remote(ref["back_out"].at[number], ref["back_in"].at[my_pos], "back", number, axis), number)
    ref["vec_own"][...] = jnp.zeros_like(ref["vec_own"])

    loaded("w_out", "bias_out")
    for number in range(third):
        columns = slice(number * 256, (number + 1) * 256)
        ref["residual"][:, columns] = (
            ref["tokens_held"][:, columns].astype(FULL)
            + dot(ref["attended"][...], ref["w_out_held"][:, columns])
            + row_of("bias_out", columns)
        )

    def second_norm(step, carry):
        rows = pl.ds(pl.multiple_of(step * 64, 64), 64)
        xhat, _ = normalised(ref["residual"][rows, :])
        ref["normed"][rows, :] = (xhat * row_of("ln2_gain") + row_of("ln2_bias")).astype(LOW)
        return carry

    loaded("ln2_gain", "ln2_bias")
    lax.fori_loop(0, 4, second_norm, 0, unroll=4)
    ref["left_up"][...] = ref["normed"][...].T

    def delta_rows():
        for number, axis in enumerate(PEERS):
            remote(ref["back_out"].at[number], ref["back_in"].at[my_pos], "back", number, axis).wait_recv()
        chosen_all = ref["chosen"][...].reshape(4 * IMG_SEQ * CAP, ROWS_SEQ)
        returned = ref["back_in"][...].reshape(4 * IMG_SEQ * CAP, -1)
        delta_proj = dot_tn(chosen_all, returned)
        ref["vec_own"][BIAS_PROJ : BIAS_PROJ + 1, : delta_proj.shape[1]] = jnp.sum(delta_proj, axis=0, keepdims=True)
        ref["right_proj"][...] = delta_proj.astype(LOW)
        swap("proj_right")

    def delta():
        for number in range(third):
            columns = slice(number * 256, (number + 1) * 256)
            part = dot_nt(ref["right_proj"][...], ref["w_proj_held"][columns, :])
            ref["delta_block"][:, columns] = part
            part = part.astype(LOW)
            ref["right_down"][:, columns] = part
            ref["vec_own"][BIAS_DOWN : BIAS_DOWN + 1, columns] = jnp.sum(part.astype(FULL), axis=0, keepdims=True)
        for which in ("delta_side", "delta_across", "side2", "across2", "side3", "across3", "delta"):
            swap(which)

    def pass_delta():
        for which, later in (("delta_side", "on_side"), ("delta_across", "on_across")):
            swapped(which)
            swap(later)

    loaded("w_up", "bias_up")
    ref["bias_up_row"][...] = row_of("bias_up")

    def chunk_columns(slot, start=0, wide=width):
        if isinstance(start, int):
            return pl.ds(slot * width + start, wide)
        return pl.ds(pl.multiple_of(slot * width + start, 128), wide)

    def feed(slot):
        columns = chunk_columns(slot)
        up = dot(ref["normed"][...], ref["w_up_held"][:, columns]) + ref["bias_up_row"][:, columns]
        square = up * up
        bent = jnp.tanh(GELU_COEF * (up + 0.044715 * up * square))
        half = 0.5 * (1.0 + bent)
        ref["slope"][slot] = half + 0.5 * up * (1.0 - bent * bent) * (GELU_COEF * (1.0 + 0.134145 * square))
        hidden = (up * half).astype(LOW)
        ref["left_down"][columns, :] = hidden.T
        swap("hidden%d" % slot)
        if slot < 2:
            swap("side%d" % slot)
            swap("across%d" % slot)
        if slot == 0:
            loaded("w_down", "bias_down")
        out = dot(hidden, ref["w_down_held"][columns, :])
        if slot == 0:
            ref["mlp_out"][...] = out
        else:
            ref["mlp_out"][...] += out

    def feed_back(slot):
        columns = chunk_columns(slot)
        back = dot_nt(ref["right_down"][...], ref["w_down_held"][columns, :])
        delta_up = (back * ref["slope"][slot]).astype(LOW)
        ref["right_up"][:, columns] = delta_up
        swap("feed%d" % slot)
        ref["bias_up_sum"][:, columns] = jnp.sum(delta_up.astype(FULL), axis=0, keepdims=True)
        delta = dot_nt(delta_up, ref["w_up_held"][:, columns])
        if slot == 0:
            ref["delta_normed"][...] = delta
        else:
            ref["delta_normed"][...] += delta

    swaps = ("norm", "delta", "proj_left", "proj_right", "out_left", "out_right", "qkv_left", "qkv_right")
    swaps += tuple("hidden%d" % slot for slot in range(4)) + tuple("feed%d" % slot for slot in range(4))
    swaps += tuple("side%d" % slot for slot in range(4)) + tuple("across%d" % slot for slot in range(4))
    swaps += ("delta_side", "delta_across", "on_side", "on_across")

    def swap_copy(which):
        other = 1 - core
        axis = "core"
        half = width // 2
        if which == "norm":
            source, target = ref["left_up"], ref["left_in_up"]
        elif which == "delta":
            source, target = ref["right_down"], ref["right_in_down"].at[0]
        elif which == "delta_side":
            source, target = ref["right_down"].at[:, pl.ds(0, half)], ref["right_in_down"].at[1, :, pl.ds(0, half)]
            axis = "x"
        elif which == "delta_across":
            source, target = ref["right_down"].at[:, pl.ds(half, half)], ref["right_in_down"].at[2, :, pl.ds(half, half)]
            axis = "across"
        elif which == "on_side":
            source = ref["right_in_down"].at[1, :, pl.ds(0, half)]
            target = ref["right_in_down"].at[2, :, pl.ds(0, half)]
        elif which == "on_across":
            source = ref["right_in_down"].at[2, :, pl.ds(half, half)]
            target = ref["right_in_down"].at[1, :, pl.ds(half, half)]
        elif which[:-1] in ("hidden", "side", "across"):
            chunk = int(which[-1])
            blocks = ref["left_down"].reshape(8, 2, 192, ROWS_SEQ)
            if which.startswith("hidden"):
                source, target = blocks.at[chunk * 2 + me["x"], other], ref["left_in_down"].at[0, chunk]
            elif which.startswith("side"):
                source, target = blocks.at[chunk * 2 + 1 - me["x"], core], ref["left_in_down"].at[1, chunk]
                axis = "x"
            else:
                source, target = blocks.at[chunk * 2 + 1 - me["x"], other], ref["left_in_down"].at[2, chunk]
                axis = "across"
        elif which.startswith("feed"):
            slot = int(which[4:])
            source = ref["right_up"].at[:, chunk_columns(slot, other * half, half)]
            target = ref["right_in_up"].at[slot]
        else:
            matrix, side = which.split("_")
            if side == "left":
                source, target = ref["left_" + matrix], ref["left_in_" + matrix]
            else:
                wide = ref["right_" + matrix].shape[1] // 2
                source = ref["right_" + matrix].at[:, pl.ds(pl.multiple_of(other * wide, 128), wide)]
                target = ref["right_in_" + matrix]
        leave = swap_leave[which] if which in swap_leave else 0
        return remote(source, target, "core", swaps.index(which), axis, ref["core_send"].at[leave])

    swap_leave = {}

    def swap(which):
        far = which[:-1] in ("side", "across") or which.startswith("delta_")
        many = sum(spot < 6 if not far else spot >= 6 for spot in swap_leave.values())
        swap_leave[which] = 6 + many if far else many % 6
        begin(swap_copy(which), ("core", swap_leave[which]))

    def swapped(which):
        swap_copy(which).wait_recv()

    job_names = tuple(JOBS)

    def job_final(job):
        matrix, slot, first, wide, _ = JOBS[job]
        final = ref["final_" + matrix]
        if slot is not None:
            final = final.at[slot]
        return final, pl.ds(first, wide)

    def job_index(job, stage, part, mine):
        dims = JOBS[job][4]
        pick, land = [], []
        for axis in axes_of(JOBS[job][0]):
            if axis in dims[:stage]:
                pick.append(me[axis])
            elif axis == dims[stage]:
                pick.append(me[axis] if mine else 1 - me[axis])
            elif axis == "zh" and part:
                pick.append("ab".index(part))
                land.append(pick[-1])
            else:
                pick.append(slice(None))
                land.append(slice(None))
        return tuple(pick), tuple(land)

    def job_send_spot(job, stage, part):
        spot = job_names.index(job)
        if stage == 6:
            return job
        return 2 * len(job_names) + spot if part == "b" else 2 * spot + stage % 2

    def job_copy(job, stage, part):
        dims = JOBS[job][4]
        spot = stage if part != "b" else 3
        send_sem = ref["job_send"].at[job_send_spot(job, min(stage, 5), part)]
        recv_sem = ref["job_recv"].at[job_names.index(job), min(spot, 5)]
        if stage < 4:
            pick, land = job_index(job, stage, part, False)
            source = ref["partial_" + job].at[pick]
            place = ref["landed_%s_%d" % (job, stage)]
            place = place.at[land] if land else place
            axis = dims[stage]
        else:
            final, columns = job_final(job)
            if stage == 4 or job in DIRECT:
                source = place = final.at[core, me["y"], :, columns]
            else:
                source = place = final.at[core, :, :, columns]
            axis = ("y", "core", "diagonal")[stage - 4]
        if stage == 6:
            send_sem = ref["direct_send"].at[DIRECT.index(job)]
            recv_sem = ref["direct_recv"].at[DIRECT.index(job)]
        return pltpu.make_async_remote_copy(
            src_ref=source,
            dst_ref=place,
            send_sem=send_sem,
            recv_sem=recv_sem,
            device_id=peer(axis),
            device_id_type=MESH_ID,
        )

    def first_parts(job):
        return ("a", "b") if JOBS[job][0] == "down" else ("",)

    def needs(job, stage):
        dims = JOBS[job][4]
        firsts = tuple((0, part) for part in first_parts(job))
        if stage == 1:
            return firsts
        if stage == 2:
            return ((1, ""),) + firsts
        if stage == 4 or job in DIRECT and stage > 4:
            return ((len(dims) - 1, ""),) + firsts
        return ((stage - 1, ""),)

    arrived, sent = set(), set()

    def send(job, stage, part=""):
        sent.add((job, stage, part))
        begin(job_copy(job, stage, part), ("job", job_send_spot(job, stage, part)))

    def arrive(job, stage, part):
        matrix, slot, _, _, dims = JOBS[job]
        axes = axes_of(matrix)
        last = len(dims) - 1
        job_copy(job, stage, part).wait_recv()
        if stage < 4:
            partial, landed = ref["partial_" + job], ref["landed_%s_%d" % (job, stage)]
            pick, land = job_index(job, stage, part, True)
            free = [spot for spot, index in enumerate(pick) if isinstance(index, slice)]
            for code in range(2 ** len(free)):
                here, there = list(pick), list(land)
                for order, spot in enumerate(free):
                    bit = (code >> (len(free) - 1 - order)) % 2
                    here[spot] = bit
                    there[[place for place, axis in enumerate(axes) if axis not in dims[: stage + 1]].index(spot)] = bit
                sums = partial[tuple(here)] + (landed[tuple(there)] if there else landed[...])
                if stage < last:
                    partial[tuple(here)] = sums
                else:
                    final, columns = job_final(job)
                    final[core, me["y"], :, columns] = sums
        arrived.add((job, stage, part))
        for later in list(range(1, last + 1)) + ([4, 6, 5] if job in DIRECT else [4, 5]):
            ready = all((job,) + need in arrived for need in needs(job, later))
            if (job, later, "") not in sent and ready:
                send(job, later)
        ends = (4, 5, 6) if job in DIRECT else (5,)
        if stage in ends and all((job, end, "") in arrived for end in ends):
            final, columns = job_final(job)
            _, _, first, wide, _ = JOBS[job]
            out = ref["grad_" + matrix]
            for side in range(2):
                if matrix == "down":
                    out[side, :, :, columns] = final[side, :, :, columns]
                else:
                    start = side * ref["final_" + matrix].shape[-1] + first
                    place = pl.ds(start, wide) if slot is None else chunk_columns(slot, start, wide)
                    out[:, :, place] = final[side, :, :, columns]

    def multiply_down(slot):
        if slot == 0:
            for which in ("delta", "on_side", "on_across"):
                swapped(which)
        for which in ("hidden", "side", "across"):
            swapped(which + str(slot))
        rows = pl.ds(pl.multiple_of((slot * 2 + me["x"]) * 384 + core * 192, 192), 192)
        total = dot(ref["left_down"][rows, :], ref["right_down"][...])
        for number in range(3):
            total = total + dot(ref["left_in_down"][number, slot], ref["right_in_down"][number])
        total = total.astype(LOW)
        for job, (matrix, _, first, wide, _) in JOBS.items():
            if matrix == "down":
                for half in range(2):
                    ref["partial_" + job][slot // 2, slot % 2, half] = total[half * 96 : (half + 1) * 96, first : first + wide]
        if slot % 2 == 1:
            for job in JOBS:
                if JOBS[job][0] == "down":
                    send(job, 0, "ab"[slot // 2])

    def multiply_up(slot):
        if slot == 0:
            swapped("norm")
        swapped("feed%d" % slot)
        for block in range(2):
            rows = slice(block * 384, (block + 1) * 384)
            total = dot(
                ref["left_up"][rows, :], ref["right_up"][:, chunk_columns(slot, core * (width // 2), width // 2)]
            ) + dot(ref["left_in_up"][rows, :], ref["right_in_up"][slot])
            total = total.astype(LOW)
            for job, (matrix, own, first, wide, _) in JOBS.items():
                if matrix == "up" and own == slot:
                    for part in range(8):
                        ref["partial_" + job][block, part // 4, (part // 2) % 2, part % 2] = total[
                            part * 48 : (part + 1) * 48, first : first + wide
                        ]
        for job, (matrix, own, _, _, _) in JOBS.items():
            if matrix == "up" and own == slot:
                send(job, 0)

    def multiply(job):
        matrix, _, first, wide, _ = JOBS[job]
        wide_half = ref["right_" + matrix].shape[1] // 2
        columns = pl.ds(pl.multiple_of(core * wide_half + first, 128), wide)
        for block in range(2):
            rows = slice(block * 384, (block + 1) * 384)
            total = dot(ref["left_" + matrix][rows, :], ref["right_" + matrix][:, columns]) + dot(
                ref["left_in_" + matrix][rows, :], ref["right_in_" + matrix][:, first : first + wide]
            )
            total = total.astype(LOW)
            for part in range(8):
                ref["partial_" + job][block, part // 4, (part // 2) % 2, part % 2] = total[part * 48 : (part + 1) * 48]
        send(job, 0)

    def vec_rows(side):
        return pl.ds(pl.multiple_of(side * 8, 8), 8)

    def vec_copy(stage):
        source = ref["vec_own"].at[vec_rows(1 - core)] if stage == 0 else ref["vec_held"].at[stage]
        return remote(source, ref["vec_in"].at[stage], "vec", stage, VEC_STEPS[stage], ref["vec_send"].at[0])

    def arrive_vec(stage):
        vec_copy(stage).wait_recv()
        if stage == 5:
            ref["vec_sums"][vec_rows(1 - core), :] = ref["vec_in"][5]
            return
        own = ref["vec_own"][vec_rows(core), :] if stage == 0 else ref["vec_held"][stage]
        ref["vec_held"][stage + 1] = own + ref["vec_in"][stage]
        begin(vec_copy(stage + 1), "vec")
        if stage == 4:
            ref["vec_sums"][vec_rows(core), :] = ref["vec_held"][5]

    swap("norm")

    def project():
        for number in range(third):
            columns = slice(number * 256, (number + 1) * 256)
            ref["block_low"][:, columns] = (
                ref["residual"][:, columns] + ref["mlp_out"][:, columns] + row_of("bias_down", columns)
            ).astype(LOW)
        ref["left_proj"][...] = ref["block_low"][...].T
        swap("proj_left")
        loaded("w_proj", "bias_proj")
        projected = (dot(ref["block_low"][...], ref["w_proj_held"][...]) + row_of("bias_proj")).astype(LOW)
        outgoing = dot(ref["chosen"][...].reshape(4 * IMG_SEQ * CAP, ROWS_SEQ), projected).astype(LOW)
        ref["grid_out"][...] = outgoing.reshape(4, IMG_SEQ * CAP, -1)
        for number, axis in enumerate(PEERS):
            begin(remote(ref["grid_out"].at[peer(axis)[1]], ref["grid_in"].at[number], "grid", number, axis), number)

    def second_back():
        sums = [jnp.zeros((1, width), FULL)] * 3
        for step in range(4):
            rows = slice(step * 64, (step + 1) * 64)
            delta = ref["delta_normed"][rows, :]
            row_term, gains = norm_rows_back(delta, ref["residual"][rows, :], row_of("ln2_gain"))
            total = ref["delta_block"][rows, :] + row_term
            low = total.astype(LOW)
            ref["delta_block"][rows, :] = total
            ref["right_out"][rows, :] = low
            news = (gains, delta, low.astype(FULL))
            sums = [old + jnp.sum(new, axis=0, keepdims=True) for old, new in zip(sums, news)]
        for spot, total in zip((LN2_GAIN, LN2_BIAS, BIAS_OUT), sums):
            ref["vec_own"][spot : spot + 1, :] = total
        swap("out_right")

    def attended_back():
        for number in range(third):
            columns = slice(number * 256, (number + 1) * 256)
            ref["delta_attended"][:, columns] = dot_nt(ref["right_out"][...], ref["w_out_held"][columns, :]).astype(LOW)

    def transposes():
        ref["left_out"][...] = ref["attended"][...].T
        swap("out_left")
        ref["left_qkv"][...] = ref["normed_one"][...].T
        swap("qkv_left")

    def attend_back(pair):
        queries = ref["qkv"][:, head_columns(pair, 0)]
        keys = ref["qkv"][:, head_columns(pair, width)]
        values = ref["qkv"][:, head_columns(pair, 2 * width)]
        delta = ref["delta_attended"][:, head_columns(pair, 0)]
        totals = [None, None, None]
        for side in range(2):
            probs = ref["probs"][pair * 2 + side]
            delta_probs = dot_nt(delta * sides[side], values)
            delta_scores = probs * (delta_probs - jnp.sum(delta_probs * probs, axis=-1, keepdims=True))
            delta_scores = delta_scores.astype(LOW)
            parts = (
                dot(delta_scores, keys) * (HEAD_DIM ** (-0.5)),
                dot_tn(delta_scores, queries),
                dot_tn(probs.astype(LOW), delta),
            )
            for spot, part in enumerate(parts):
                part = part * sides_full[side]
                totals[spot] = part if totals[spot] is None else totals[spot] + part
        for spot, total in enumerate(totals):
            ref["right_qkv"][:, head_columns(pair, spot * width)] = total.astype(LOW)
        if pair == HEADS // 2 - 1:
            swap("qkv_right")

    def delta_first():
        for number in range(third):
            columns = slice(number * 256, (number + 1) * 256)
            ref["delta_normed"][:, columns] = dot_nt(ref["right_qkv"][...], ref["w_qkv_held"][columns, :])
        for spot, first in ((BIAS_Q, 0), (BIAS_V, 2 * width)):
            ref["vec_own"][spot : spot + 1, :] = jnp.sum(
                ref["right_qkv"][:, first : first + width].astype(FULL), axis=0, keepdims=True
            )

    def first_back():
        sums = [jnp.zeros((1, width), FULL)] * 2
        for step in range(4):
            rows = slice(step * 64, (step + 1) * 64)
            delta = ref["delta_normed"][rows, :]
            row_term, gains = norm_rows_back(delta, ref["tokens_held"][rows, :].astype(FULL), row_of("ln1_gain"))
            ref["grad_tokens"][rows, :] = (ref["delta_block"][rows, :] + row_term).astype(LOW)
            sums = [old + jnp.sum(new, axis=0, keepdims=True) for old, new in zip(sums, (gains, delta))]
        for spot, total in zip((LN1_GAIN, LN1_BIAS), sums):
            ref["vec_own"][spot : spot + 1, :] = total
        for number in range(ff // width):
            ref["vec_own"][BIAS_UP + number : BIAS_UP + number + 1, :] = ref["bias_up_sum"][
                :, number * width : (number + 1) * width
            ]
        mask_sum = jnp.zeros((8, ref["cot_wide"].shape[2]), FULL)
        for number, axis in enumerate(PEERS + ("self",)):
            source = my_pos if axis == "self" else peer(axis)[1]
            cot = ref["cot_wide"][pl.ds(source * IMG_SEQ, IMG_SEQ)].reshape(IMG_SEQ * PLACES, -1)
            seen = dot_nt(jnp.ones((8, IMG_SEQ * CAP), LOW), ref["placing"][number])
            mask_sum = mask_sum + dot((1.0 - seen).astype(LOW), cot)
        ref["vec_own"][MASK : MASK + 1, : mask_sum.shape[1]] = mask_sum[0:1]
        begin(vec_copy(0), "vec")

    def decode():
        loaded("mask_token")
        for number, axis in enumerate(PEERS + ("self",)):
            if axis == "self":
                source = my_pos
                arrived_rows = ref["grid_out"][my_pos]
            else:
                source = peer(axis)[1]
                remote(ref["grid_out"].at[source], ref["grid_in"].at[number], "grid", number, axis).wait_recv()
                arrived_rows = ref["grid_in"][number]
            placing = ref["placing"][number]
            visible = jnp.sum(placing.astype(FULL), axis=1, keepdims=True)
            filled = jnp.where(visible > 0.5, dot(placing, arrived_rows), row_of("mask_token").astype(FULL)).astype(LOW)
            for image in range(IMG_SEQ):
                ref["decoder_input"][source * IMG_SEQ + image] = filled[
                    image * PLACES : image * PLACES + quarter_len
                ]

    segments = {
        "project": project,
        "delta_rows": delta_rows,
        "delta": delta,
        "pass_delta": pass_delta,
        "transposes": transposes,
        "second_back": second_back,
        "attended_back": attended_back,
        "delta_first": delta_first,
        "first_back": first_back,
        "decode": decode,
    }
    for slot in range(4):
        segments["feed%d" % slot] = functools.partial(feed, slot)
        segments["feed_back%d" % slot] = functools.partial(feed_back, slot)
        segments["multiply_down%d" % slot] = functools.partial(multiply_down, slot)
        segments["multiply_up%d" % slot] = functools.partial(multiply_up, slot)
    for pair in range(HEADS // 2):
        segments["attend_back%d" % pair] = functools.partial(attend_back, pair)
    for which in swaps[2:8]:
        segments["swapped_" + which] = functools.partial(swapped, which)
    for job in JOBS:
        if JOBS[job][0] not in ("down", "up"):
            segments["multiply_" + job] = functools.partial(multiply, job)
    for step in PLAN:
        if step[0] == "do":
            segments[step[1]]()
        elif step[0] == "vec":
            arrive_vec(step[1])
        else:
            arrive(*step)
    for copy in leaving.values():
        copy.wait_send()


def finish_kernel(names, *refs):
    ref = dict(zip(names, refs))
    stores = []
    for number in (5, 6, 1, 0, 4, 3, 2):
        source = ref["in%d" % number]
        if number < 5:
            source = ref["full%d" % number]
            source[...] = ref["in%d" % number][...].astype(FULL)
        store = pltpu.make_async_copy(source, ref["out%d" % number], ref["store"].at[number])
        store.start()
        stores.append(store)
    sums = ref["sums"]
    for spot, number in zip(
        (LN1_GAIN, LN1_BIAS, BIAS_Q, BIAS_V, BIAS_OUT, LN2_GAIN, LN2_BIAS, BIAS_DOWN, BIAS_PROJ, MASK), range(10)
    ):
        target = ref["vec%d" % number]
        target[...] = sums[spot, : target.shape[0]]
    wide = sums.shape[1]
    for number in range(ref["vec10"].shape[1] // wide):
        ref["vec10"][:, number * wide : (number + 1) * wide] = sums[BIAS_UP + number : BIAS_UP + number + 1, :]
    for store in stores:
        store.wait()


def layer_device(
    tokens,
    image_slot,
    patch_position,
    ln1_gain,
    ln1_bias,
    w_qkv,
    bias_query,
    bias_value,
    w_out,
    bias_out,
    ln2_gain,
    ln2_bias,
    w_up,
    bias_up,
    w_down,
    bias_down,
    w_proj,
    bias_proj,
    mask_token,
    cotangent,
):
    rows, width = tokens.shape
    ff = w_up.shape[1]
    out_width = w_proj.shape[1]
    vmem = pl.BlockSpec(memory_space=pltpu.VMEM)
    hbm = pl.BlockSpec(memory_space=pl.ANY)
    inputs = {
        "tokens": tokens,
        "slot": image_slot,
        "position": patch_position,
        "ln1_gain": ln1_gain,
        "ln1_bias": ln1_bias,
        "bias_query": bias_query,
        "bias_value": bias_value,
        "bias_out": bias_out,
        "ln2_gain": ln2_gain,
        "ln2_bias": ln2_bias,
        "bias_up": bias_up,
        "bias_down": bias_down,
        "bias_proj": bias_proj,
        "mask_token": mask_token,
        "cotangent": cotangent,
        "w_qkv": w_qkv,
        "w_out": w_out,
        "w_proj": w_proj,
        "w_up": w_up,
        "w_down": w_down,
    }
    lefts = {"down": ff, "up": width, "proj": width, "out": width, "qkv": width}
    rights = {"down": width, "up": ff, "proj": out_width, "out": width, "qkv": 3 * width}
    outs = {}
    for name in MATRICES:
        block = (2, 2, 96) if name == "down" else (2, 48)
        outs["grad_" + name] = pltpu.VMEM(block + (rights[name],), LOW)
    outs["decoder_input"] = pltpu.VMEM(cotangent.shape, LOW)
    outs["grad_tokens"] = pltpu.VMEM(tokens.shape, LOW)
    outs["vec_sums"] = pltpu.VMEM((16, width), FULL)
    dma = pltpu.SemaphoreType.DMA
    room = {name + "_held": (array.shape, array.dtype) for name, array in inputs.items()}
    room |= {
        "slope": ((4, rows, width), FULL),
        "bias_up_row": ((1, ff), FULL),
        "places": ((4, 8, rows), jnp.int32),
        "chosen": ((4, IMG_SEQ * CAP, rows), LOW),
        "placing": ((4, IMG_SEQ * PLACES, IMG_SEQ * CAP), LOW),
        "allowed": ((rows, rows), FULL),
        "cot_wide": ((4 * IMG_SEQ, PLACES, out_width), LOW),
        "back_out": ((3, IMG_SEQ * CAP, out_width), LOW),
        "back_in": ((4, IMG_SEQ * CAP, out_width), LOW),
        "grid_out": ((4, IMG_SEQ * CAP, out_width), LOW),
        "grid_in": ((3, IMG_SEQ * CAP, out_width), LOW),
        "normed": ((rows, width), LOW),
        "normed_one": ((rows, width), LOW),
        "qkv": ((rows, 3 * width), LOW),
        "probs": ((HEADS, rows, rows), FULL),
        "attended": ((rows, width), LOW),
        "residual": ((rows, width), FULL),
        "delta_block": ((rows, width), FULL),
        "mlp_out": ((rows, width), FULL),
        "delta_normed": ((rows, width), FULL),
        "block_low": ((rows, width), LOW),
        "delta_attended": ((rows, width), LOW),
        "bias_up_sum": ((1, ff), FULL),
        "vec_own": ((16, width), FULL),
        "vec_held": ((6, 8, width), FULL),
        "vec_in": ((6, 8, width), FULL),
        "left_in_down": ((3, 4, 192, rows), LOW),
        "right_in_down": ((3, rows, width), LOW),
        "right_in_up": ((4, rows, width // 2), LOW),
        "final_down": ((2, 2, 96, width), LOW),
        "final_up": ((4, 2, 2, 48, width // 2), LOW),
    }
    for name in MATRICES:
        room["left_" + name] = ((lefts[name], rows), LOW)
        room["right_" + name] = ((rows, rights[name]), LOW)
        if name != "down":
            room["left_in_" + name] = ((lefts[name], rows), LOW)
        if name in ("proj", "out", "qkv"):
            room["right_in_" + name] = ((rows, rights[name] // 2), LOW)
            room["final_" + name] = ((2, 2, 48, rights[name] // 2), LOW)
    for job, (name, _, _, wide, _) in JOBS.items():
        block = (96 if name == "down" else 48, wide)
        count = len(axes_of(name))
        room["partial_" + job] = ((2,) * count + block, LOW)
        for stage in range(count):
            room["landed_%s_%d" % (job, stage)] = ((2,) * (count - 1 - stage) + block, LOW)
    scratch = {name: pltpu.VMEM(shape, dtype) for name, (shape, dtype) in room.items()}
    scratch["load"] = dma((len(inputs),))
    scratch["direct_send"] = dma((len(DIRECT),))
    scratch["direct_recv"] = dma((len(DIRECT),))
    downs = sum(job[0] == "down" for job in JOBS.values())
    for kind, shape in (("small", (3,)), ("core", (16,)), ("job", (2 * len(JOBS) + downs,)), ("vec", (1,))):
        scratch[kind + "_send"] = dma(shape)
    for kind, shape in (
        ("place", (3,)),
        ("back", (3,)),
        ("grid", (3,)),
        ("core", (28,)),
        ("job", (len(JOBS), 6)),
        ("vec", (6,)),
    ):
        scratch[kind + "_recv"] = dma(shape)
    names = tuple(inputs) + tuple(outs) + tuple(scratch)
    found = pl.pallas_call(
        functools.partial(layer_kernel, names),
        out_shape=list(outs.values()),
        in_specs=[hbm] * len(inputs),
        out_specs=[vmem] * len(outs),
        scratch_shapes=list(scratch.values()),
        compiler_params=pltpu.CompilerParams(
            collective_id=0, has_side_effects=True, vmem_limit_bytes=59 * 2**20
        ),
        name="layer",
    )(*inputs.values())
    found = dict(zip(outs, found))
    sources = [found["grad_" + name].reshape(-1, rights[name]) for name in MATRICES]
    sources += [found["decoder_input"], found["grad_tokens"]]
    operands = {"in%d" % number: source for number, source in enumerate(sources)}
    operands["sums"] = found["vec_sums"]
    results = {}
    for number, source in enumerate(sources):
        results["out%d" % number] = jax.ShapeDtypeStruct(source.shape, FULL if number < 5 else LOW)
    for number, wide in enumerate([width] * 8 + [out_width] * 2):
        results["vec%d" % number] = jax.ShapeDtypeStruct((wide,), FULL)
    results["vec10"] = jax.ShapeDtypeStruct((1, ff), FULL)
    held = {"full%d" % number: pltpu.VMEM(source.shape, FULL) for number, source in enumerate(sources[:5])}
    held["store"] = dma((7,))
    done = pl.pallas_call(
        functools.partial(finish_kernel, tuple(operands) + tuple(results) + tuple(held)),
        out_shape=list(results.values()),
        in_specs=[vmem] * 8,
        out_specs=[hbm] * 7 + [vmem] * 11,
        scratch_shapes=list(held.values()),
        compiler_params=pltpu.CompilerParams(vmem_limit_bytes=24 * 2**20),
        name="finish",
    )(*operands.values())
    down, up, proj, out, qkv, decoder_input, grad_tokens = done[:7]
    gain1, bias1, b_query, b_value, b_out, gain2, bias2, b_down, b_proj, mask, b_up = done[7:]
    b_up = b_up.reshape(-1)
    return (
        decoder_input,
        grad_tokens,
        gain1,
        bias1,
        qkv,
        b_query,
        b_value,
        out,
        b_out,
        gain2,
        bias2,
        up,
        b_up,
        down,
        b_down,
        proj,
        b_proj,
        mask,
    )


def solution(mesh):
    placed = (
        P(("img", "pos"), None),
        P(("img", "pos")),
        P(("img", "pos")),
        P(),
        P(),
        P(),
        P(),
        P(),
        P(),
        P(),
        P(),
        P(),
        P(),
        P(),
        P(),
        P(),
        P(),
        P(),
        P(),
        P("img", "pos", None),
    )
    fits = mesh.shape["img"] == 8 and mesh.shape["pos"] == 4
    return jax.shard_map(
        layer_device if fits else general_device,
        mesh=mesh,
        in_specs=placed,
        out_specs=(
            P("img", "pos", None),
            P(("img", "pos"), None),
            P(),
            P(),
            P("img", None),
            P(),
            P(),
            P("img", None),
            P(),
            P(),
            P(),
            P("img", None),
            P(),
            P("img", None),
            P(),
            P("img", None),
            P(),
            P(),
        ),
        check_vma=False,
    )
```

```python
import functools

import jax
import jax.numpy as jnp
from jax import lax
from jax.experimental import pallas as pl
from jax.experimental.pallas import tpu as pltpu
from jax.sharding import PartitionSpec as P

HEADS = 12
HEAD_DIM = 64
ROWS_SEQ = 256
IMG_SEQ = 5
POSITIONS = 196
CAP = 16


EPSILON = 1e-05
NEGATIVE = -1e30
GELU_COEF = 0.7978845608028654


def layer_norm(values, gain_vec, shift_vec):
    centre = jnp.mean(values, axis=-1, keepdims=True)
    centred = values - centre
    return (
        centred
        * lax.rsqrt(jnp.mean(centred * centred, axis=-1, keepdims=True) + EPSILON)
        * gain_vec
        + shift_vec
    )


def gelu_tanh(values):
    return (
        0.5 * values * (1.0 + jnp.tanh(GELU_COEF * (values + 0.044715 * values * values * values)))
    )


def matmul_rows(left, right):
    return jnp.dot(left, right, preferred_element_type=jnp.float32)


def column_sums(values):
    return jnp.sum(values.astype(jnp.float32), axis=0)


def reduce_matrices(members):
    img_count = lax.axis_size("img")
    pos_count = lax.axis_size("pos")
    pieces = [member.reshape(img_count, pos_count, -1) for member in members]
    bucket = jnp.concatenate(pieces, axis=2)
    flat_bucket = bucket.reshape(img_count * pos_count, -1)
    share = lax.psum_scatter(flat_bucket, ("img", "pos"), scatter_dimension=0, tiled=True).reshape(
        1, 1, -1
    )
    summed = lax.all_gather(share.astype(jnp.bfloat16), "pos", axis=1, tiled=True).astype(
        share.dtype
    )
    results = []
    offset = 0
    for member in members:
        extent = member.size // (img_count * pos_count)
        block = summed[0, :, offset : offset + extent]
        results.append(block.reshape(member.shape[0] // img_count, member.shape[1]))
        offset = offset + extent
    return results


def reduce_vectors(members):
    return lax.psum(tuple(members), ("img", "pos"))


def general_device(
    tokens,
    image_slot,
    patch_position,
    ln1_gain,
    ln1_bias,
    w_qkv,
    bias_query,
    bias_value,
    w_out,
    bias_out,
    ln2_gain,
    ln2_bias,
    w_up,
    bias_up,
    w_down,
    bias_down,
    w_proj,
    bias_proj,
    mask_token,
    cotangent,
):
    seq_count = tokens.shape[0] // ROWS_SEQ
    width = w_out.shape[0]
    out_width = w_proj.shape[1]
    pos_count = lax.axis_size("pos")
    quarter_len = POSITIONS // pos_count
    score_scale = HEAD_DIM ** (-0.5)
    head_shape = (seq_count, ROWS_SEQ, HEADS, HEAD_DIM)
    rows_f = tokens.astype(jnp.float32)
    normed_low = layer_norm(rows_f, ln1_gain, ln1_bias).astype(jnp.bfloat16)
    qkv_all = matmul_rows(normed_low, w_qkv)
    queries = (qkv_all[:, :width] + bias_query).astype(jnp.bfloat16).reshape(head_shape)
    keys_h = qkv_all[:, width : 2 * width].astype(jnp.bfloat16).reshape(head_shape)
    values_h = (qkv_all[:, 2 * width :] + bias_value).astype(jnp.bfloat16).reshape(head_shape)
    slot_rows = image_slot.reshape(seq_count, ROWS_SEQ)
    allowed = slot_rows[:, None, :, None] == slot_rows[:, None, None, :]
    raw_scores = (
        jnp.einsum("sqhd,skhd->shqk", queries, keys_h, preferred_element_type=jnp.float32)
        * score_scale
    )
    scores = jnp.where(allowed, raw_scores, NEGATIVE)
    top_score = jnp.max(scores, axis=-1, keepdims=True)
    log_total = top_score + jnp.log(jnp.sum(jnp.exp(scores - top_score), axis=-1, keepdims=True))
    attn_probs = jnp.exp(scores - log_total)
    probs_low = attn_probs.astype(jnp.bfloat16)
    attended = jnp.einsum(
        "shqk,skhd->sqhd", probs_low, values_h, preferred_element_type=jnp.float32
    )
    attended = attended.reshape(-1, width).astype(jnp.bfloat16)
    residual = rows_f + matmul_rows(attended, w_out) + bias_out
    normed_mlp = layer_norm(residual, ln2_gain, ln2_bias).astype(jnp.bfloat16)
    up_proj = matmul_rows(normed_mlp, w_up) + bias_up
    hidden = gelu_tanh(up_proj).astype(jnp.bfloat16)
    block_out = residual + matmul_rows(hidden, w_down) + bias_down
    block_low = block_out.astype(jnp.bfloat16)
    projected = (matmul_rows(block_low, w_proj) + bias_proj).astype(jnp.bfloat16)
    row_index = jnp.arange(ROWS_SEQ, dtype=jnp.int32)
    pos_rows = patch_position.reshape(seq_count, ROWS_SEQ)
    live = slot_rows >= 0
    bucket_id = jnp.where(live, slot_rows * pos_count + pos_rows // quarter_len, -1)
    earlier = (bucket_id[:, :, None] == bucket_id[:, None, :]) & (
        row_index[None, :, None] > row_index[None, None, :]
    )
    rank_in = jnp.sum(earlier.astype(jnp.int32), axis=2)
    target = jnp.where(live, bucket_id * CAP + rank_in, -1)
    slot_index = jnp.arange(IMG_SEQ * pos_count * CAP, dtype=jnp.int32)
    selected = slot_index[None, :, None] == target[:, None, :]
    select_low = selected.astype(jnp.bfloat16)
    outgoing = jnp.einsum(
        "sjr,src->sjc",
        select_low,
        projected.reshape(seq_count, ROWS_SEQ, out_width),
        preferred_element_type=jnp.float32,
    ).astype(jnp.bfloat16)
    outgoing = outgoing.reshape(seq_count * IMG_SEQ, pos_count, CAP, out_width)
    slot_place = (
        jnp.sum(jnp.where(selected, (pos_rows % quarter_len + 1)[:, None, :], 0), axis=2) - 1
    )
    slot_place = slot_place.reshape(seq_count * IMG_SEQ, pos_count, CAP)
    arrived, arrived_place = (
        lax.all_to_all(outgoing, "pos", split_axis=1, concat_axis=0, tiled=True),
        lax.all_to_all(slot_place, "pos", split_axis=1, concat_axis=0, tiled=True),
    )
    arrived = arrived[:, 0]
    arrived_place = arrived_place[:, 0]
    placing = jnp.arange(quarter_len, dtype=jnp.int32)[None, :, None] == arrived_place[:, None, :]
    placing_low = placing.astype(jnp.bfloat16)
    visible = jnp.any(placing, axis=2)
    filled = jnp.einsum("gqj,gjc->gqc", placing_low, arrived, preferred_element_type=jnp.float32)
    decoder_input = jnp.where(
        visible[:, :, None], filled, mask_token.astype(jnp.float32)[None, None, :]
    )
    decoder_input = decoder_input.astype(jnp.bfloat16)
    grad_mask = jnp.sum(
        jnp.where(visible[:, :, None], 0.0, cotangent.astype(jnp.float32)), axis=(0, 1)
    )
    back_slots = jnp.einsum(
        "gqj,gqc->gjc", placing_low, cotangent, preferred_element_type=jnp.float32
    ).astype(jnp.bfloat16)
    returned = lax.all_to_all(back_slots[:, None], "pos", split_axis=0, concat_axis=1, tiled=True)
    delta_proj = (
        jnp.einsum(
            "sjr,sjc->src",
            select_low,
            returned.reshape(seq_count, -1, out_width),
            preferred_element_type=jnp.float32,
        )
        .reshape(-1, out_width)
        .astype(jnp.bfloat16)
    )
    grad_proj = jnp.einsum("rd,rc->dc", block_low, delta_proj, preferred_element_type=jnp.float32)
    grad_bproj = column_sums(delta_proj)
    delta_block = jnp.einsum("rc,dc->rd", delta_proj, w_proj, preferred_element_type=jnp.float32)
    delta_down = delta_block.astype(jnp.bfloat16)
    grad_down = jnp.einsum("rf,rd->fd", hidden, delta_down, preferred_element_type=jnp.float32)
    grad_bdown = column_sums(delta_down)
    delta_hidden = jnp.einsum("rd,fd->rf", delta_down, w_down, preferred_element_type=jnp.float32)
    gelu_back = jax.vjp(gelu_tanh, up_proj)[1]
    delta_up = gelu_back(delta_hidden)[0].astype(jnp.bfloat16)
    grad_up = jnp.einsum("rd,rf->df", normed_mlp, delta_up, preferred_element_type=jnp.float32)
    grad_bup = column_sums(delta_up)
    delta_normed = jnp.einsum("rf,df->rd", delta_up, w_up, preferred_element_type=jnp.float32)
    norm_back = jax.vjp(layer_norm, residual, ln2_gain, ln2_bias)[1]
    delta_resid_norm, grad_gain_two, grad_shift_two = norm_back(delta_normed)
    delta_residual = delta_block + delta_resid_norm
    mlp_mats = reduce_matrices((grad_proj, grad_down, grad_up))
    mlp_vecs = reduce_vectors(
        (grad_bproj, grad_bdown, grad_bup, grad_gain_two, grad_shift_two, grad_mask)
    )
    delta_branch = delta_residual.astype(jnp.bfloat16)
    grad_out = jnp.einsum("re,rd->ed", attended, delta_branch, preferred_element_type=jnp.float32)
    grad_bout = column_sums(delta_branch)
    delta_attended = jnp.einsum(
        "rd,ed->re", delta_branch, w_out, preferred_element_type=jnp.float32
    )
    delta_attended = delta_attended.astype(jnp.bfloat16).reshape(head_shape)
    delta_values = jnp.einsum(
        "shqk,sqhd->skhd", probs_low, delta_attended, preferred_element_type=jnp.float32
    ).astype(jnp.bfloat16)
    delta_probs = jnp.einsum(
        "sqhd,skhd->shqk", delta_attended, values_h, preferred_element_type=jnp.float32
    )
    delta_scores = attn_probs * (
        delta_probs - jnp.sum(delta_probs * attn_probs, axis=-1, keepdims=True)
    )
    delta_scores = delta_scores.astype(jnp.bfloat16)
    delta_queries = (
        (
            jnp.einsum("shqk,skhd->sqhd", delta_scores, keys_h, preferred_element_type=jnp.float32)
            * score_scale
        )
        .astype(jnp.bfloat16)
        .reshape(-1, width)
    )
    delta_keys = (
        (
            jnp.einsum("shqk,sqhd->skhd", delta_scores, queries, preferred_element_type=jnp.float32)
            * score_scale
        )
        .astype(jnp.bfloat16)
        .reshape(-1, width)
    )
    delta_values = delta_values.reshape(-1, width)
    delta_qkv = jnp.concatenate([delta_queries, delta_keys, delta_values], axis=1)
    grad_qkv = jnp.einsum("rd,re->de", normed_low, delta_qkv, preferred_element_type=jnp.float32)
    grad_bquery = column_sums(delta_queries)
    grad_bvalue = column_sums(delta_values)
    delta_first = jnp.einsum("re,de->rd", delta_qkv, w_qkv, preferred_element_type=jnp.float32)
    first_back = jax.vjp(layer_norm, rows_f, ln1_gain, ln1_bias)[1]
    delta_rows, grad_gain_one, grad_shift_one = first_back(delta_first)
    grad_tokens = (delta_residual + delta_rows).astype(jnp.bfloat16)
    attn_mats = reduce_matrices((grad_qkv, grad_out))
    attn_vecs = reduce_vectors((grad_bquery, grad_bvalue, grad_bout, grad_gain_one, grad_shift_one))
    return (
        decoder_input,
        grad_tokens,
        attn_vecs[3],
        attn_vecs[4],
        attn_mats[0],
        attn_vecs[0],
        attn_vecs[1],
        attn_mats[1],
        attn_vecs[2],
        mlp_vecs[3],
        mlp_vecs[4],
        mlp_mats[2],
        mlp_vecs[2],
        mlp_mats[1],
        mlp_vecs[1],
        mlp_mats[0],
        mlp_vecs[0],
        mlp_vecs[5],
    )


MESH_ID = pl.DeviceIdType.MESH
LOW = jnp.bfloat16
FULL = jnp.float32

AXES = ("zh", "zl", "x", "y")
MATRICES = ("down", "up", "proj", "out", "qkv")
JOBS = {
    "down0": ("down", None, 0, 256, ("zl", "zh", "y")),
    "down1": ("down", None, 256, 256, ("y", "zl", "zh")),
    "down2": ("down", None, 512, 256, ("y", "zl", "zh")),
    "up0a": ("up", 0, 0, 256, ("y", "zl", "zh", "x")),
    "up0b": ("up", 0, 256, 128, ("zl", "x", "zh", "y")),
    "up1a": ("up", 1, 0, 384, ("x", "zl", "y", "zh")),
    "up2a": ("up", 2, 0, 384, ("zl", "y", "zh", "x")),
    "up3a": ("up", 3, 0, 384, ("y", "zl", "zh", "x")),
    "proj0": ("proj", None, 0, 256, ("zl", "y", "x", "zh")),
    "out0": ("out", None, 0, 384, ("x", "y", "zl", "zh")),
    "qkv0": ("qkv", None, 0, 256, ("y", "x", "zl", "zh")),
    "qkv1": ("qkv", None, 256, 256, ("y", "zl", "zh", "x")),
    "qkv2": ("qkv", None, 512, 256, ("x", "y", "zl", "zh")),
    "qkv3": ("qkv", None, 768, 256, ("x", "y", "zl", "zh")),
    "qkv4": ("qkv", None, 1024, 128, ("x", "y", "zl", "zh")),
}
PLAN = (
    ("do", "feed0"),
    ("do", "feed1"),
    ("do", "feed2"),
    ("do", "feed3"),
    ("do", "project"),
    ("do", "delta_rows"),
    ("do", "delta"),
    ("do", "feed_back0"),
    ("do", "feed_back1"),
    ("do", "swapped_proj_left"),
    ("do", "swapped_proj_right"),
    ("do", "multiply_proj0"),
    ("do", "feed_back2"),
    ("do", "multiply_up0"),
    ("do", "feed_back3"),
    ("do", "second_back"),
    ("do", "attended_back"),
    ("do", "attend_back0"),
    ("do", "multiply_up1"),
    ("do", "multiply_up3"),
    ("do", "multiply_up2"),
    ("do", "transposes"),
    ("proj0", 0, ""),
    ("do", "attend_back1"),
    ("do", "attend_back2"),
    ("up0a", 0, ""),
    ("do", "attend_back3"),
    ("up0b", 0, ""),
    ("do", "attend_back4"),
    ("do", "attend_back5"),
    ("do", "delta_first"),
    ("do", "pass_delta"),
    ("do", "decode"),
    ("do", "swapped_out_left"),
    ("do", "swapped_out_right"),
    ("do", "multiply_out0"),
    ("do", "multiply_down0"),
    ("do", "multiply_down1"),
    ("up3a", 0, ""),
    ("do", "swapped_qkv_left"),
    ("do", "swapped_qkv_right"),
    ("do", "multiply_qkv0"),
    ("do", "multiply_qkv1"),
    ("do", "multiply_qkv2"),
    ("do", "multiply_qkv3"),
    ("do", "multiply_qkv4"),
    ("up2a", 0, ""),
    ("proj0", 1, ""),
    ("do", "first_back"),
    ("up0a", 1, ""),
    ("down1", 0, "a"),
    ("down0", 0, "a"),
    ("vec", 0),
    ("do", "multiply_down2"),
    ("do", "multiply_down3"),
    ("down2", 0, "a"),
    ("up3a", 1, ""),
    ("qkv0", 0, ""),
    ("up0a", 2, ""),
    ("down0", 0, "b"),
    ("up1a", 0, ""),
    ("up0b", 1, ""),
    ("qkv1", 0, ""),
    ("up3a", 2, ""),
    ("up2a", 1, ""),
    ("up1a", 1, ""),
    ("out0", 0, ""),
    ("down0", 1, ""),
    ("down1", 0, "b"),
    ("up0b", 2, ""),
    ("qkv1", 1, ""),
    ("down2", 0, "b"),
    ("qkv2", 0, ""),
    ("up1a", 2, ""),
    ("down1", 1, ""),
    ("up2a", 2, ""),
    ("out0", 1, ""),
    ("qkv3", 0, ""),
    ("qkv1", 2, ""),
    ("down2", 1, ""),
    ("down0", 2, ""),
    ("up0b", 3, ""),
    ("qkv4", 0, ""),
    ("qkv2", 1, ""),
    ("proj0", 2, ""),
    ("up1a", 3, ""),
    ("vec", 1),
    ("out0", 2, ""),
    ("qkv3", 1, ""),
    ("down1", 2, ""),
    ("qkv0", 1, ""),
    ("qkv2", 2, ""),
    ("down0", 4, ""),
    ("up0a", 3, ""),
    ("up0b", 4, ""),
    ("up3a", 3, ""),
    ("down2", 2, ""),
    ("qkv4", 1, ""),
    ("up2a", 3, ""),
    ("down0", 5, ""),
    ("up0b", 5, ""),
    ("up1a", 4, ""),
    ("qkv1", 3, ""),
    ("proj0", 3, ""),
    ("qkv3", 2, ""),
    ("vec", 2),
    ("qkv0", 2, ""),
    ("down1", 4, ""),
    ("up1a", 5, ""),
    ("out0", 3, ""),
    ("up0a", 4, ""),
    ("qkv4", 2, ""),
    ("up3a", 4, ""),
    ("down1", 5, ""),
    ("qkv2", 3, ""),
    ("vec", 3),
    ("up0a", 5, ""),
    ("down2", 4, ""),
    ("qkv3", 3, ""),
    ("up3a", 5, ""),
    ("up2a", 4, ""),
    ("qkv1", 4, ""),
    ("qkv0", 3, ""),
    ("down2", 5, ""),
    ("proj0", 4, ""),
    ("qkv4", 3, ""),
    ("up2a", 5, ""),
    ("out0", 4, ""),
    ("qkv1", 5, ""),
    ("qkv2", 4, ""),
    ("proj0", 5, ""),
    ("qkv3", 4, ""),
    ("vec", 4),
    ("qkv0", 4, ""),
    ("out0", 5, ""),
    ("qkv4", 4, ""),
    ("qkv2", 5, ""),
    ("qkv3", 5, ""),
    ("vec", 5),
    ("qkv0", 5, ""),
    ("qkv0", 6, ""),
    ("qkv4", 5, ""),
    ("qkv4", 6, ""),
)
DIRECT = ("qkv0", "qkv4",)
VEC_STEPS = ("core", "x", "y", "zl", "zh", "core")
PEERS = ("diagonal", "y", "core")
PLACES = 64
INPUTS = (
    "slot", "position", "ln1_gain", "ln1_bias", "tokens", "w_qkv", "cotangent", "bias_query", "bias_value", "w_out",
    "bias_out", "ln2_gain", "ln2_bias", "bias_up", "w_up", "w_down", "bias_down", "w_proj", "bias_proj", "mask_token",
)
LN1_GAIN, LN1_BIAS, BIAS_Q, BIAS_V, BIAS_OUT, LN2_GAIN, LN2_BIAS, BIAS_DOWN, BIAS_UP, BIAS_PROJ, MASK = (
    0, 1, 2, 3, 4, 5, 6, 7, 8, 12, 13,
)


def axes_of(matrix):
    return ("zh", "zl", "y") if matrix == "down" else AXES


def device_coords():
    img = lax.axis_index("img")
    pos = lax.axis_index("pos")
    return {"zh": img // 4, "zl": (img // 2) % 2, "x": img % 2, "y": pos // 2, "core": pos % 2}


def device_of(where):
    return (where["zh"] * 4 + where["zl"] * 2 + where["x"], where["y"] * 2 + where["core"])


def block_rows(name):
    return 96 if name == "down" else 48


def dot(left, right):
    return jnp.dot(left, right, preferred_element_type=FULL)


def dot_nt(left, right):
    return lax.dot_general(left, right, (((1,), (1,)), ((), ())), preferred_element_type=FULL)


def dot_tn(left, right):
    return lax.dot_general(left, right, (((0,), (0,)), ((), ())), preferred_element_type=FULL)


def normalised(values):
    centred = values - jnp.mean(values, axis=-1, keepdims=True)
    rstd = lax.rsqrt(jnp.mean(centred * centred, axis=-1, keepdims=True) + EPSILON)
    return centred * rstd, rstd


def norm_rows_back(delta, values, gain):
    xhat, rstd = normalised(values)
    scaled = delta * gain
    rows = rstd * (
        scaled
        - jnp.mean(scaled, axis=-1, keepdims=True)
        - xhat * jnp.mean(scaled * xhat, axis=-1, keepdims=True)
    )
    return rows, delta * xhat


def layer_kernel(names, *refs):
    ref = dict(zip(names, refs))

    def row_of(name, columns=slice(None)):
        return ref[name + "_held"][...].reshape(1, -1)[:, columns]

    me = device_coords()
    core = me["core"]
    my_pos = me["y"] * 2 + core
    width = ref["tokens_held"].shape[1]
    ff = ref["w_up"].shape[1]
    quarter_len = POSITIONS // 4

    def peer(axis):
        if axis == "diagonal":
            return device_of({**me, "y": 1 - me["y"], "core": 1 - core})
        if axis == "across":
            return device_of({**me, "x": 1 - me["x"], "core": 1 - core})
        return device_of({**me, axis: 1 - me[axis]})

    leaving = {}

    def remote(source, target, kind, spot, axis, leave=None):
        leave = ref["small_send"].at[spot] if leave is None else leave
        return pltpu.make_async_remote_copy(
            src_ref=source,
            dst_ref=target,
            send_sem=leave,
            recv_sem=ref[kind + "_recv"].at[spot],
            device_id=peer(axis),
            device_id_type=MESH_ID,
        )

    def begin(copy, use):
        if use in leaving:
            leaving.pop(use).wait_send()
        copy.start()
        leaving[use] = copy

    barrier = pltpu.get_barrier_semaphore()
    for axis in AXES + ("core", "diagonal", "across"):
        pl.semaphore_signal(barrier, inc=1, device_id=peer(axis), device_id_type=MESH_ID)

    loads = {}
    for number, name in enumerate(INPUTS):
        loads[name] = pltpu.make_async_copy(ref[name], ref[name + "_held"], ref["load"].at[number])
        loads[name].start()

    def loaded(*which):
        for name in which:
            loads[name].wait()

    loaded("slot", "position", "tokens", "ln1_gain", "ln1_bias")
    ref["places"][my_pos, 0:1, :] = row_of("slot")
    ref["places"][my_pos, 1:2, :] = row_of("position")

    def first_norm(step, carry):
        rows = pl.ds(pl.multiple_of(step * 64, 64), 64)
        xhat, _ = normalised(ref["tokens_held"][rows, :].astype(FULL))
        ref["normed"][rows, :] = (xhat * row_of("ln1_gain") + row_of("ln1_bias")).astype(LOW)
        return carry

    lax.fori_loop(0, 4, first_norm, 0, unroll=4)

    loaded("w_qkv", "bias_query", "bias_value")
    third = width // 256
    for number in range(3 * third):
        columns = slice(number * 256, (number + 1) * 256)
        if number == 6:
            pl.semaphore_wait(barrier, 7)
            for spot, axis in enumerate(PEERS):
                begin(remote(ref["places"].at[my_pos], ref["places"].at[my_pos], "place", spot, axis), spot)
        part = dot(ref["normed"][...], ref["w_qkv_held"][:, columns])
        if number < third:
            part = part + row_of("bias_query", columns)
            part = part.astype(LOW) * LOW(HEAD_DIM ** (-0.5))
        elif number >= 2 * third:
            part = part + row_of("bias_value", slice((number - 2 * third) * 256, (number - 2 * third + 1) * 256))
        ref["qkv"][:, columns] = part.astype(LOW)
    ref["normed_one"][...] = ref["normed"][...]

    row_ids = lax.broadcasted_iota(jnp.int32, (ROWS_SEQ, ROWS_SEQ), 0)
    lane_ids = lax.broadcasted_iota(jnp.int32, (ROWS_SEQ, ROWS_SEQ), 1)
    earlier = (row_ids < lane_ids).astype(FULL).astype(LOW)

    def one_hot(count, row):
        ids = lax.broadcasted_iota(jnp.int32, (count, ROWS_SEQ), 0)
        return jnp.where(ids == row, 1.0, 0.0)

    def picked(slot, position, quarter):
        offset = position - quarter * quarter_len
        inside = (slot >= 0) & (offset >= 0) & (offset < quarter_len)
        kinds = one_hot(8, jnp.where(inside, slot, -1))
        ranks = jnp.sum(kinds * dot(kinds.astype(LOW), earlier), axis=0, keepdims=True).astype(jnp.int32)
        chosen = one_hot(IMG_SEQ * CAP, jnp.where(inside, slot * CAP + ranks, -1))
        return chosen.astype(LOW), jnp.where(inside, slot * PLACES + offset, -1)

    for quarter in range(4):
        chosen, _ = picked(row_of("slot"), row_of("position"), quarter)
        ref["chosen"][quarter] = chosen

    slots = one_hot(8, row_of("slot") + 1).astype(LOW)
    ref["allowed"][...] = jnp.where(dot_tn(slots, slots) > 0.5, 0.0, NEGATIVE)

    lane = lax.broadcasted_iota(jnp.int32, (1, 2 * HEAD_DIM), 1)
    sides_full = [(lane < HEAD_DIM).astype(FULL), (lane >= HEAD_DIM).astype(FULL)]
    sides = [side.astype(LOW) for side in sides_full]

    def head_columns(pair, first):
        return pl.ds(first + pair * 2 * HEAD_DIM, 2 * HEAD_DIM)

    def attend(pair, carry):
        queries = ref["qkv"][:, head_columns(pair, 0)]
        keys = ref["qkv"][:, head_columns(pair, width)]
        values = ref["qkv"][:, head_columns(pair, 2 * width)]
        total = None
        for side in range(2):
            scores = dot_nt(queries * sides[side], keys) + ref["allowed"][...]
            powers = jnp.exp(scores - jnp.max(scores, axis=-1, keepdims=True))
            probs = powers / jnp.sum(powers, axis=-1, keepdims=True)
            ref["probs"][pair * 2 + side] = probs
            part = dot(probs.astype(LOW), values) * sides_full[side]
            total = part if total is None else total + part
        ref["attended"][:, head_columns(pair, 0)] = total.astype(LOW)
        return carry

    for pair in range(HEADS // 2):
        attend(pair, 0)

    ref["cot_wide"][...] = jnp.zeros_like(ref["cot_wide"])
    loaded("cotangent")
    for image in range(4 * IMG_SEQ):
        ref["cot_wide"][image, 0:quarter_len, :] = ref["cotangent_held"][image]
    for number, axis in enumerate(PEERS):
        source = peer(axis)[1]
        remote(ref["places"].at[source], ref["places"].at[source], "place", number, axis).wait_recv()
    for number, axis in enumerate(PEERS + ("self",)):
        source = my_pos if axis == "self" else peer(axis)[1]
        slot = ref["places"][source, 0:1, :]
        position = ref["places"][source, 1:2, :]
        chosen, place = picked(slot, position, my_pos)
        filled = one_hot(IMG_SEQ * PLACES, place).astype(LOW)
        placing = dot_nt(filled, chosen).astype(LOW)
        ref["placing"][number] = placing
        cot = ref["cot_wide"][pl.ds(source * IMG_SEQ, IMG_SEQ)].reshape(IMG_SEQ * PLACES, -1)
        back = dot_tn(placing, cot).astype(LOW)
        if axis == "self":
            ref["back_in"][my_pos] = back
        else:
            ref["back_out"][number] = back
    for number, axis in enumerate(PEERS):
        begin(remote(ref["back_out"].at[number], ref["back_in"].at[my_pos], "back", number, axis), number)
    ref["vec_own"][...] = jnp.zeros_like(ref["vec_own"])

    loaded("w_out", "bias_out")
    for number in range(third):
        columns = slice(number * 256, (number + 1) * 256)
        ref["residual"][:, columns] = (
            ref["tokens_held"][:, columns].astype(FULL)
            + dot(ref["attended"][...], ref["w_out_held"][:, columns])
            + row_of("bias_out", columns)
        )

    def second_norm(step, carry):
        rows = pl.ds(pl.multiple_of(step * 64, 64), 64)
        xhat, _ = normalised(ref["residual"][rows, :])
        ref["normed"][rows, :] = (xhat * row_of("ln2_gain") + row_of("ln2_bias")).astype(LOW)
        return carry

    loaded("ln2_gain", "ln2_bias")
    lax.fori_loop(0, 4, second_norm, 0, unroll=4)
    ref["left_up"][...] = ref["normed"][...].T

    def delta_rows():
        for number, axis in enumerate(PEERS):
            remote(ref["back_out"].at[number], ref["back_in"].at[my_pos], "back", number, axis).wait_recv()
        chosen_all = ref["chosen"][...].reshape(4 * IMG_SEQ * CAP, ROWS_SEQ)
        returned = ref["back_in"][...].reshape(4 * IMG_SEQ * CAP, -1)
        delta_proj = dot_tn(chosen_all, returned)
        ref["vec_own"][BIAS_PROJ : BIAS_PROJ + 1, : delta_proj.shape[1]] = jnp.sum(delta_proj, axis=0, keepdims=True)
        ref["right_proj"][...] = delta_proj.astype(LOW)
        swap("proj_right")

    def delta():
        for number in range(third):
            columns = slice(number * 256, (number + 1) * 256)
            part = dot_nt(ref["right_proj"][...], ref["w_proj_held"][columns, :])
            ref["delta_block"][:, columns] = part
            part = part.astype(LOW)
            ref["right_down"][:, columns] = part
            ref["vec_own"][BIAS_DOWN : BIAS_DOWN + 1, columns] = jnp.sum(part.astype(FULL), axis=0, keepdims=True)
        for which in ("delta_side", "delta_across", "side2", "across2", "side3", "across3", "delta"):
            swap(which)

    def pass_delta():
        for which, later in (("delta_side", "on_side"), ("delta_across", "on_across")):
            swapped(which)
            swap(later)

    loaded("w_up", "bias_up")
    ref["bias_up_row"][...] = row_of("bias_up")

    def chunk_columns(slot, start=0, wide=width):
        if isinstance(start, int):
            return pl.ds(slot * width + start, wide)
        return pl.ds(pl.multiple_of(slot * width + start, 128), wide)

    def feed(slot):
        columns = chunk_columns(slot)
        up = dot(ref["normed"][...], ref["w_up_held"][:, columns]) + ref["bias_up_row"][:, columns]
        square = up * up
        bent = jnp.tanh(GELU_COEF * (up + 0.044715 * up * square))
        half = 0.5 * (1.0 + bent)
        ref["slope"][slot] = half + 0.5 * up * (1.0 - bent * bent) * (GELU_COEF * (1.0 + 0.134145 * square))
        hidden = (up * half).astype(LOW)
        ref["left_down"][columns, :] = hidden.T
        swap("hidden%d" % slot)
        if slot < 2:
            swap("side%d" % slot)
            swap("across%d" % slot)
        if slot == 0:
            loaded("w_down", "bias_down")
        out = dot(hidden, ref["w_down_held"][columns, :])
        if slot == 0:
            ref["mlp_out"][...] = out
        else:
            ref["mlp_out"][...] += out

    def feed_back(slot):
        columns = chunk_columns(slot)
        back = dot_nt(ref["right_down"][...], ref["w_down_held"][columns, :])
        delta_up = (back * ref["slope"][slot]).astype(LOW)
        ref["right_up"][:, columns] = delta_up
        swap("feed%d" % slot)
        ref["bias_up_sum"][:, columns] = jnp.sum(delta_up.astype(FULL), axis=0, keepdims=True)
        delta = dot_nt(delta_up, ref["w_up_held"][:, columns])
        if slot == 0:
            ref["delta_normed"][...] = delta
        else:
            ref["delta_normed"][...] += delta

    swaps = ("norm", "delta", "proj_left", "proj_right", "out_left", "out_right", "qkv_left", "qkv_right")
    swaps += tuple("hidden%d" % slot for slot in range(4)) + tuple("feed%d" % slot for slot in range(4))
    swaps += tuple("side%d" % slot for slot in range(4)) + tuple("across%d" % slot for slot in range(4))
    swaps += ("delta_side", "delta_across", "on_side", "on_across")

    def swap_copy(which):
        other = 1 - core
        axis = "core"
        half = width // 2
        if which == "norm":
            source, target = ref["left_up"], ref["left_in_up"]
        elif which == "delta":
            source, target = ref["right_down"], ref["right_in_down"].at[0]
        elif which == "delta_side":
            source, target = ref["right_down"].at[:, pl.ds(0, half)], ref["right_in_down"].at[1, :, pl.ds(0, half)]
            axis = "x"
        elif which == "delta_across":
            source, target = ref["right_down"].at[:, pl.ds(half, half)], ref["right_in_down"].at[2, :, pl.ds(half, half)]
            axis = "across"
        elif which == "on_side":
            source = ref["right_in_down"].at[1, :, pl.ds(0, half)]
            target = ref["right_in_down"].at[2, :, pl.ds(0, half)]
        elif which == "on_across":
            source = ref["right_in_down"].at[2, :, pl.ds(half, half)]
            target = ref["right_in_down"].at[1, :, pl.ds(half, half)]
        elif which[:-1] in ("hidden", "side", "across"):
            chunk = int(which[-1])
            blocks = ref["left_down"].reshape(8, 2, 192, ROWS_SEQ)
            if which.startswith("hidden"):
                source, target = blocks.at[chunk * 2 + me["x"], other], ref["left_in_down"].at[0, chunk]
            elif which.startswith("side"):
                source, target = blocks.at[chunk * 2 + 1 - me["x"], core], ref["left_in_down"].at[1, chunk]
                axis = "x"
            else:
                source, target = blocks.at[chunk * 2 + 1 - me["x"], other], ref["left_in_down"].at[2, chunk]
                axis = "across"
        elif which.startswith("feed"):
            slot = int(which[4:])
            source = ref["right_up"].at[:, chunk_columns(slot, other * half, half)]
            target = ref["right_in_up"].at[slot]
        else:
            matrix, side = which.split("_")
            if side == "left":
                source, target = ref["left_" + matrix], ref["left_in_" + matrix]
            else:
                wide = ref["right_" + matrix].shape[1] // 2
                source = ref["right_" + matrix].at[:, pl.ds(pl.multiple_of(other * wide, 128), wide)]
                target = ref["right_in_" + matrix]
        leave = swap_leave[which] if which in swap_leave else 0
        return remote(source, target, "core", swaps.index(which), axis, ref["core_send"].at[leave])

    swap_leave = {}

    def swap(which):
        far = which[:-1] in ("side", "across") or which.startswith("delta_")
        many = sum(spot < 6 if not far else spot >= 6 for spot in swap_leave.values())
        swap_leave[which] = 6 + many if far else many % 6
        begin(swap_copy(which), ("core", swap_leave[which]))

    def swapped(which):
        swap_copy(which).wait_recv()

    job_names = tuple(JOBS)

    def job_final(job):
        matrix, slot, first, wide, _ = JOBS[job]
        final = ref["final_" + matrix]
        if slot is not None:
            final = final.at[slot]
        return final, pl.ds(first, wide)

    def job_index(job, stage, part, mine):
        dims = JOBS[job][4]
        pick, land = [], []
        for axis in axes_of(JOBS[job][0]):
            if axis in dims[:stage]:
                pick.append(me[axis])
            elif axis == dims[stage]:
                pick.append(me[axis] if mine else 1 - me[axis])
            elif axis == "zh" and part:
                pick.append("ab".index(part))
                land.append(pick[-1])
            else:
                pick.append(slice(None))
                land.append(slice(None))
        return tuple(pick), tuple(land)

    def job_send_spot(job, stage, part):
        spot = job_names.index(job)
        if stage == 6:
            return job
        return 2 * len(job_names) + spot if part == "b" else 2 * spot + stage % 2

    def job_copy(job, stage, part):
        dims = JOBS[job][4]
        spot = stage if part != "b" else 3
        send_sem = ref["job_send"].at[job_send_spot(job, min(stage, 5), part)]
        recv_sem = ref["job_recv"].at[job_names.index(job), min(spot, 5)]
        if stage < 4:
            pick, land = job_index(job, stage, part, False)
            source = ref["partial_" + job].at[pick]
            place = ref["landed_%s_%d" % (job, stage)]
            place = place.at[land] if land else place
            axis = dims[stage]
        else:
            final, columns = job_final(job)
            if stage == 4 or job in DIRECT:
                source = place = final.at[core, me["y"], :, columns]
            else:
                source = place = final.at[core, :, :, columns]
            axis = ("y", "core", "diagonal")[stage - 4]
        if stage == 6:
            send_sem = ref["direct_send"].at[DIRECT.index(job)]
            recv_sem = ref["direct_recv"].at[DIRECT.index(job)]
        return pltpu.make_async_remote_copy(
            src_ref=source,
            dst_ref=place,
            send_sem=send_sem,
            recv_sem=recv_sem,
            device_id=peer(axis),
            device_id_type=MESH_ID,
        )

    def first_parts(job):
        return ("a", "b") if JOBS[job][0] == "down" else ("",)

    def needs(job, stage):
        dims = JOBS[job][4]
        firsts = tuple((0, part) for part in first_parts(job))
        if stage == 1:
            return firsts
        if stage == 2:
            return ((1, ""),) + firsts
        if stage == 4 or job in DIRECT and stage > 4:
            return ((len(dims) - 1, ""),) + firsts
        return ((stage - 1, ""),)

    arrived, sent = set(), set()

    def send(job, stage, part=""):
        sent.add((job, stage, part))
        begin(job_copy(job, stage, part), ("job", job_send_spot(job, stage, part)))

    def arrive(job, stage, part):
        matrix, slot, _, _, dims = JOBS[job]
        axes = axes_of(matrix)
        last = len(dims) - 1
        job_copy(job, stage, part).wait_recv()
        if stage < 4:
            partial, landed = ref["partial_" + job], ref["landed_%s_%d" % (job, stage)]
            pick, land = job_index(job, stage, part, True)
            free = [spot for spot, index in enumerate(pick) if isinstance(index, slice)]
            for code in range(2 ** len(free)):
                here, there = list(pick), list(land)
                for order, spot in enumerate(free):
                    bit = (code >> (len(free) - 1 - order)) % 2
                    here[spot] = bit
                    there[[place for place, axis in enumerate(axes) if axis not in dims[: stage + 1]].index(spot)] = bit
                sums = partial[tuple(here)] + (landed[tuple(there)] if there else landed[...])
                if stage < last:
                    partial[tuple(here)] = sums
                else:
                    final, columns = job_final(job)
                    final[core, me["y"], :, columns] = sums
        arrived.add((job, stage, part))
        for later in list(range(1, last + 1)) + ([4, 6, 5] if job in DIRECT else [4, 5]):
            ready = all((job,) + need in arrived for need in needs(job, later))
            if (job, later, "") not in sent and ready:
                send(job, later)
        ends = (4, 5, 6) if job in DIRECT else (5,)
        if stage in ends and all((job, end, "") in arrived for end in ends):
            final, columns = job_final(job)
            _, _, first, wide, _ = JOBS[job]
            out = ref["grad_" + matrix]
            for side in range(2):
                if matrix == "down":
                    out[side, :, :, columns] = final[side, :, :, columns]
                else:
                    start = side * ref["final_" + matrix].shape[-1] + first
                    place = pl.ds(start, wide) if slot is None else chunk_columns(slot, start, wide)
                    out[:, :, place] = final[side, :, :, columns]

    def multiply_down(slot):
        if slot == 0:
            for which in ("delta", "on_side", "on_across"):
                swapped(which)
        for which in ("hidden", "side", "across"):
            swapped(which + str(slot))
        rows = pl.ds(pl.multiple_of((slot * 2 + me["x"]) * 384 + core * 192, 192), 192)
        total = dot(ref["left_down"][rows, :], ref["right_down"][...])
        for number in range(3):
            total = total + dot(ref["left_in_down"][number, slot], ref["right_in_down"][number])
        total = total.astype(LOW)
        for job, (matrix, _, first, wide, _) in JOBS.items():
            if matrix == "down":
                for half in range(2):
                    ref["partial_" + job][slot // 2, slot % 2, half] = total[half * 96 : (half + 1) * 96, first : first + wide]
        if slot % 2 == 1:
            for job in JOBS:
                if JOBS[job][0] == "down":
                    send(job, 0, "ab"[slot // 2])

    def multiply_up(slot):
        if slot == 0:
            swapped("norm")
        swapped("feed%d" % slot)
        for block in range(2):
            rows = slice(block * 384, (block + 1) * 384)
            total = dot(
                ref["left_up"][rows, :], ref["right_up"][:, chunk_columns(slot, core * (width // 2), width // 2)]
            ) + dot(ref["left_in_up"][rows, :], ref["right_in_up"][slot])
            total = total.astype(LOW)
            for job, (matrix, own, first, wide, _) in JOBS.items():
                if matrix == "up" and own == slot:
                    for part in range(8):
                        ref["partial_" + job][block, part // 4, (part // 2) % 2, part % 2] = total[
                            part * 48 : (part + 1) * 48, first : first + wide
                        ]
        for job, (matrix, own, _, _, _) in JOBS.items():
            if matrix == "up" and own == slot:
                send(job, 0)

    def multiply(job):
        matrix, _, first, wide, _ = JOBS[job]
        wide_half = ref["right_" + matrix].shape[1] // 2
        columns = pl.ds(pl.multiple_of(core * wide_half + first, 128), wide)
        for block in range(2):
            rows = slice(block * 384, (block + 1) * 384)
            total = dot(ref["left_" + matrix][rows, :], ref["right_" + matrix][:, columns]) + dot(
                ref["left_in_" + matrix][rows, :], ref["right_in_" + matrix][:, first : first + wide]
            )
            total = total.astype(LOW)
            for part in range(8):
                ref["partial_" + job][block, part // 4, (part // 2) % 2, part % 2] = total[part * 48 : (part + 1) * 48]
        send(job, 0)

    def vec_rows(side):
        return pl.ds(pl.multiple_of(side * 8, 8), 8)

    def vec_copy(stage):
        source = ref["vec_own"].at[vec_rows(1 - core)] if stage == 0 else ref["vec_held"].at[stage]
        return remote(source, ref["vec_in"].at[stage], "vec", stage, VEC_STEPS[stage], ref["vec_send"].at[0])

    def arrive_vec(stage):
        vec_copy(stage).wait_recv()
        if stage == 5:
            ref["vec_sums"][vec_rows(1 - core), :] = ref["vec_in"][5]
            return
        own = ref["vec_own"][vec_rows(core), :] if stage == 0 else ref["vec_held"][stage]
        ref["vec_held"][stage + 1] = own + ref["vec_in"][stage]
        begin(vec_copy(stage + 1), "vec")
        if stage == 4:
            ref["vec_sums"][vec_rows(core), :] = ref["vec_held"][5]

    swap("norm")

    def project():
        for number in range(third):
            columns = slice(number * 256, (number + 1) * 256)
            ref["block_low"][:, columns] = (
                ref["residual"][:, columns] + ref["mlp_out"][:, columns] + row_of("bias_down", columns)
            ).astype(LOW)
        ref["left_proj"][...] = ref["block_low"][...].T
        swap("proj_left")
        loaded("w_proj", "bias_proj")
        projected = (dot(ref["block_low"][...], ref["w_proj_held"][...]) + row_of("bias_proj")).astype(LOW)
        outgoing = dot(ref["chosen"][...].reshape(4 * IMG_SEQ * CAP, ROWS_SEQ), projected).astype(LOW)
        ref["grid_out"][...] = outgoing.reshape(4, IMG_SEQ * CAP, -1)
        for number, axis in enumerate(PEERS):
            begin(remote(ref["grid_out"].at[peer(axis)[1]], ref["grid_in"].at[number], "grid", number, axis), number)

    def second_back():
        sums = [jnp.zeros((1, width), FULL)] * 3
        for step in range(4):
            rows = slice(step * 64, (step + 1) * 64)
            delta = ref["delta_normed"][rows, :]
            row_term, gains = norm_rows_back(delta, ref["residual"][rows, :], row_of("ln2_gain"))
            total = ref["delta_block"][rows, :] + row_term
            low = total.astype(LOW)
            ref["delta_block"][rows, :] = total
            ref["right_out"][rows, :] = low
            news = (gains, delta, low.astype(FULL))
            sums = [old + jnp.sum(new, axis=0, keepdims=True) for old, new in zip(sums, news)]
        for spot, total in zip((LN2_GAIN, LN2_BIAS, BIAS_OUT), sums):
            ref["vec_own"][spot : spot + 1, :] = total
        swap("out_right")

    def attended_back():
        for number in range(third):
            columns = slice(number * 256, (number + 1) * 256)
            ref["delta_attended"][:, columns] = dot_nt(ref["right_out"][...], ref["w_out_held"][columns, :]).astype(LOW)

    def transposes():
        ref["left_out"][...] = ref["attended"][...].T
        swap("out_left")
        ref["left_qkv"][...] = ref["normed_one"][...].T
        swap("qkv_left")

    def attend_back(pair):
        queries = ref["qkv"][:, head_columns(pair, 0)]
        keys = ref["qkv"][:, head_columns(pair, width)]
        values = ref["qkv"][:, head_columns(pair, 2 * width)]
        delta = ref["delta_attended"][:, head_columns(pair, 0)]
        totals = [None, None, None]
        for side in range(2):
            probs = ref["probs"][pair * 2 + side]
            delta_probs = dot_nt(delta * sides[side], values)
            delta_scores = probs * (delta_probs - jnp.sum(delta_probs * probs, axis=-1, keepdims=True))
            delta_scores = delta_scores.astype(LOW)
            parts = (
                dot(delta_scores, keys) * (HEAD_DIM ** (-0.5)),
                dot_tn(delta_scores, queries),
                dot_tn(probs.astype(LOW), delta),
            )
            for spot, part in enumerate(parts):
                part = part * sides_full[side]
                totals[spot] = part if totals[spot] is None else totals[spot] + part
        for spot, total in enumerate(totals):
            ref["right_qkv"][:, head_columns(pair, spot * width)] = total.astype(LOW)
        if pair == HEADS // 2 - 1:
            swap("qkv_right")

    def delta_first():
        for number in range(third):
            columns = slice(number * 256, (number + 1) * 256)
            ref["delta_normed"][:, columns] = dot_nt(ref["right_qkv"][...], ref["w_qkv_held"][columns, :])
        for spot, first in ((BIAS_Q, 0), (BIAS_V, 2 * width)):
            ref["vec_own"][spot : spot + 1, :] = jnp.sum(
                ref["right_qkv"][:, first : first + width].astype(FULL), axis=0, keepdims=True
            )

    def first_back():
        sums = [jnp.zeros((1, width), FULL)] * 2
        for step in range(4):
            rows = slice(step * 64, (step + 1) * 64)
            delta = ref["delta_normed"][rows, :]
            row_term, gains = norm_rows_back(delta, ref["tokens_held"][rows, :].astype(FULL), row_of("ln1_gain"))
            ref["grad_tokens"][rows, :] = (ref["delta_block"][rows, :] + row_term).astype(LOW)
            sums = [old + jnp.sum(new, axis=0, keepdims=True) for old, new in zip(sums, (gains, delta))]
        for spot, total in zip((LN1_GAIN, LN1_BIAS), sums):
            ref["vec_own"][spot : spot + 1, :] = total
        for number in range(ff // width):
            ref["vec_own"][BIAS_UP + number : BIAS_UP + number + 1, :] = ref["bias_up_sum"][
                :, number * width : (number + 1) * width
            ]
        mask_sum = jnp.zeros((8, ref["cot_wide"].shape[2]), FULL)
        for number, axis in enumerate(PEERS + ("self",)):
            source = my_pos if axis == "self" else peer(axis)[1]
            cot = ref["cot_wide"][pl.ds(source * IMG_SEQ, IMG_SEQ)].reshape(IMG_SEQ * PLACES, -1)
            seen = dot_nt(jnp.ones((8, IMG_SEQ * CAP), LOW), ref["placing"][number])
            mask_sum = mask_sum + dot((1.0 - seen).astype(LOW), cot)
        ref["vec_own"][MASK : MASK + 1, : mask_sum.shape[1]] = mask_sum[0:1]
        begin(vec_copy(0), "vec")

    def decode():
        loaded("mask_token")
        for number, axis in enumerate(PEERS + ("self",)):
            if axis == "self":
                source = my_pos
                arrived_rows = ref["grid_out"][my_pos]
            else:
                source = peer(axis)[1]
                remote(ref["grid_out"].at[source], ref["grid_in"].at[number], "grid", number, axis).wait_recv()
                arrived_rows = ref["grid_in"][number]
            placing = ref["placing"][number]
            visible = jnp.sum(placing.astype(FULL), axis=1, keepdims=True)
            filled = jnp.where(visible > 0.5, dot(placing, arrived_rows), row_of("mask_token").astype(FULL)).astype(LOW)
            for image in range(IMG_SEQ):
                ref["decoder_input"][source * IMG_SEQ + image] = filled[
                    image * PLACES : image * PLACES + quarter_len
                ]

    segments = {
        "project": project,
        "delta_rows": delta_rows,
        "delta": delta,
        "pass_delta": pass_delta,
        "transposes": transposes,
        "second_back": second_back,
        "attended_back": attended_back,
        "delta_first": delta_first,
        "first_back": first_back,
        "decode": decode,
    }
    for slot in range(4):
        segments["feed%d" % slot] = functools.partial(feed, slot)
        segments["feed_back%d" % slot] = functools.partial(feed_back, slot)
        segments["multiply_down%d" % slot] = functools.partial(multiply_down, slot)
        segments["multiply_up%d" % slot] = functools.partial(multiply_up, slot)
    for pair in range(HEADS // 2):
        segments["attend_back%d" % pair] = functools.partial(attend_back, pair)
    for which in swaps[2:8]:
        segments["swapped_" + which] = functools.partial(swapped, which)
    for job in JOBS:
        if JOBS[job][0] not in ("down", "up"):
            segments["multiply_" + job] = functools.partial(multiply, job)
    for step in PLAN:
        if step[0] == "do":
            segments[step[1]]()
        elif step[0] == "vec":
            arrive_vec(step[1])
        else:
            arrive(*step)
    for copy in leaving.values():
        copy.wait_send()


def finish_kernel(names, *refs):
    ref = dict(zip(names, refs))
    stores = []
    for number in (5, 6, 1, 0, 4, 3, 2):
        source = ref["in%d" % number]
        if number < 5:
            source = ref["full%d" % number]
            source[...] = ref["in%d" % number][...].astype(FULL)
        store = pltpu.make_async_copy(source, ref["out%d" % number], ref["store"].at[number])
        store.start()
        stores.append(store)
    sums = ref["sums"]
    for spot, number in zip(
        (LN1_GAIN, LN1_BIAS, BIAS_Q, BIAS_V, BIAS_OUT, LN2_GAIN, LN2_BIAS, BIAS_DOWN, BIAS_PROJ, MASK), range(10)
    ):
        target = ref["vec%d" % number]
        target[...] = sums[spot, : target.shape[0]]
    wide = sums.shape[1]
    for number in range(ref["vec10"].shape[1] // wide):
        ref["vec10"][:, number * wide : (number + 1) * wide] = sums[BIAS_UP + number : BIAS_UP + number + 1, :]
    for store in stores:
        store.wait()


def layer_device(
    tokens,
    image_slot,
    patch_position,
    ln1_gain,
    ln1_bias,
    w_qkv,
    bias_query,
    bias_value,
    w_out,
    bias_out,
    ln2_gain,
    ln2_bias,
    w_up,
    bias_up,
    w_down,
    bias_down,
    w_proj,
    bias_proj,
    mask_token,
    cotangent,
):
    rows, width = tokens.shape
    ff = w_up.shape[1]
    out_width = w_proj.shape[1]
    vmem = pl.BlockSpec(memory_space=pltpu.VMEM)
    hbm = pl.BlockSpec(memory_space=pl.ANY)
    inputs = {
        "tokens": tokens,
        "slot": image_slot,
        "position": patch_position,
        "ln1_gain": ln1_gain,
        "ln1_bias": ln1_bias,
        "bias_query": bias_query,
        "bias_value": bias_value,
        "bias_out": bias_out,
        "ln2_gain": ln2_gain,
        "ln2_bias": ln2_bias,
        "bias_up": bias_up,
        "bias_down": bias_down,
        "bias_proj": bias_proj,
        "mask_token": mask_token,
        "cotangent": cotangent,
        "w_qkv": w_qkv,
        "w_out": w_out,
        "w_proj": w_proj,
        "w_up": w_up,
        "w_down": w_down,
    }
    lefts = {"down": ff, "up": width, "proj": width, "out": width, "qkv": width}
    rights = {"down": width, "up": ff, "proj": out_width, "out": width, "qkv": 3 * width}
    outs = {}
    for name in MATRICES:
        block = (2, 2, 96) if name == "down" else (2, 48)
        outs["grad_" + name] = pltpu.VMEM(block + (rights[name],), LOW)
    outs["decoder_input"] = pltpu.VMEM(cotangent.shape, LOW)
    outs["grad_tokens"] = pltpu.VMEM(tokens.shape, LOW)
    outs["vec_sums"] = pltpu.VMEM((16, width), FULL)
    dma = pltpu.SemaphoreType.DMA
    room = {name + "_held": (array.shape, array.dtype) for name, array in inputs.items()}
    room |= {
        "slope": ((4, rows, width), FULL),
        "bias_up_row": ((1, ff), FULL),
        "places": ((4, 8, rows), jnp.int32),
        "chosen": ((4, IMG_SEQ * CAP, rows), LOW),
        "placing": ((4, IMG_SEQ * PLACES, IMG_SEQ * CAP), LOW),
        "allowed": ((rows, rows), FULL),
        "cot_wide": ((4 * IMG_SEQ, PLACES, out_width), LOW),
        "back_out": ((3, IMG_SEQ * CAP, out_width), LOW),
        "back_in": ((4, IMG_SEQ * CAP, out_width), LOW),
        "grid_out": ((4, IMG_SEQ * CAP, out_width), LOW),
        "grid_in": ((3, IMG_SEQ * CAP, out_width), LOW),
        "normed": ((rows, width), LOW),
        "normed_one": ((rows, width), LOW),
        "qkv": ((rows, 3 * width), LOW),
        "probs": ((HEADS, rows, rows), FULL),
        "attended": ((rows, width), LOW),
        "residual": ((rows, width), FULL),
        "delta_block": ((rows, width), FULL),
        "mlp_out": ((rows, width), FULL),
        "delta_normed": ((rows, width), FULL),
        "block_low": ((rows, width), LOW),
        "delta_attended": ((rows, width), LOW),
        "bias_up_sum": ((1, ff), FULL),
        "vec_own": ((16, width), FULL),
        "vec_held": ((6, 8, width), FULL),
        "vec_in": ((6, 8, width), FULL),
        "left_in_down": ((3, 4, 192, rows), LOW),
        "right_in_down": ((3, rows, width), LOW),
        "right_in_up": ((4, rows, width // 2), LOW),
        "final_down": ((2, 2, 96, width), LOW),
        "final_up": ((4, 2, 2, 48, width // 2), LOW),
    }
    for name in MATRICES:
        room["left_" + name] = ((lefts[name], rows), LOW)
        room["right_" + name] = ((rows, rights[name]), LOW)
        if name != "down":
            room["left_in_" + name] = ((lefts[name], rows), LOW)
        if name in ("proj", "out", "qkv"):
            room["right_in_" + name] = ((rows, rights[name] // 2), LOW)
            room["final_" + name] = ((2, 2, 48, rights[name] // 2), LOW)
    for job, (name, _, _, wide, _) in JOBS.items():
        block = (96 if name == "down" else 48, wide)
        count = len(axes_of(name))
        room["partial_" + job] = ((2,) * count + block, LOW)
        for stage in range(count):
            room["landed_%s_%d" % (job, stage)] = ((2,) * (count - 1 - stage) + block, LOW)
    scratch = {name: pltpu.VMEM(shape, dtype) for name, (shape, dtype) in room.items()}
    scratch["load"] = dma((len(inputs),))
    scratch["direct_send"] = dma((len(DIRECT),))
    scratch["direct_recv"] = dma((len(DIRECT),))
    downs = sum(job[0] == "down" for job in JOBS.values())
    for kind, shape in (("small", (3,)), ("core", (16,)), ("job", (2 * len(JOBS) + downs,)), ("vec", (1,))):
        scratch[kind + "_send"] = dma(shape)
    for kind, shape in (
        ("place", (3,)),
        ("back", (3,)),
        ("grid", (3,)),
        ("core", (28,)),
        ("job", (len(JOBS), 6)),
        ("vec", (6,)),
    ):
        scratch[kind + "_recv"] = dma(shape)
    names = tuple(inputs) + tuple(outs) + tuple(scratch)
    found = pl.pallas_call(
        functools.partial(layer_kernel, names),
        out_shape=list(outs.values()),
        in_specs=[hbm] * len(inputs),
        out_specs=[vmem] * len(outs),
        scratch_shapes=list(scratch.values()),
        compiler_params=pltpu.CompilerParams(
            collective_id=0, has_side_effects=True, vmem_limit_bytes=59 * 2**20
        ),
        name="layer",
    )(*inputs.values())
    found = dict(zip(outs, found))
    sources = [found["grad_" + name].reshape(-1, rights[name]) for name in MATRICES]
    sources += [found["decoder_input"], found["grad_tokens"]]
    operands = {"in%d" % number: source for number, source in enumerate(sources)}
    operands["sums"] = found["vec_sums"]
    results = {}
    for number, source in enumerate(sources):
        results["out%d" % number] = jax.ShapeDtypeStruct(source.shape, FULL if number < 5 else LOW)
    for number, wide in enumerate([width] * 8 + [out_width] * 2):
        results["vec%d" % number] = jax.ShapeDtypeStruct((wide,), FULL)
    results["vec10"] = jax.ShapeDtypeStruct((1, ff), FULL)
    held = {"full%d" % number: pltpu.VMEM(source.shape, FULL) for number, source in enumerate(sources[:5])}
    held["store"] = dma((7,))
    done = pl.pallas_call(
        functools.partial(finish_kernel, tuple(operands) + tuple(results) + tuple(held)),
        out_shape=list(results.values()),
        in_specs=[vmem] * 8,
        out_specs=[hbm] * 7 + [vmem] * 11,
        scratch_shapes=list(held.values()),
        compiler_params=pltpu.CompilerParams(vmem_limit_bytes=24 * 2**20),
        name="finish",
    )(*operands.values())
    down, up, proj, out, qkv, decoder_input, grad_tokens = done[:7]
    gain1, bias1, b_query, b_value, b_out, gain2, bias2, b_down, b_proj, mask, b_up = done[7:]
    b_up = b_up.reshape(-1)
    return (
        decoder_input,
        grad_tokens,
        gain1,
        bias1,
        qkv,
        b_query,
        b_value,
        out,
        b_out,
        gain2,
        bias2,
        up,
        b_up,
        down,
        b_down,
        proj,
        b_proj,
        mask,
    )


def solution(mesh):
    placed = (
        P(("img", "pos"), None),
        P(("img", "pos")),
        P(("img", "pos")),
        P(),
        P(),
        P(),
        P(),
        P(),
        P(),
        P(),
        P(),
        P(),
        P(),
        P(),
        P(),
        P(),
        P(),
        P(),
        P(),
        P("img", "pos", None),
    )
    fits = mesh.shape["img"] == 8 and mesh.shape["pos"] == 4
    return jax.shard_map(
        layer_device if fits else general_device,
        mesh=mesh,
        in_specs=placed,
        out_specs=(
            P("img", "pos", None),
            P(("img", "pos"), None),
            P(),
            P(),
            P("img", None),
            P(),
            P(),
            P("img", None),
            P(),
            P(),
            P(),
            P("img", None),
            P(),
            P("img", None),
            P(),
            P("img", None),
            P(),
            P(),
        ),
        check_vma=False,
    )
```
